32 devices in a mesh: hel: 4 (over x, core), rad: 8 (over z, y).
Axes of the slice: x: 2, y: 2, z: 4, core: 2. Of those that a mesh axis runs over, the one named last changes fastest.
Arguments:
- packet: bfloat16 [1024, 2, 16, 4, 512], P('rad', None, 'hel'), may hold values from -6 to 6
- first_propagator: bfloat16 [2, 1024, 1024], replicated, may hold values from -0.125 to 0.125
- second_propagator: bfloat16 [2, 512, 512], replicated, may hold values from -0.1875 to 0.1875
- potential: float32 [1024, 4, 512], P('rad'), may hold values from -3.140625 to 3.140625
- coupling: float32 [16, 4], replicated, may hold values from 0.2 to 0.8
- radial_weight: float32 [1024, 512], P('rad'), may hold values from 0.25 to 1
Outputs:
- advanced: bfloat16 [1024, 2, 16, 4, 512], P('rad', None, 'hel')
The draws below stay inside these ranges and needn't reach their ends.
All inputs are finite; a program needn't handle non-finite values.
Results may differ from the reference program's by a relative error of at most 0.007.
Values may be sent and summed in bfloat16 or wider, within the bound.
No kernel may reach another device: no remote copies, remote signals or barrier semaphores. Data moves between devices by JAX's collectives and lax.ppermute only.
A program may use at most 128 MiB of HBM per device.

```python
import math
import jax
import jax.numpy as jnp
from jax import lax

R1 = 1024
R2 = 512
J = 4
K = 16


def steps_of(own_key, shape, shards, least, high):
    level = 1.0
    for position, shards_of in shards:
        steps = jax.random.uniform(jax.random.fold_in(jax.random.fold_in(own_key, 6), position), (shards_of,), jnp.float32, least / len(shards), high / len(shards))
        level = level * jnp.repeat(jnp.exp(steps), shape[position] // shards_of).reshape((-1,) + (1,) * (len(shape) - 1 - position))
    return level


def normal_values(rng, shape, deviation, bound, cuts=(), kind=jnp.bfloat16):
    gain = steps_of(rng, shape, cuts, -0.22, 0.18) if cuts else 1.0
    array = jax.random.normal(rng, shape, jnp.float32) * deviation * gain
    return jnp.minimum(jnp.maximum(array, -bound), bound).astype(kind)


def setup_inputs(seed: int = 0) -> dict:
    key_list = jax.random.split(jax.random.key(seed), 7)
    return {
        "packet": normal_values(key_list[0], (R1, 2, K, J, R2), 1.0, 6.0, ((0, 8), (2, 4))),
        "first_propagator": normal_values(key_list[1], (2, R1, R1), (2 * R1) ** -0.5, 0.125),
        "second_propagator": normal_values(key_list[2], (2, R2, R2), (2 * R2) ** -0.5, 0.1875),
        "potential": jnp.clip(jax.random.uniform(key_list[3], (R1, J, R2), jnp.float32, -3.140625, 3.140625), -3.140625, 3.140625),
        "coupling": jnp.clip(jax.random.uniform(key_list[4], (K, J), jnp.float32, 0.2, 0.8), 0.2, 0.8),
        "radial_weight": jnp.clip(jnp.exp(math.log(1.0) - 1.3862944 * jax.random.uniform(key_list[5], (R1, R2), jnp.float32) ** steps_of(key_list[5], (R1, R2), ((0, 8),), -0.2, 0.2)), 0.25, 1.0),
    }


def along_second(packet, propagator):
    width = propagator.shape[1]
    joined = jnp.concatenate([propagator[0], propagator[1]], axis=1).astype(jnp.float32)
    product = jnp.einsum("cjas,sq->cjaq", packet.astype(jnp.float32), joined)
    real_part = product[0, ..., :width] - product[1, ..., width:]
    imag_part = product[0, ..., width:] + product[1, ..., :width]
    return jnp.stack([real_part, imag_part]).astype(jnp.bfloat16)


def along_first(packet, propagator):
    width = propagator.shape[1]
    joined = jnp.concatenate([propagator[0], propagator[1]], axis=1).astype(jnp.float32)
    product = jnp.einsum("cjrs,rq->cjqs", packet.astype(jnp.float32), joined)
    real_part = product[0, :, :width, :] - product[1, :, width:, :]
    imag_part = product[0, :, width:, :] + product[1, :, :width, :]
    return jnp.stack([real_part, imag_part]).astype(jnp.bfloat16)


def reference(packet, first_propagator, second_propagator, potential, coupling, radial_weight):
    packet_old = jnp.transpose(packet, (1, 2, 3, 0, 4))
    angles = jnp.transpose(potential, (1, 0, 2))
    cosine = jnp.cos(angles)
    sine = jnp.sin(angles)
    count = packet_old.shape[1]

    def propagate(single):
        half = along_second(single, second_propagator)
        moved = along_first(half, first_propagator).astype(jnp.float32)
        phased = jnp.stack([moved[0] * cosine + moved[1] * sine, moved[1] * cosine - moved[0] * sine]).astype(jnp.bfloat16)
        return along_second(phased, second_propagator)

    kinetic = lax.map(propagate, jnp.moveaxis(packet_old, 1, 0))
    helicities = jnp.arange(count, dtype=jnp.int32)
    couple_up = jnp.where(helicities[:, None] < count - 1, coupling, 0.0)
    couple_down = jnp.concatenate([jnp.zeros((1, coupling.shape[1]), jnp.float32), coupling[:-1]], axis=0)

    def mix(helicity):
        current = lax.dynamic_index_in_dim(kinetic, helicity, 0, False).astype(jnp.float32)
        upper = lax.dynamic_index_in_dim(kinetic, jnp.minimum(helicity + 1, count - 1), 0, False).astype(jnp.float32)
        lower = lax.dynamic_index_in_dim(kinetic, jnp.maximum(helicity - 1, 0), 0, False).astype(jnp.float32)
        factor_up = lax.dynamic_index_in_dim(couple_up, helicity, 0, False)[None, :, None, None]
        factor_down = lax.dynamic_index_in_dim(couple_down, helicity, 0, False)[None, :, None, None]
        mixing = factor_up * upper + factor_down * lower
        real_part = current[0] + radial_weight * mixing[1]
        imag_part = current[1] - radial_weight * mixing[0]
        return jnp.stack([real_part, imag_part]).astype(jnp.bfloat16)

    advanced = lax.map(mix, helicities)
    return jnp.transpose(advanced, (3, 1, 0, 2, 4))
```

```python
import jax
import jax.numpy as jnp
from jax import lax
from jax.sharding import PartitionSpec as P


def real_form(propagator):
    real, imag = propagator[0], propagator[1]
    return jnp.stack([jnp.stack([real, imag], 1), jnp.stack([-imag, real], 1)], 0)


def along_second(parts, second):
    product = jnp.einsum("ckrs,csdq->dkrq", parts, second, preferred_element_type=jnp.float32)
    return product.astype(jnp.bfloat16)


def neighbour(edge, axis, step):
    count = lax.axis_size(axis)
    pairs = [(i, i + step) for i in range(count) if 0 <= i + step < count]
    return lax.ppermute(edge, axis, pairs)


def per_device(packet, first_propagator, second_propagator, potential, coupling, radial_weight):
    rows, _, blocks, states, width = packet.shape
    ranks = lax.axis_size("rad")
    second = real_form(second_propagator)
    whole = first_propagator.shape[1]
    first = real_form(first_propagator).reshape(2, ranks, rows, 2, ranks, rows)
    first = first.transpose(4, 3, 5, 1, 0, 2).reshape(2 * whole, 2 * whole)
    count = coupling.shape[0]
    helicities = jnp.arange(count, dtype=jnp.int32)
    couple_up = jnp.where(helicities[:, None] < count - 1, coupling, 0.0)
    couple_down = jnp.concatenate(
        [jnp.zeros((1, coupling.shape[1]), jnp.float32), coupling[:-1]], axis=0
    )
    start = lax.axis_index("hel") * blocks
    factor_up = lax.dynamic_slice_in_dim(couple_up, start, blocks, 0)
    factor_down = lax.dynamic_slice_in_dim(couple_down, start, blocks, 0)

    piece = blocks * width // ranks
    results = []
    for j in range(states):
        parts = packet[:, :, :, j].transpose(1, 2, 0, 3)
        half = along_second(parts, second)
        send = half.reshape(2, blocks, rows, width // piece, piece) if piece <= width else None
        send = send.transpose(1, 3, 0, 2, 4).reshape(ranks, 2, rows, piece)
        lines = lax.all_to_all(send, "rad", 0, 0, tiled=True)
        moved = jnp.dot(
            first, lines.reshape(2 * whole, piece), preferred_element_type=jnp.float32
        ).astype(jnp.bfloat16)
        back = lax.all_to_all(moved.reshape(ranks, 2, rows, piece), "rad", 0, 0, tiled=True)
        back = back.reshape(blocks, width // piece, 2, rows, piece).transpose(2, 0, 3, 1, 4)
        back = back.reshape(2, blocks, rows, width).astype(jnp.float32)
        cosine, sine = jnp.cos(potential[:, j]), jnp.sin(potential[:, j])
        phased = jnp.stack(
            [back[0] * cosine + back[1] * sine, back[1] * cosine - back[0] * sine]
        ).astype(jnp.bfloat16)
        kinetic = along_second(phased, second)
        below = neighbour(kinetic[:, -1:], "hel", 1)
        above = neighbour(kinetic[:, :1], "hel", -1)
        padded = jnp.concatenate([below, kinetic, above], 1).astype(jnp.float32)
        mixing = (
            factor_up[:, j, None, None] * padded[:, 2:]
            + factor_down[:, j, None, None] * padded[:, :-2]
        )
        current = padded[:, 1:-1]
        results.append(
            jnp.stack(
                [current[0] + radial_weight * mixing[1], current[1] - radial_weight * mixing[0]]
            ).astype(jnp.bfloat16)
        )
    return jnp.stack(results).transpose(3, 1, 2, 0, 4)


def solution(mesh):
    return jax.shard_map(
        per_device,
        mesh=mesh,
        in_specs=(
            P("rad", None, "hel", None, None),
            P(),
            P(),
            P("rad", None, None),
            P(),
            P("rad", None),
        ),
        out_specs=P("rad", None, "hel", None, None),
        check_vma=False,
    )
```

```python
import functools

import jax
import jax.numpy as jnp
from jax import lax
from jax.experimental import pallas as pl
from jax.experimental.pallas import tpu as pltpu
from jax.sharding import PartitionSpec as P

LANES = 128
LIMIT = 48 * 1024 * 1024
SMEM = pl.BlockSpec(memory_space=pltpu.SMEM)


def params(limit=LIMIT):
    return pltpu.CompilerParams(vmem_limit_bytes=limit)


def cost(flops, moved):
    return pl.CostEstimate(flops=flops, bytes_accessed=moved, transcendentals=0)


def complex_rows(real, imag):
    return jnp.concatenate([real, -imag], 1), jnp.concatenate([imag, real], 1)


def right_kernel(ranks, states, me_ref, second_ref, *refs):
    kinds = len(refs) - 2 - ranks
    packets, outs, wide, slabs = refs[:kinds], refs[kinds:-2], refs[-2], refs[-1]
    me = me_ref[0]
    rows = packets[0].shape[0]
    group = packets[0].shape[2]
    tiles = group // states
    piece = slabs.shape[2] // 2
    cuts = tiles * LANES // piece
    for n, packet in enumerate(packets):
        wide[...] = packet[...].reshape(rows * 2 * group, LANES).astype(jnp.float32)

        def part(c, j):
            return jnp.concatenate(
                [
                    wide[pl.ds(c * group + t * states + j, rows, stride=2 * group), :]
                    for t in range(tiles)
                ],
                1,
            ).astype(jnp.bfloat16)

        pairs = [complex_rows(part(0, j), part(1, j)) for j in range(states)]
        left = jnp.concatenate([p[0] for p in pairs] + [p[1] for p in pairs], 0)
        product = jnp.dot(left, second_ref[...], preferred_element_type=jnp.float32)
        product = product.astype(jnp.bfloat16)
        for c in range(2):
            for j in range(states):
                first = (c * states + j) * rows
                for p in range(cuts):
                    slabs[j * cuts + p, :, c * piece : (c + 1) * piece] = product[
                        first : first + rows, p * piece : (p + 1) * piece
                    ]
        for s, out in enumerate(outs):
            out[n] = slabs[me ^ s]


def right_call(me, second, view, chosen, ranks, states, piece):
    rows, _, _, group, _ = view.shape
    width = second.shape[1]
    block = rows // 2
    kinds = len(chosen)
    return pl.pallas_call(
        functools.partial(right_kernel, ranks, states),
        grid=(rows // block,),
        in_specs=[SMEM, pl.BlockSpec(second.shape, lambda i: (0, 0))]
        + [
            pl.BlockSpec((block, 2, None, group, LANES), lambda i, k=k: (i, 0, k, 0, 0))
            for k in chosen
        ],
        out_specs=[pl.BlockSpec((kinds, block, 2 * piece), lambda i: (0, i, 0))] * ranks,
        out_shape=[jax.ShapeDtypeStruct((kinds, rows, 2 * piece), jnp.bfloat16)] * ranks,
        scratch_shapes=[
            pltpu.VMEM((block * 2 * group, LANES), jnp.float32),
            pltpu.VMEM((ranks, block, 2 * piece), jnp.bfloat16),
        ],
        compiler_params=params(),
        cost_estimate=cost(
            8 * kinds * states * rows * width * width, 8 * kinds * states * rows * width
        ),
        name="right",
    )(me, second, *([view] * kinds))


def left_kernel(ranks, me_ref, first_ref, *refs):
    ins, outs, lines, slabs = refs[:ranks], refs[ranks:-2], refs[-2], refs[-1]
    me = me_ref[0]
    rows, wide = ins[0].shape
    piece = wide // 2
    whole = ranks * rows
    for s, part in enumerate(ins):
        value = part[...]
        first = pl.multiple_of((me ^ s) * rows, rows)
        lines[pl.ds(first, rows), :] = value
        lines[pl.ds(first + whole, rows), :] = jnp.concatenate(
            [-value[:, piece:], value[:, :piece]], 1
        )
    product = jnp.dot(first_ref[...], lines[...], preferred_element_type=jnp.float32)
    slabs[...] = product.astype(jnp.bfloat16).reshape(ranks, rows, wide)
    for s, out in enumerate(outs):
        out[...] = slabs[me ^ s]


def left_call(me, first, slabs):
    ranks = len(slabs)
    kinds, rows, wide = slabs[0].shape
    whole = ranks * rows
    spec = pl.BlockSpec((None, rows, wide), lambda i: (i, 0, 0))
    return pl.pallas_call(
        functools.partial(left_kernel, ranks),
        grid=(kinds,),
        in_specs=[SMEM, pl.BlockSpec(first.shape, lambda i: (0, 0))] + [spec] * ranks,
        out_specs=[spec] * ranks,
        out_shape=[jax.ShapeDtypeStruct(slabs[0].shape, jnp.bfloat16)] * ranks,
        scratch_shapes=[
            pltpu.VMEM((2 * whole, wide), jnp.bfloat16),
            pltpu.VMEM((ranks, rows, wide), jnp.bfloat16),
        ],
        compiler_params=params(),
        cost_estimate=cost(
            4 * kinds * whole * whole * wide, 4 * whole * whole + 4 * kinds * whole * wide
        ),
        name="left",
    )(me, first, *slabs)


def phase_kernel(ranks, me_ref, second_ref, cosine_ref, sine_ref, *refs):
    ins, outs, slabs = refs[:ranks], refs[ranks:-1], refs[-1]
    me = me_ref[0]
    states, rows, width = cosine_ref.shape
    piece = slabs.shape[2] // 2
    cuts = width // piece
    for n, out in enumerate(outs):
        for s, part in enumerate(ins):
            slabs[me ^ s] = part[n]
        pairs = []
        for j in range(states):
            real, imag = (
                jnp.concatenate(
                    [
                        slabs[j * cuts + p, :, c * piece : (c + 1) * piece]
                        for p in range(cuts)
                    ],
                    1,
                ).astype(jnp.float32)
                for c in range(2)
            )
            cosine, sine = cosine_ref[j], sine_ref[j]
            pairs.append(
                complex_rows(
                    (real * cosine + imag * sine).astype(jnp.bfloat16),
                    (imag * cosine - real * sine).astype(jnp.bfloat16),
                )
            )
        left = jnp.concatenate([p[0] for p in pairs] + [p[1] for p in pairs], 0)
        product = jnp.dot(left, second_ref[...], preferred_element_type=jnp.float32)
        out[...] = product.astype(jnp.bfloat16).reshape(2, states, rows, width)


def phase_call(me, second, cosine, sine, slabs):
    ranks = len(slabs)
    kinds, rows, wide = slabs[0].shape
    states, _, width = cosine.shape
    block = rows // 2
    table = pl.BlockSpec((states, block, width), lambda i: (0, i, 0))
    return pl.pallas_call(
        functools.partial(phase_kernel, ranks),
        grid=(rows // block,),
        in_specs=[SMEM, pl.BlockSpec(second.shape, lambda i: (0, 0)), table, table]
        + [pl.BlockSpec((kinds, block, wide), lambda i: (0, i, 0))] * ranks,
        out_specs=[pl.BlockSpec((2, states, block, width), lambda i: (0, 0, i, 0))] * kinds,
        out_shape=[jax.ShapeDtypeStruct((2, states, rows, width), jnp.bfloat16)] * kinds,
        scratch_shapes=[pltpu.VMEM((ranks, block, wide), jnp.bfloat16)],
        compiler_params=params(),
        cost_estimate=cost(
            8 * kinds * states * rows * width * width, 8 * kinds * states * rows * width
        ),
        name="phase",
    )(me, second, cosine, sine, *slabs)


def mix_kernel(up_ref, down_ref, weight_ref, *refs):
    kinetic, out, wide = refs[:-2], refs[-2], refs[-1]
    _, states, rows, width = kinetic[0].shape
    tiles = width // LANES
    group = tiles * states
    weight = weight_ref[...]
    for k in range(len(kinetic) - 2):
        below, here, above = kinetic[k : k + 3]
        for j in range(states):
            up, down = up_ref[k, j], down_ref[k, j]
            mixed = [
                up * above[c, j].astype(jnp.float32) + down * below[c, j].astype(jnp.float32)
                for c in range(2)
            ]
            parts = (
                here[0, j].astype(jnp.float32) + weight * mixed[1],
                here[1, j].astype(jnp.float32) - weight * mixed[0],
            )
            for c in range(2):
                for t in range(tiles):
                    wide[pl.ds(c * group + t * states + j, rows, stride=2 * group), :] = parts[c][
                        :, t * LANES : (t + 1) * LANES
                    ]
        out[:, :, k] = wide[...].astype(jnp.bfloat16).reshape(rows, 2, group, LANES)


def mix_call(up, down, weight, kinetic):
    _, states, rows, width = kinetic[0].shape
    blocks = len(kinetic) - 2
    group = width // LANES * states
    block = rows // 4
    return pl.pallas_call(
        mix_kernel,
        grid=(rows // block,),
        in_specs=[SMEM, SMEM, pl.BlockSpec((block, width), lambda i: (i, 0))]
        + [pl.BlockSpec((2, states, block, width), lambda i: (0, 0, i, 0))] * len(kinetic),
        out_specs=pl.BlockSpec((block, 2, blocks, group, LANES), lambda i: (i, 0, 0, 0, 0)),
        out_shape=jax.ShapeDtypeStruct((rows, 2, blocks, group, LANES), jnp.bfloat16),
        scratch_shapes=[pltpu.VMEM((block * 2 * group, LANES), jnp.float32)],
        compiler_params=params(),
        cost_estimate=cost(
            20 * blocks * states * rows * width, 10 * blocks * states * rows * width
        ),
        name="mix",
    )(up, down, weight, *kinetic)


def exchanged(slabs, axis):
    count = lax.axis_size(axis)
    result = [slabs[0]] + [None] * (count - 1)
    for s in reversed(range(1, count)):
        result[s] = lax.ppermute(slabs[s], axis, [(i, i ^ s) for i in range(count)])
    return result


def neighbour(edge, axis, step):
    count = lax.axis_size(axis)
    pairs = [(i, i + step) for i in range(count) if 0 <= i + step < count]
    return lax.ppermute(edge, axis, pairs)


def per_device(packet, first_propagator, second_propagator, potential, coupling, radial_weight):
    rows, _, blocks, states, width = packet.shape
    ranks = lax.axis_size("rad")
    whole = first_propagator.shape[1]
    tiles = width // LANES
    piece = states * width // ranks
    me = lax.axis_index("rad").astype(jnp.int32).reshape(1)
    second = second_propagator.reshape(2 * width, width)
    first = first_propagator.reshape(2 * whole, whole).T
    view = packet.reshape(rows, 2, blocks, states, tiles, LANES).transpose(0, 1, 2, 4, 3, 5)
    view = view.reshape(rows, 2, blocks, tiles * states, LANES)
    edges = sorted({0, blocks - 1})
    inner = [k for k in range(blocks) if k not in edges]
    chunks = [c for c in (edges, inner) if c]

    halves = [right_call(me, second, view, c, ranks, states, piece) for c in chunks]
    lines = [exchanged(h, "rad") for h in halves]
    moved = [left_call(me, first, x) for x in lines]
    backs = [exchanged(m, "rad") for m in moved]

    angles = potential.transpose(1, 0, 2)
    cosine, sine = jnp.cos(angles), jnp.sin(angles)
    kinetic = [None] * blocks
    for chosen, back in zip(chunks, backs):
        for k, value in zip(chosen, phase_call(me, second, cosine, sine, back)):
            kinetic[k] = value
    below = neighbour(kinetic[-1], "hel", 1)
    above = neighbour(kinetic[0], "hel", -1)

    count = coupling.shape[0]
    helicities = jnp.arange(count, dtype=jnp.int32)
    couple_up = jnp.where(helicities[:, None] < count - 1, coupling, 0.0)
    couple_down = jnp.concatenate(
        [jnp.zeros((1, coupling.shape[1]), jnp.float32), coupling[:-1]], axis=0
    )
    start = lax.axis_index("hel") * blocks
    up = lax.dynamic_slice_in_dim(couple_up, start, blocks, 0)
    down = lax.dynamic_slice_in_dim(couple_down, start, blocks, 0)
    out = mix_call(up, down, radial_weight, [below] + kinetic + [above])
    out = out.reshape(rows, 2, blocks, tiles, states, LANES).transpose(0, 1, 2, 4, 3, 5)
    return out.reshape(rows, 2, blocks, states, width)


def solution(mesh):
    return jax.shard_map(
        per_device,
        mesh=mesh,
        in_specs=(
            P("rad", None, "hel", None, None),
            P(),
            P(),
            P("rad", None, None),
            P(),
            P("rad", None),
        ),
        out_specs=P("rad", None, "hel", None, None),
        check_vma=False,
    )
```

```python
import functools

import jax
import jax.numpy as jnp
from jax import lax
from jax.experimental import pallas as pl
from jax.experimental.pallas import tpu as pltpu
from jax.sharding import PartitionSpec as P

LANES = 128
LIMIT = 48 * 1024 * 1024
SMEM = pl.BlockSpec(memory_space=pltpu.SMEM)


def params(limit=LIMIT):
    return pltpu.CompilerParams(vmem_limit_bytes=limit)


def cost(flops, moved):
    return pl.CostEstimate(flops=flops, bytes_accessed=moved, transcendentals=0)


def complex_rows(real, imag):
    return jnp.concatenate([real, -imag], 1), jnp.concatenate([imag, real], 1)


def right_kernel(ranks, states, me_ref, second_ref, *refs):
    half = ranks // 2
    kinds = len(refs) - 3 - half
    packets, near, far = refs[:kinds], refs[kinds], refs[kinds + 1 : -2]
    wide, slabs = refs[-2:]
    me = me_ref[0]
    rows = packets[0].shape[0]
    group = packets[0].shape[2]
    tiles = group // states
    piece = slabs.shape[2] // 2
    cuts = tiles * LANES // piece
    for n, packet in enumerate(packets):
        wide[...] = packet[...].reshape(rows * 2 * group, LANES).astype(jnp.float32)

        def part(c, j):
            return jnp.concatenate(
                [
                    wide[pl.ds(c * group + t * states + j, rows, stride=2 * group), :]
                    for t in range(tiles)
                ],
                1,
            ).astype(jnp.bfloat16)

        pairs = [complex_rows(part(0, j), part(1, j)) for j in range(states)]
        left = jnp.concatenate([p[0] for p in pairs] + [p[1] for p in pairs], 0)
        product = jnp.dot(left, second_ref[...], preferred_element_type=jnp.float32)
        product = product.astype(jnp.bfloat16)
        for c in range(2):
            for j in range(states):
                first = (c * states + j) * rows
                for p in range(cuts):
                    slabs[j * cuts + p, :, c * piece : (c + 1) * piece] = product[
                        first : first + rows, p * piece : (p + 1) * piece
                    ]
        near[:, n] = slabs[pl.ds(me & half, half)]
        for s, out in enumerate(far):
            out[n] = slabs[me ^ (half + s)]


def right_call(me, second, view, chosen, ranks, states, piece):
    rows, _, _, group, _ = view.shape
    width = second.shape[1]
    block = rows // 2
    half = ranks // 2
    kinds = len(chosen)
    return pl.pallas_call(
        functools.partial(right_kernel, ranks, states),
        grid=(rows // block,),
        in_specs=[SMEM, pl.BlockSpec(second.shape, lambda i: (0, 0))]
        + [
            pl.BlockSpec((block, 2, None, group, LANES), lambda i, k=k: (i, 0, k, 0, 0))
            for k in chosen
        ],
        out_specs=[pl.BlockSpec((half, kinds, block, 2 * piece), lambda i: (0, 0, i, 0))]
        + [pl.BlockSpec((kinds, block, 2 * piece), lambda i: (0, i, 0))] * half,
        out_shape=[jax.ShapeDtypeStruct((half, kinds, rows, 2 * piece), jnp.bfloat16)]
        + [jax.ShapeDtypeStruct((kinds, rows, 2 * piece), jnp.bfloat16)] * half,
        scratch_shapes=[
            pltpu.VMEM((block * 2 * group, LANES), jnp.float32),
            pltpu.VMEM((ranks, block, 2 * piece), jnp.bfloat16),
        ],
        compiler_params=params(),
        cost_estimate=cost(
            8 * kinds * states * rows * width * width, 8 * kinds * states * rows * width
        ),
        name="right",
    )(me, second, *([view] * kinds))


def sources(me, parts):
    near, far = parts[0], parts[1:]
    half = len(far)
    for low in range(half):
        yield (me & half) + low, near[low]
    for s, part in enumerate(far):
        yield me ^ (half + s), part[...]


def left_kernel(ranks, me_ref, first_ref, *refs):
    half = ranks // 2
    ins, (near, *far), (lines, slabs) = refs[: half + 1], refs[half + 1 : -2], refs[-2:]
    me = me_ref[0]
    _, rows, wide = near.shape
    piece = wide // 2
    whole = ranks * rows
    for source, value in sources(me, ins):
        first = pl.multiple_of(source * rows, rows)
        lines[pl.ds(first, rows), :] = value
        lines[pl.ds(first + whole, rows), :] = jnp.concatenate(
            [-value[:, piece:], value[:, :piece]], 1
        )
    product = jnp.dot(first_ref[...], lines[...], preferred_element_type=jnp.float32)
    slabs[...] = product.astype(jnp.bfloat16).reshape(ranks, rows, wide)
    near[...] = slabs[pl.ds(me & half, half)]
    for s, out in enumerate(far):
        out[...] = slabs[me ^ (half + s)]


def left_call(me, first, slabs):
    half, kinds, rows, wide = slabs[0].shape
    ranks = 2 * half
    whole = ranks * rows
    specs = [pl.BlockSpec((half, None, rows, wide), lambda i: (0, i, 0, 0))]
    specs += [pl.BlockSpec((None, rows, wide), lambda i: (i, 0, 0))] * half
    return pl.pallas_call(
        functools.partial(left_kernel, ranks),
        grid=(kinds,),
        in_specs=[SMEM, pl.BlockSpec(first.shape, lambda i: (0, 0))] + specs,
        out_specs=specs,
        out_shape=[jax.ShapeDtypeStruct(x.shape, jnp.bfloat16) for x in slabs],
        scratch_shapes=[
            pltpu.VMEM((2 * whole, wide), jnp.bfloat16),
            pltpu.VMEM((ranks, rows, wide), jnp.bfloat16),
        ],
        compiler_params=params(),
        cost_estimate=cost(
            4 * kinds * whole * whole * wide, 4 * whole * whole + 4 * kinds * whole * wide
        ),
        name="left",
    )(me, first, *slabs)


def phase_kernel(ranks, me_ref, second_ref, cosine_ref, sine_ref, *refs):
    half = ranks // 2
    ins, outs, slabs = refs[: half + 1], refs[half + 1 : -1], refs[-1]
    me = me_ref[0]
    states, rows, width = cosine_ref.shape
    piece = slabs.shape[2] // 2
    cuts = width // piece
    for n, out in enumerate(outs):
        for source, value in sources(me, [ins[0].at[:, n]] + [x.at[n] for x in ins[1:]]):
            slabs[source] = value
        pairs = []
        for j in range(states):
            real, imag = (
                jnp.concatenate(
                    [
                        slabs[j * cuts + p, :, c * piece : (c + 1) * piece]
                        for p in range(cuts)
                    ],
                    1,
                ).astype(jnp.float32)
                for c in range(2)
            )
            cosine, sine = cosine_ref[j], sine_ref[j]
            pairs.append(
                complex_rows(
                    (real * cosine + imag * sine).astype(jnp.bfloat16),
                    (imag * cosine - real * sine).astype(jnp.bfloat16),
                )
            )
        left = jnp.concatenate([p[0] for p in pairs] + [p[1] for p in pairs], 0)
        product = jnp.dot(left, second_ref[...], preferred_element_type=jnp.float32)
        out[...] = product.astype(jnp.bfloat16).reshape(2, states, rows, width)


def phase_call(me, second, cosine, sine, slabs):
    half, kinds, rows, wide = slabs[0].shape
    ranks = 2 * half
    states, _, width = cosine.shape
    block = rows // 2
    table = pl.BlockSpec((states, block, width), lambda i: (0, i, 0))
    return pl.pallas_call(
        functools.partial(phase_kernel, ranks),
        grid=(rows // block,),
        in_specs=[SMEM, pl.BlockSpec(second.shape, lambda i: (0, 0)), table, table]
        + [pl.BlockSpec((half, kinds, block, wide), lambda i: (0, 0, i, 0))]
        + [pl.BlockSpec((kinds, block, wide), lambda i: (0, i, 0))] * half,
        out_specs=[pl.BlockSpec((2, states, block, width), lambda i: (0, 0, i, 0))] * kinds,
        out_shape=[jax.ShapeDtypeStruct((2, states, rows, width), jnp.bfloat16)] * kinds,
        scratch_shapes=[pltpu.VMEM((ranks, block, wide), jnp.bfloat16)],
        compiler_params=params(),
        cost_estimate=cost(
            8 * kinds * states * rows * width * width, 8 * kinds * states * rows * width
        ),
        name="phase",
    )(me, second, cosine, sine, *slabs)


def mix_kernel(up_ref, down_ref, weight_ref, *refs):
    kinetic, out, wide = refs[:-2], refs[-2], refs[-1]
    _, states, rows, width = kinetic[0].shape
    tiles = width // LANES
    group = tiles * states
    weight = weight_ref[...]
    for k in range(len(kinetic) - 2):
        below, here, above = kinetic[k : k + 3]
        for j in range(states):
            up, down = up_ref[k, j], down_ref[k, j]
            mixed = [
                up * above[c, j].astype(jnp.float32) + down * below[c, j].astype(jnp.float32)
                for c in range(2)
            ]
            parts = (
                here[0, j].astype(jnp.float32) + weight * mixed[1],
                here[1, j].astype(jnp.float32) - weight * mixed[0],
            )
            for c in range(2):
                for t in range(tiles):
                    wide[pl.ds(c * group + t * states + j, rows, stride=2 * group), :] = parts[c][
                        :, t * LANES : (t + 1) * LANES
                    ]
        out[:, :, k] = wide[...].astype(jnp.bfloat16).reshape(rows, 2, group, LANES)


def mix_call(up, down, weight, kinetic):
    _, states, rows, width = kinetic[0].shape
    blocks = len(kinetic) - 2
    group = width // LANES * states
    block = rows // 4
    return pl.pallas_call(
        mix_kernel,
        grid=(rows // block,),
        in_specs=[SMEM, SMEM, pl.BlockSpec((block, width), lambda i: (i, 0))]
        + [pl.BlockSpec((2, states, block, width), lambda i: (0, 0, i, 0))] * len(kinetic),
        out_specs=pl.BlockSpec((block, 2, blocks, group, LANES), lambda i: (i, 0, 0, 0, 0)),
        out_shape=jax.ShapeDtypeStruct((rows, 2, blocks, group, LANES), jnp.bfloat16),
        scratch_shapes=[pltpu.VMEM((block * 2 * group, LANES), jnp.float32)],
        compiler_params=params(),
        cost_estimate=cost(
            20 * blocks * states * rows * width, 10 * blocks * states * rows * width
        ),
        name="mix",
    )(up, down, weight, *kinetic)


def exchanged(slabs, axis):
    count = lax.axis_size(axis)
    half = count // 2
    groups = [list(range(half)), list(range(half, count))]
    far = [
        lax.ppermute(slab, axis, [(i, i ^ (half + s)) for i in range(count)])
        for s, slab in enumerate(slabs[1:])
    ]
    near = lax.all_to_all(slabs[0], axis, 0, 0, axis_index_groups=groups, tiled=True)
    return [near] + far


def neighbour(edge, axis, step):
    count = lax.axis_size(axis)
    pairs = [(i, i + step) for i in range(count) if 0 <= i + step < count]
    return lax.ppermute(edge, axis, pairs)


def per_device(packet, first_propagator, second_propagator, potential, coupling, radial_weight):
    rows, _, blocks, states, width = packet.shape
    ranks = lax.axis_size("rad")
    whole = first_propagator.shape[1]
    tiles = width // LANES
    piece = states * width // ranks
    me = lax.axis_index("rad").astype(jnp.int32).reshape(1)
    second = second_propagator.reshape(2 * width, width)
    first = first_propagator.reshape(2 * whole, whole).T
    view = packet.reshape(rows, 2, blocks, states, tiles, LANES).transpose(0, 1, 2, 4, 3, 5)
    view = view.reshape(rows, 2, blocks, tiles * states, LANES)
    edges = sorted({0, blocks - 1})
    inner = [k for k in range(blocks) if k not in edges]
    chunks = [[k] for k in edges + inner]

    halves = [right_call(me, second, view, c, ranks, states, piece) for c in chunks]
    lines = [exchanged(h, "rad") for h in halves]
    moved = [left_call(me, first, x) for x in lines]
    backs = [exchanged(m, "rad") for m in moved]

    angles = potential.transpose(1, 0, 2)
    cosine, sine = jnp.cos(angles), jnp.sin(angles)
    kinetic = [None] * blocks
    for chosen, back in zip(chunks, backs):
        for k, value in zip(chosen, phase_call(me, second, cosine, sine, back)):
            kinetic[k] = value
    below = neighbour(kinetic[-1], "hel", 1)
    above = neighbour(kinetic[0], "hel", -1)

    count = coupling.shape[0]
    helicities = jnp.arange(count, dtype=jnp.int32)
    couple_up = jnp.where(helicities[:, None] < count - 1, coupling, 0.0)
    couple_down = jnp.concatenate(
        [jnp.zeros((1, coupling.shape[1]), jnp.float32), coupling[:-1]], axis=0
    )
    start = lax.axis_index("hel") * blocks
    up = lax.dynamic_slice_in_dim(couple_up, start, blocks, 0)
    down = lax.dynamic_slice_in_dim(couple_down, start, blocks, 0)
    out = mix_call(up, down, radial_weight, [below] + kinetic + [above])
    out = out.reshape(rows, 2, blocks, tiles, states, LANES).transpose(0, 1, 2, 4, 3, 5)
    return out.reshape(rows, 2, blocks, states, width)


def solution(mesh):
    return jax.shard_map(
        per_device,
        mesh=mesh,
        in_specs=(
            P("rad", None, "hel", None, None),
            P(),
            P(),
            P("rad", None, None),
            P(),
            P("rad", None),
        ),
        out_specs=P("rad", None, "hel", None, None),
        check_vma=False,
    )
```

```python
import functools

import jax
import jax.numpy as jnp
from jax import lax
from jax.experimental import pallas as pl
from jax.experimental.pallas import tpu as pltpu
from jax.sharding import PartitionSpec as P

LANES = 128
LIMIT = 48 * 1024 * 1024
SMEM = pl.BlockSpec(memory_space=pltpu.SMEM)
AFTER = pl.BlockSpec(memory_space=pl.ANY)


def params(limit=LIMIT):
    return pltpu.CompilerParams(vmem_limit_bytes=limit)


def cost(flops, moved):
    return pl.CostEstimate(flops=flops, bytes_accessed=moved, transcendentals=0)


def complex_rows(real, imag):
    return jnp.concatenate([real, -imag], 1), jnp.concatenate([imag, real], 1)


def right_kernel(after, ranks, states, me_ref, second_ref, *refs):
    refs = refs[after:]
    kinds = len(refs) - 2 - ranks
    packets, outs, wide, slabs = refs[:kinds], refs[kinds:-2], refs[-2], refs[-1]
    me = me_ref[0]
    rows = packets[0].shape[0]
    group = packets[0].shape[2]
    tiles = group // states
    piece = slabs.shape[2] // 2
    cuts = tiles * LANES // piece
    for n, packet in enumerate(packets):
        wide[...] = packet[...].reshape(rows * 2 * group, LANES).astype(jnp.float32)

        def part(c, j):
            return jnp.concatenate(
                [
                    wide[pl.ds(c * group + t * states + j, rows, stride=2 * group), :]
                    for t in range(tiles)
                ],
                1,
            ).astype(jnp.bfloat16)

        pairs = [complex_rows(part(0, j), part(1, j)) for j in range(states)]
        left = jnp.concatenate([p[0] for p in pairs] + [p[1] for p in pairs], 0)
        product = jnp.dot(left, second_ref[...], preferred_element_type=jnp.float32)
        product = product.astype(jnp.bfloat16)
        for c in range(2):
            for j in range(states):
                first = (c * states + j) * rows
                for p in range(cuts):
                    slabs[j * cuts + p, :, c * piece : (c + 1) * piece] = product[
                        first : first + rows, p * piece : (p + 1) * piece
                    ]
        for s, out in enumerate(outs):
            out[n] = slabs[me ^ s]


def right_call(after, me, second, view, chosen, ranks, states, piece):
    rows, _, _, group, _ = view.shape
    width = second.shape[1]
    block = rows // 2
    kinds = len(chosen)
    return pl.pallas_call(
        functools.partial(right_kernel, len(after), ranks, states),
        grid=(rows // block,),
        in_specs=[SMEM, pl.BlockSpec(second.shape, lambda i: (0, 0))]
        + [AFTER] * len(after)
        + [
            pl.BlockSpec((block, 2, None, group, LANES), lambda i, k=k: (i, 0, k, 0, 0))
            for k in chosen
        ],
        out_specs=[pl.BlockSpec((kinds, block, 2 * piece), lambda i: (0, i, 0))] * ranks,
        out_shape=[jax.ShapeDtypeStruct((kinds, rows, 2 * piece), jnp.bfloat16)] * ranks,
        scratch_shapes=[
            pltpu.VMEM((block * 2 * group, LANES), jnp.float32),
            pltpu.VMEM((ranks, block, 2 * piece), jnp.bfloat16),
        ],
        compiler_params=params(),
        cost_estimate=cost(
            8 * kinds * states * rows * width * width, 8 * kinds * states * rows * width
        ),
        name="right",
    )(me, second, *after, *([view] * kinds))


def left_kernel(after, ranks, me_ref, first_ref, *refs):
    refs = refs[after:]
    ins, outs, lines, slabs = refs[:ranks], refs[ranks:-2], refs[-2], refs[-1]
    me = me_ref[0]
    rows, wide = ins[0].shape
    piece = wide // 2
    whole = ranks * rows
    for s, part in enumerate(ins):
        value = part[...]
        first = pl.multiple_of((me ^ s) * rows, rows)
        lines[pl.ds(first, rows), :] = value
        lines[pl.ds(first + whole, rows), :] = jnp.concatenate(
            [-value[:, piece:], value[:, :piece]], 1
        )
    product = jnp.dot(first_ref[...], lines[...], preferred_element_type=jnp.float32)
    slabs[...] = product.astype(jnp.bfloat16).reshape(ranks, rows, wide)
    for s, out in enumerate(outs):
        out[...] = slabs[me ^ s]


def left_call(after, me, first, slabs):
    ranks = len(slabs)
    kinds, rows, wide = slabs[0].shape
    whole = ranks * rows
    spec = pl.BlockSpec((None, rows, wide), lambda i: (i, 0, 0))
    return pl.pallas_call(
        functools.partial(left_kernel, len(after), ranks),
        grid=(kinds,),
        in_specs=[SMEM, pl.BlockSpec(first.shape, lambda i: (0, 0))]
        + [AFTER] * len(after)
        + [spec] * ranks,
        out_specs=[spec] * ranks,
        out_shape=[jax.ShapeDtypeStruct(slabs[0].shape, jnp.bfloat16)] * ranks,
        scratch_shapes=[
            pltpu.VMEM((2 * whole, wide), jnp.bfloat16),
            pltpu.VMEM((ranks, rows, wide), jnp.bfloat16),
        ],
        compiler_params=params(),
        cost_estimate=cost(
            4 * kinds * whole * whole * wide, 4 * whole * whole + 4 * kinds * whole * wide
        ),
        name="left",
    )(me, first, *after, *slabs)


def phase_kernel(after, ranks, me_ref, second_ref, cosine_ref, sine_ref, *refs):
    refs = refs[after:]
    ins, outs, slabs = refs[:ranks], refs[ranks:-1], refs[-1]
    me = me_ref[0]
    states, rows, width = cosine_ref.shape
    piece = slabs.shape[2] // 2
    cuts = width // piece
    for n, out in enumerate(outs):
        for s, part in enumerate(ins):
            slabs[me ^ s] = part[n]
        pairs = []
        for j in range(states):
            real, imag = (
                jnp.concatenate(
                    [
                        slabs[j * cuts + p, :, c * piece : (c + 1) * piece]
                        for p in range(cuts)
                    ],
                    1,
                ).astype(jnp.float32)
                for c in range(2)
            )
            cosine, sine = cosine_ref[j], sine_ref[j]
            pairs.append(
                complex_rows(
                    (real * cosine + imag * sine).astype(jnp.bfloat16),
                    (imag * cosine - real * sine).astype(jnp.bfloat16),
                )
            )
        left = jnp.concatenate([p[0] for p in pairs] + [p[1] for p in pairs], 0)
        product = jnp.dot(left, second_ref[...], preferred_element_type=jnp.float32)
        out[...] = product.astype(jnp.bfloat16).reshape(2, states, rows, width)


def phase_call(after, me, second, cosine, sine, slabs):
    ranks = len(slabs)
    kinds, rows, wide = slabs[0].shape
    states, _, width = cosine.shape
    block = rows // 2
    table = pl.BlockSpec((states, block, width), lambda i: (0, i, 0))
    return pl.pallas_call(
        functools.partial(phase_kernel, len(after), ranks),
        grid=(rows // block,),
        in_specs=[SMEM, pl.BlockSpec(second.shape, lambda i: (0, 0)), table, table]
        + [AFTER] * len(after)
        + [pl.BlockSpec((kinds, block, wide), lambda i: (0, i, 0))] * ranks,
        out_specs=[pl.BlockSpec((2, states, block, width), lambda i: (0, 0, i, 0))] * kinds,
        out_shape=[jax.ShapeDtypeStruct((2, states, rows, width), jnp.bfloat16)] * kinds,
        scratch_shapes=[pltpu.VMEM((ranks, block, wide), jnp.bfloat16)],
        compiler_params=params(),
        cost_estimate=cost(
            8 * kinds * states * rows * width * width, 8 * kinds * states * rows * width
        ),
        name="phase",
    )(me, second, cosine, sine, *after, *slabs)


def mix_kernel(up_ref, down_ref, weight_ref, *refs):
    kinetic, out, wide = refs[:-2], refs[-2], refs[-1]
    _, states, rows, width = kinetic[0].shape
    tiles = width // LANES
    group = tiles * states
    weight = weight_ref[...]
    for k in range(len(kinetic) - 2):
        below, here, above = kinetic[k : k + 3]
        for j in range(states):
            up, down = up_ref[k, j], down_ref[k, j]
            mixed = [
                up * above[c, j].astype(jnp.float32) + down * below[c, j].astype(jnp.float32)
                for c in range(2)
            ]
            parts = (
                here[0, j].astype(jnp.float32) + weight * mixed[1],
                here[1, j].astype(jnp.float32) - weight * mixed[0],
            )
            for c in range(2):
                for t in range(tiles):
                    wide[pl.ds(c * group + t * states + j, rows, stride=2 * group), :] = parts[c][
                        :, t * LANES : (t + 1) * LANES
                    ]
        out[:, :, k] = wide[...].astype(jnp.bfloat16).reshape(rows, 2, group, LANES)


def mix_call(up, down, weight, kinetic):
    _, states, rows, width = kinetic[0].shape
    blocks = len(kinetic) - 2
    group = width // LANES * states
    block = rows // 4
    return pl.pallas_call(
        mix_kernel,
        grid=(rows // block,),
        in_specs=[SMEM, SMEM, pl.BlockSpec((block, width), lambda i: (i, 0))]
        + [pl.BlockSpec((2, states, block, width), lambda i: (0, 0, i, 0))] * len(kinetic),
        out_specs=pl.BlockSpec((block, 2, blocks, group, LANES), lambda i: (i, 0, 0, 0, 0)),
        out_shape=jax.ShapeDtypeStruct((rows, 2, blocks, group, LANES), jnp.bfloat16),
        scratch_shapes=[pltpu.VMEM((block * 2 * group, LANES), jnp.float32)],
        compiler_params=params(),
        cost_estimate=cost(
            20 * blocks * states * rows * width, 10 * blocks * states * rows * width
        ),
        name="mix",
    )(up, down, weight, *kinetic)


def exchanged(slabs, axis):
    count = lax.axis_size(axis)
    result = [slabs[0]] + [None] * (count - 1)
    for s in reversed(range(1, count)):
        result[s] = lax.ppermute(slabs[s], axis, [(i, i ^ s) for i in range(count)])
    return result


def neighbour(edge, axis, step):
    count = lax.axis_size(axis)
    pairs = [(i, i + step) for i in range(count) if 0 <= i + step < count]
    return lax.ppermute(edge, axis, pairs)


def per_device(packet, first_propagator, second_propagator, potential, coupling, radial_weight):
    rows, _, blocks, states, width = packet.shape
    ranks = lax.axis_size("rad")
    whole = first_propagator.shape[1]
    tiles = width // LANES
    piece = states * width // ranks
    me = lax.axis_index("rad").astype(jnp.int32).reshape(1)
    second = second_propagator.reshape(2 * width, width)
    first = first_propagator.reshape(2 * whole, whole).T
    view = packet.reshape(rows, 2, blocks, states, tiles, LANES).transpose(0, 1, 2, 4, 3, 5)
    view = view.reshape(rows, 2, blocks, tiles * states, LANES)
    edges = sorted({0, blocks - 1})
    chunks = [edges] + [[k] for k in range(blocks) if k not in edges]

    last = me
    lines = []
    for chosen in chunks:
        half = right_call([last], me, second, view, chosen, ranks, states, piece)
        last = half[0]
        lines.append(exchanged(half, "rad"))
    backs = []
    for line in lines:
        moved = left_call([last], me, first, line)
        last = moved[0]
        backs.append(exchanged(moved, "rad"))

    angles = potential.transpose(1, 0, 2)
    cosine, sine = jnp.cos(angles), jnp.sin(angles)
    kinetic = [None] * blocks
    for n, (chosen, back) in enumerate(zip(chunks, backs)):
        after = [last, below, above] if n == 1 else [last]
        if n == 0:
            after += backs[1][4:]
        values = phase_call(after, me, second, cosine, sine, back)
        last = values[0]
        for k, value in zip(chosen, values):
            kinetic[k] = value
        if n == 0:
            below = neighbour(kinetic[-1], "hel", 1)
            above = neighbour(kinetic[0], "hel", -1)

    count = coupling.shape[0]
    helicities = jnp.arange(count, dtype=jnp.int32)
    couple_up = jnp.where(helicities[:, None] < count - 1, coupling, 0.0)
    couple_down = jnp.concatenate(
        [jnp.zeros((1, coupling.shape[1]), jnp.float32), coupling[:-1]], axis=0
    )
    start = lax.axis_index("hel") * blocks
    up = lax.dynamic_slice_in_dim(couple_up, start, blocks, 0)
    down = lax.dynamic_slice_in_dim(couple_down, start, blocks, 0)
    out = mix_call(up, down, radial_weight, [below] + kinetic + [above])
    out = out.reshape(rows, 2, blocks, tiles, states, LANES).transpose(0, 1, 2, 4, 3, 5)
    return out.reshape(rows, 2, blocks, states, width)


def solution(mesh):
    return jax.shard_map(
        per_device,
        mesh=mesh,
        in_specs=(
            P("rad", None, "hel", None, None),
            P(),
            P(),
            P("rad", None, None),
            P(),
            P("rad", None),
        ),
        out_specs=P("rad", None, "hel", None, None),
        check_vma=False,
    )
```

```python
import functools

import jax
import jax.numpy as jnp
from jax import lax
from jax.experimental import pallas as pl
from jax.experimental.pallas import tpu as pltpu
from jax.sharding import PartitionSpec as P

LANES = 128
LIMIT = 48 * 1024 * 1024
SMEM = pl.BlockSpec(memory_space=pltpu.SMEM)
AFTER = pl.BlockSpec(memory_space=pl.ANY)


def params(limit=LIMIT):
    return pltpu.CompilerParams(vmem_limit_bytes=limit)


def cost(flops, moved):
    return pl.CostEstimate(flops=flops, bytes_accessed=moved, transcendentals=0)


def complex_rows(real, imag):
    return jnp.concatenate([real, -imag], 1), jnp.concatenate([imag, real], 1)


def right_kernel(after, ranks, states, me_ref, second_ref, *refs):
    refs = refs[after:]
    kinds = len(refs) - 2 - ranks
    packets, outs, wide, slabs = refs[:kinds], refs[kinds:-2], refs[-2], refs[-1]
    me = me_ref[0]
    rows = packets[0].shape[0]
    group = packets[0].shape[2]
    tiles = group // states
    piece = slabs.shape[2] // 2
    cuts = tiles * LANES // piece
    for n, packet in enumerate(packets):
        wide[...] = packet[...].reshape(rows * 2 * group, LANES).astype(jnp.float32)

        def part(c, j):
            return jnp.concatenate(
                [
                    wide[pl.ds(c * group + t * states + j, rows, stride=2 * group), :]
                    for t in range(tiles)
                ],
                1,
            ).astype(jnp.bfloat16)

        pairs = [complex_rows(part(0, j), part(1, j)) for j in range(states)]
        left = jnp.concatenate([p[0] for p in pairs] + [p[1] for p in pairs], 0)
        product = jnp.dot(left, second_ref[...], preferred_element_type=jnp.float32)
        product = product.astype(jnp.bfloat16)
        for c in range(2):
            for j in range(states):
                first = (c * states + j) * rows
                for p in range(cuts):
                    slabs[j * cuts + p, :, c * piece : (c + 1) * piece] = product[
                        first : first + rows, p * piece : (p + 1) * piece
                    ]
        for s, out in enumerate(outs):
            out[n] = slabs[me ^ s]


def right_call(after, me, second, view, chosen, ranks, states, piece):
    rows, _, _, group, _ = view.shape
    width = second.shape[1]
    block = rows // 2
    kinds = len(chosen)
    return pl.pallas_call(
        functools.partial(right_kernel, len(after), ranks, states),
        grid=(rows // block,),
        in_specs=[SMEM, pl.BlockSpec(second.shape, lambda i: (0, 0))]
        + [AFTER] * len(after)
        + [
            pl.BlockSpec((block, 2, None, group, LANES), lambda i, k=k: (i, 0, k, 0, 0))
            for k in chosen
        ],
        out_specs=[pl.BlockSpec((kinds, block, 2 * piece), lambda i: (0, i, 0))] * ranks,
        out_shape=[jax.ShapeDtypeStruct((kinds, rows, 2 * piece), jnp.bfloat16)] * ranks,
        scratch_shapes=[
            pltpu.VMEM((block * 2 * group, LANES), jnp.float32),
            pltpu.VMEM((ranks, block, 2 * piece), jnp.bfloat16),
        ],
        compiler_params=params(),
        cost_estimate=cost(
            8 * kinds * states * rows * width * width, 8 * kinds * states * rows * width
        ),
        name="right",
    )(me, second, *after, *([view] * kinds))


def left_kernel(after, ranks, me_ref, first_ref, *refs):
    refs = refs[after:]
    ins, outs, lines, slabs = refs[:ranks], refs[ranks:-2], refs[-2], refs[-1]
    me = me_ref[0]
    rows, wide = ins[0].shape
    piece = wide // 2
    whole = ranks * rows
    for s, part in enumerate(ins):
        value = part[...]
        first = pl.multiple_of((me ^ s) * rows, rows)
        lines[pl.ds(first, rows), :] = value
        lines[pl.ds(first + whole, rows), :] = jnp.concatenate(
            [-value[:, piece:], value[:, :piece]], 1
        )
    product = jnp.dot(first_ref[...], lines[...], preferred_element_type=jnp.float32)
    slabs[...] = product.astype(jnp.bfloat16).reshape(ranks, rows, wide)
    for s, out in enumerate(outs):
        out[...] = slabs[me ^ s]


def left_call(after, me, first, slabs):
    ranks = len(slabs)
    kinds, rows, wide = slabs[0].shape
    whole = ranks * rows
    spec = pl.BlockSpec((None, rows, wide), lambda i: (i, 0, 0))
    return pl.pallas_call(
        functools.partial(left_kernel, len(after), ranks),
        grid=(kinds,),
        in_specs=[SMEM, pl.BlockSpec(first.shape, lambda i: (0, 0))]
        + [AFTER] * len(after)
        + [spec] * ranks,
        out_specs=[spec] * ranks,
        out_shape=[jax.ShapeDtypeStruct(slabs[0].shape, jnp.bfloat16)] * ranks,
        scratch_shapes=[
            pltpu.VMEM((2 * whole, wide), jnp.bfloat16),
            pltpu.VMEM((ranks, rows, wide), jnp.bfloat16),
        ],
        compiler_params=params(),
        cost_estimate=cost(
            4 * kinds * whole * whole * wide, 4 * whole * whole + 4 * kinds * whole * wide
        ),
        name="left",
    )(me, first, *after, *slabs)


def phase_kernel(after, ranks, me_ref, second_ref, cosine_ref, sine_ref, *refs):
    refs = refs[after:]
    ins, outs, slabs = refs[:ranks], refs[ranks:-1], refs[-1]
    me = me_ref[0]
    states, rows, width = cosine_ref.shape
    piece = slabs.shape[2] // 2
    cuts = width // piece
    for n in range(len(outs) // states):
        for s, part in enumerate(ins):
            slabs[me ^ s] = part[n]
        pairs = []
        for j in range(states):
            real, imag = (
                jnp.concatenate(
                    [
                        slabs[j * cuts + p, :, c * piece : (c + 1) * piece]
                        for p in range(cuts)
                    ],
                    1,
                ).astype(jnp.float32)
                for c in range(2)
            )
            cosine, sine = cosine_ref[j], sine_ref[j]
            pairs.append(
                complex_rows(
                    (real * cosine + imag * sine).astype(jnp.bfloat16),
                    (imag * cosine - real * sine).astype(jnp.bfloat16),
                )
            )
        left = jnp.concatenate([p[0] for p in pairs] + [p[1] for p in pairs], 0)
        product = jnp.dot(left, second_ref[...], preferred_element_type=jnp.float32)
        product = product.astype(jnp.bfloat16)
        for c in range(2):
            for j in range(states):
                first = (c * states + j) * rows
                outs[n * states + j][c] = product[first : first + rows]


def phase_call(after, me, second, cosine, sine, slabs):
    ranks = len(slabs)
    kinds, rows, wide = slabs[0].shape
    states, _, width = cosine.shape
    block = rows // 2
    table = pl.BlockSpec((states, block, width), lambda i: (0, i, 0))
    return pl.pallas_call(
        functools.partial(phase_kernel, len(after), ranks),
        grid=(rows // block,),
        in_specs=[SMEM, pl.BlockSpec(second.shape, lambda i: (0, 0)), table, table]
        + [AFTER] * len(after)
        + [pl.BlockSpec((kinds, block, wide), lambda i: (0, i, 0))] * ranks,
        out_specs=[pl.BlockSpec((2, block, width), lambda i: (0, i, 0))] * (kinds * states),
        out_shape=[jax.ShapeDtypeStruct((2, rows, width), jnp.bfloat16)] * (kinds * states),
        scratch_shapes=[pltpu.VMEM((ranks, block, wide), jnp.bfloat16)],
        compiler_params=params(),
        cost_estimate=cost(
            8 * kinds * states * rows * width * width, 8 * kinds * states * rows * width
        ),
        name="phase",
    )(me, second, cosine, sine, *after, *slabs)


def mix_kernel(up_ref, down_ref, weight_ref, *refs):
    kinetic, out, wide = refs[:-2], refs[-2], refs[-1]
    _, rows, width = kinetic[0].shape
    blocks, states = up_ref.shape
    tiles = width // LANES
    group = tiles * states
    weight = weight_ref[...]
    for k in range(blocks):
        for j in range(states):
            below, here, above = (kinetic[(k + n) * states + j] for n in range(3))
            up, down = up_ref[k, j], down_ref[k, j]
            mixed = [
                up * above[c].astype(jnp.float32) + down * below[c].astype(jnp.float32)
                for c in range(2)
            ]
            parts = (
                here[0].astype(jnp.float32) + weight * mixed[1],
                here[1].astype(jnp.float32) - weight * mixed[0],
            )
            for c in range(2):
                for t in range(tiles):
                    wide[pl.ds(c * group + t * states + j, rows, stride=2 * group), :] = parts[c][
                        :, t * LANES : (t + 1) * LANES
                    ]
        out[:, :, k] = wide[...].astype(jnp.bfloat16).reshape(rows, 2, group, LANES)


def mix_call(up, down, weight, kinetic):
    _, rows, width = kinetic[0].shape
    blocks, states = up.shape
    group = width // LANES * states
    block = rows // 4
    return pl.pallas_call(
        mix_kernel,
        grid=(rows // block,),
        in_specs=[SMEM, SMEM, pl.BlockSpec((block, width), lambda i: (i, 0))]
        + [pl.BlockSpec((2, block, width), lambda i: (0, i, 0))] * len(kinetic),
        out_specs=pl.BlockSpec((block, 2, blocks, group, LANES), lambda i: (i, 0, 0, 0, 0)),
        out_shape=jax.ShapeDtypeStruct((rows, 2, blocks, group, LANES), jnp.bfloat16),
        scratch_shapes=[pltpu.VMEM((block * 2 * group, LANES), jnp.float32)],
        compiler_params=params(),
        cost_estimate=cost(
            20 * blocks * states * rows * width, 10 * blocks * states * rows * width
        ),
        name="mix",
    )(up, down, weight, *kinetic)


def exchanged(slabs, axis):
    count = lax.axis_size(axis)
    result = [slabs[0]] + [None] * (count - 1)
    for s in reversed(range(1, count)):
        result[s] = lax.ppermute(slabs[s], axis, [(i, i ^ s) for i in range(count)])
    return result


def neighbour(edge, axis, step):
    count = lax.axis_size(axis)
    pairs = [(i, i + step) for i in range(count) if 0 <= i + step < count]
    return lax.ppermute(edge, axis, pairs)


def per_device(packet, first_propagator, second_propagator, potential, coupling, radial_weight):
    rows, _, blocks, states, width = packet.shape
    ranks = lax.axis_size("rad")
    whole = first_propagator.shape[1]
    tiles = width // LANES
    piece = states * width // ranks
    me = lax.axis_index("rad").astype(jnp.int32).reshape(1)
    second = second_propagator.reshape(2 * width, width)
    first = first_propagator.reshape(2 * whole, whole).T
    view = packet.reshape(rows, 2, blocks, states, tiles, LANES).transpose(0, 1, 2, 4, 3, 5)
    view = view.reshape(rows, 2, blocks, tiles * states, LANES)
    edges = sorted({0, blocks - 1})
    chunks = [edges, [k for k in range(blocks) if k not in edges]]

    last = me
    lines = []
    for chosen in chunks:
        half = right_call([last], me, second, view, chosen, ranks, states, piece)
        last = half[0]
        lines.append(exchanged(half, "rad"))
    backs = []
    for line in lines:
        moved = left_call([last], me, first, line)
        last = moved[0]
        backs.append(exchanged(moved, "rad"))

    angles = potential.transpose(1, 0, 2)
    cosine, sine = jnp.cos(angles), jnp.sin(angles)
    kinetic = [None] * blocks
    for n, (chosen, back) in enumerate(zip(chunks, backs)):
        after = [last]
        values = phase_call(after, me, second, cosine, sine, back)
        last = values[0]
        for i, k in enumerate(chosen):
            kinetic[k] = values[i * states : (i + 1) * states]
        if n == 0:
            below = [neighbour(edge, "hel", 1) for edge in kinetic[-1]]
            above = [neighbour(edge, "hel", -1) for edge in kinetic[0]]

    count = coupling.shape[0]
    helicities = jnp.arange(count, dtype=jnp.int32)
    couple_up = jnp.where(helicities[:, None] < count - 1, coupling, 0.0)
    couple_down = jnp.concatenate(
        [jnp.zeros((1, coupling.shape[1]), jnp.float32), coupling[:-1]], axis=0
    )
    start = lax.axis_index("hel") * blocks
    up = lax.dynamic_slice_in_dim(couple_up, start, blocks, 0)
    down = lax.dynamic_slice_in_dim(couple_down, start, blocks, 0)
    out = mix_call(up, down, radial_weight, sum([list(x) for x in (below, *kinetic, above)], []))
    out = out.reshape(rows, 2, blocks, tiles, states, LANES).transpose(0, 1, 2, 4, 3, 5)
    return out.reshape(rows, 2, blocks, states, width)


def solution(mesh):
    return jax.shard_map(
        per_device,
        mesh=mesh,
        in_specs=(
            P("rad", None, "hel", None, None),
            P(),
            P(),
            P("rad", None, None),
            P(),
            P("rad", None),
        ),
        out_specs=P("rad", None, "hel", None, None),
        check_vma=False,
    )
```

```python
import functools

import jax
import jax.numpy as jnp
from jax import lax
from jax.experimental import pallas as pl
from jax.experimental.pallas import tpu as pltpu
from jax.sharding import PartitionSpec as P

LANES = 128
PIECES = 2
LIMIT = 48 * 1024 * 1024
SMEM = pl.BlockSpec(memory_space=pltpu.SMEM)
AFTER = pl.BlockSpec(memory_space=pl.ANY)


def params(limit=LIMIT):
    return pltpu.CompilerParams(vmem_limit_bytes=limit)


def cost(flops, moved):
    return pl.CostEstimate(flops=flops, bytes_accessed=moved, transcendentals=0)


def complex_rows(real, imag):
    return jnp.concatenate([real, -imag], 1), jnp.concatenate([imag, real], 1)


def right_kernel(after, ranks, states, me_ref, second_ref, *refs):
    refs = refs[after:]
    kinds = len(refs) - 1 - ranks
    packets, outs, slabs = refs[:kinds], refs[kinds:-1], refs[-1]
    me = me_ref[0]
    rows = packets[0].shape[0]
    group = packets[0].shape[2]
    tiles = group // states
    piece = slabs.shape[2] // 2
    cuts = tiles * LANES // piece
    for n, packet in enumerate(packets):
        turned = [
            packet[:, c].astype(jnp.float32).transpose(1, 0, 2).astype(jnp.bfloat16)
            for c in range(2)
        ]

        def part(c, j):
            return jnp.concatenate([turned[c][t * states + j] for t in range(tiles)], 1)

        pairs = [complex_rows(part(0, j), part(1, j)) for j in range(states)]
        left = jnp.concatenate([p[0] for p in pairs] + [p[1] for p in pairs], 0)
        product = jnp.dot(left, second_ref[...], preferred_element_type=jnp.float32)
        product = product.astype(jnp.bfloat16)
        for c in range(2):
            for j in range(states):
                first = (c * states + j) * rows
                for p in range(cuts):
                    slabs[j * cuts + p, :, c * piece : (c + 1) * piece] = product[
                        first : first + rows, p * piece : (p + 1) * piece
                    ]
        for s, out in enumerate(outs):
            out[n] = slabs[me ^ s]


def right_call(after, me, second, view, chosen, ranks, states, piece):
    rows, _, _, group, _ = view.shape
    width = second.shape[1]
    block = rows // 2
    kinds = len(chosen)
    return pl.pallas_call(
        functools.partial(right_kernel, len(after), ranks, states),
        grid=(rows // block,),
        in_specs=[SMEM, pl.BlockSpec(second.shape, lambda i: (0, 0))]
        + [AFTER] * len(after)
        + [
            pl.BlockSpec((block, 2, None, group, LANES), lambda i, k=k: (i, 0, k, 0, 0))
            for k in chosen
        ],
        out_specs=[pl.BlockSpec((kinds, block, 2 * piece), lambda i: (0, i, 0))] * ranks,
        out_shape=[jax.ShapeDtypeStruct((kinds, rows, 2 * piece), jnp.bfloat16)] * ranks,
        scratch_shapes=[
            pltpu.VMEM((ranks, block, 2 * piece), jnp.bfloat16),
        ],
        compiler_params=params(),
        cost_estimate=cost(
            8 * kinds * states * rows * width * width, 8 * kinds * states * rows * width
        ),
        name="right",
    )(me, second, *after, *([view] * kinds))


def left_kernel(after, ranks, me_ref, first_ref, *refs):
    refs = refs[after:]
    ins, outs, lines, slabs = refs[:ranks], refs[ranks:-2], refs[-2], refs[-1]
    me = me_ref[0]
    rows, wide = ins[0].shape
    piece = wide // 2
    whole = ranks * rows
    for s, part in enumerate(ins):
        value = part[...]
        first = pl.multiple_of((me ^ s) * rows, rows)
        lines[pl.ds(first, rows), :] = value
        lines[pl.ds(first + whole, rows), :] = jnp.concatenate(
            [-value[:, piece:], value[:, :piece]], 1
        )
    product = jnp.dot(first_ref[...], lines[...], preferred_element_type=jnp.float32)
    slabs[...] = product.astype(jnp.bfloat16).reshape(ranks, rows, wide)
    for s, out in enumerate(outs):
        out[...] = slabs[me ^ s]


def left_call(after, me, first, slabs):
    ranks = len(slabs)
    kinds, rows, wide = slabs[0].shape
    whole = ranks * rows
    spec = pl.BlockSpec((None, rows, wide), lambda i: (i, 0, 0))
    return pl.pallas_call(
        functools.partial(left_kernel, len(after), ranks),
        grid=(kinds,),
        in_specs=[SMEM, pl.BlockSpec(first.shape, lambda i: (0, 0))]
        + [AFTER] * len(after)
        + [spec] * ranks,
        out_specs=[spec] * ranks,
        out_shape=[jax.ShapeDtypeStruct(slabs[0].shape, jnp.bfloat16)] * ranks,
        scratch_shapes=[
            pltpu.VMEM((2 * whole, wide), jnp.bfloat16),
            pltpu.VMEM((ranks, rows, wide), jnp.bfloat16),
        ],
        compiler_params=params(),
        cost_estimate=cost(
            4 * kinds * whole * whole * wide, 4 * whole * whole + 4 * kinds * whole * wide
        ),
        name="left",
    )(me, first, *after, *slabs)


def phased_product(me, n, second_ref, cosine_ref, sine_ref, ins, order, slabs):
    states, _, width = cosine_ref.shape
    piece = slabs.shape[2] // 2
    cuts = width // piece
    for s, part in zip(order, ins):
        slabs[me ^ s] = part[n]
    pairs = []
    for j in range(states):
        real, imag = (
            jnp.concatenate(
                [slabs[j * cuts + p, :, c * piece : (c + 1) * piece] for p in range(cuts)], 1
            ).astype(jnp.float32)
            for c in range(2)
        )
        cosine, sine = cosine_ref[j], sine_ref[j]
        pairs.append(
            complex_rows(
                (real * cosine + imag * sine).astype(jnp.bfloat16),
                (imag * cosine - real * sine).astype(jnp.bfloat16),
            )
        )
    left = jnp.concatenate([p[0] for p in pairs] + [p[1] for p in pairs], 0)
    product = jnp.dot(left, second_ref[...], preferred_element_type=jnp.float32)
    return product.astype(jnp.bfloat16)


def phase_kernel(after, ranks, me_ref, second_ref, cosine_ref, sine_ref, *refs):
    refs = refs[after:]
    ins, outs, slabs = refs[:ranks], refs[ranks:-1], refs[-1]
    states, rows, _ = cosine_ref.shape
    share = outs[0].shape[1]
    pieces = states // share
    for n in range(len(outs) // pieces):
        product = phased_product(
            me_ref[0], n, second_ref, cosine_ref, sine_ref, ins, range(ranks), slabs
        )
        for c in range(2):
            for j in range(states):
                first = (c * states + j) * rows
                outs[n * pieces + j // share][c, j % share] = product[first : first + rows]


def phase_call(after, me, second, cosine, sine, slabs):
    ranks = len(slabs)
    kinds, rows, wide = slabs[0].shape
    states, _, width = cosine.shape
    block = rows // 2
    share = states // PIECES
    count = kinds * PIECES
    table = pl.BlockSpec((states, block, width), lambda i: (0, i, 0))
    return pl.pallas_call(
        functools.partial(phase_kernel, len(after), ranks),
        grid=(rows // block,),
        in_specs=[SMEM, pl.BlockSpec(second.shape, lambda i: (0, 0)), table, table]
        + [AFTER] * len(after)
        + [pl.BlockSpec((kinds, block, wide), lambda i: (0, i, 0))] * ranks,
        out_specs=[pl.BlockSpec((2, share, block, width), lambda i: (0, 0, i, 0))] * count,
        out_shape=[jax.ShapeDtypeStruct((2, share, rows, width), jnp.bfloat16)] * count,
        scratch_shapes=[pltpu.VMEM((ranks, block, wide), jnp.bfloat16)],
        compiler_params=params(),
        cost_estimate=cost(
            8 * kinds * states * rows * width * width, 8 * kinds * states * rows * width
        ),
        name="phase",
    )(me, second, cosine, sine, *after, *slabs)


def mix_kernel(
    chosen, order, me_ref, up_ref, down_ref, second_ref, cosine_ref, sine_ref, weight_ref, *refs
):
    ranks = len(order)
    ins, known, (out, slabs, fresh) = refs[:ranks], refs[ranks:-3], refs[-3:]
    blocks, states = up_ref.shape
    rows, width = weight_ref.shape
    share = known[0].shape[1]
    pieces = states // share
    group = out.shape[3]
    weight = weight_ref[...]
    others = [k for k in range(-1, blocks + 1) if k not in chosen]
    for n in range(len(chosen)):
        product = phased_product(
            me_ref[0], n, second_ref, cosine_ref, sine_ref, ins, order, slabs
        )
        fresh[n] = product.reshape(2, states, rows, width)

    def kinetic(k, c, j):
        if k in chosen:
            value = fresh[chosen.index(k), c, j]
        else:
            value = known[others.index(k) * pieces + j // share][c, j % share]
        return value.astype(jnp.float32)

    for k in range(blocks):
        columns = [[None] * group for _ in range(2)]
        for j in range(states):
            up, down = up_ref[k, j], down_ref[k, j]
            mixed = [up * kinetic(k + 1, c, j) + down * kinetic(k - 1, c, j) for c in range(2)]
            parts = (
                kinetic(k, 0, j) + weight * mixed[1],
                kinetic(k, 1, j) - weight * mixed[0],
            )
            for c in range(2):
                for t in range(width // LANES):
                    columns[c][t * states + j] = parts[c][:, t * LANES : (t + 1) * LANES]
        for c in range(2):
            out[:, c, k] = jnp.stack(columns[c], 0).transpose(1, 0, 2).astype(jnp.bfloat16)


def mix_call(me, up, down, second, cosine, sine, weight, chosen, slabs, known):
    ranks = len(slabs)
    half = ranks // 2
    order = (*range(half, ranks), *range(half))
    kinds, rows, wide = slabs[0].shape
    _, share, _, width = known[0].shape
    blocks, states = up.shape
    group = width // LANES * states
    block = rows // 4
    table = pl.BlockSpec((states, block, width), lambda i: (0, i, 0))
    return pl.pallas_call(
        functools.partial(mix_kernel, tuple(chosen), order),
        grid=(rows // block,),
        in_specs=[SMEM] * 3
        + [pl.BlockSpec(second.shape, lambda i: (0, 0)), table, table]
        + [pl.BlockSpec((block, width), lambda i: (i, 0))]
        + [pl.BlockSpec((kinds, block, wide), lambda i: (0, i, 0))] * ranks
        + [pl.BlockSpec((2, share, block, width), lambda i: (0, 0, i, 0))] * len(known),
        out_specs=pl.BlockSpec((block, 2, blocks, group, LANES), lambda i: (i, 0, 0, 0, 0)),
        out_shape=jax.ShapeDtypeStruct((rows, 2, blocks, group, LANES), jnp.bfloat16),
        scratch_shapes=[
            pltpu.VMEM((ranks, block, wide), jnp.bfloat16),
            pltpu.VMEM((kinds, 2, states, block, width), jnp.bfloat16),
        ],
        compiler_params=params(),
        cost_estimate=cost(
            8 * kinds * states * rows * width * width, 10 * blocks * states * rows * width
        ),
        name="mix",
    )(me, up, down, second, cosine, sine, weight, *[slabs[s] for s in order], *known)


def exchanged(slabs, axis):
    count = lax.axis_size(axis)
    result = [slabs[0]] + [None] * (count - 1)
    for s in reversed(range(1, count)):
        result[s] = lax.ppermute(slabs[s], axis, [(i, i ^ s) for i in range(count)])
    return result


def neighbour(edge, axis, step):
    count = lax.axis_size(axis)
    pairs = [(i, i + step) for i in range(count) if 0 <= i + step < count]
    return lax.ppermute(edge, axis, pairs)


def per_device(packet, first_propagator, second_propagator, potential, coupling, radial_weight):
    rows, _, blocks, states, width = packet.shape
    ranks = lax.axis_size("rad")
    whole = first_propagator.shape[1]
    tiles = width // LANES
    piece = states * width // ranks
    me = lax.axis_index("rad").astype(jnp.int32).reshape(1)
    second = second_propagator.reshape(2 * width, width)
    first = first_propagator.reshape(2 * whole, whole).T
    view = packet.reshape(rows, 2, blocks, states, tiles, LANES).transpose(0, 1, 2, 4, 3, 5)
    view = view.reshape(rows, 2, blocks, tiles * states, LANES)
    edges = sorted({0, blocks - 1})
    chunks = [edges, [k for k in range(blocks) if k not in edges]]

    last = me
    lines = []
    for chosen in chunks:
        half = right_call([last], me, second, view, chosen, ranks, states, piece)
        last = half[0]
        lines.append(exchanged(half, "rad"))
    backs = []
    for line in lines:
        moved = left_call([last], me, first, line)
        last = moved[0]
        backs.append(exchanged(moved, "rad"))

    angles = potential.transpose(1, 0, 2)
    cosine, sine = jnp.cos(angles), jnp.sin(angles)
    edge = phase_call([last], me, second, cosine, sine, backs[0])
    low, high = edge[:PIECES], edge[-PIECES:]
    below = [neighbour(x, "hel", 1) for x in high]
    above = [neighbour(x, "hel", -1) for x in low]

    count = coupling.shape[0]
    helicities = jnp.arange(count, dtype=jnp.int32)
    couple_up = jnp.where(helicities[:, None] < count - 1, coupling, 0.0)
    couple_down = jnp.concatenate(
        [jnp.zeros((1, coupling.shape[1]), jnp.float32), coupling[:-1]], axis=0
    )
    start = lax.axis_index("hel") * blocks
    up = lax.dynamic_slice_in_dim(couple_up, start, blocks, 0)
    down = lax.dynamic_slice_in_dim(couple_down, start, blocks, 0)
    known = [*below, *low, *high, *above]
    out = mix_call(
        me, up, down, second, cosine, sine, radial_weight, chunks[1], backs[1], known
    )
    out = out.reshape(rows, 2, blocks, tiles, states, LANES).transpose(0, 1, 2, 4, 3, 5)
    return out.reshape(rows, 2, blocks, states, width)


def solution(mesh):
    return jax.shard_map(
        per_device,
        mesh=mesh,
        in_specs=(
            P("rad", None, "hel", None, None),
            P(),
            P(),
            P("rad", None, None),
            P(),
            P("rad", None),
        ),
        out_specs=P("rad", None, "hel", None, None),
        check_vma=False,
    )
```

```python
import functools

import jax
import jax.numpy as jnp
from jax import lax
from jax.experimental import pallas as pl
from jax.experimental.pallas import tpu as pltpu
from jax.sharding import PartitionSpec as P

LANES = 128
PIECES = 2
LIMIT = 20 * 1024 * 1024
SMEM = pl.BlockSpec(memory_space=pltpu.SMEM)
AFTER = pl.BlockSpec(memory_space=pl.ANY)


def params(limit=LIMIT):
    return pltpu.CompilerParams(vmem_limit_bytes=limit)


def cost(flops, moved):
    return pl.CostEstimate(flops=flops, bytes_accessed=moved, transcendentals=0)


def complex_rows(real, imag):
    return jnp.concatenate([real, -imag], 1), jnp.concatenate([imag, real], 1)


def right_kernel(after, ranks, states, me_ref, second_ref, *refs):
    refs = refs[after:]
    kinds = len(refs) - 1 - ranks
    packets, outs, slabs = refs[:kinds], refs[kinds:-1], refs[-1]
    me = me_ref[0]
    rows = packets[0].shape[0]
    group = packets[0].shape[2]
    tiles = group // states
    piece = slabs.shape[2] // 2
    cuts = tiles * LANES // piece
    for n, packet in enumerate(packets):
        turned = [
            packet[:, c].astype(jnp.float32).transpose(1, 0, 2).astype(jnp.bfloat16)
            for c in range(2)
        ]

        def part(c, j):
            return jnp.concatenate([turned[c][t * states + j] for t in range(tiles)], 1)

        pairs = [complex_rows(part(0, j), part(1, j)) for j in range(states)]
        left = jnp.concatenate([p[0] for p in pairs] + [p[1] for p in pairs], 0)
        product = jnp.dot(left, second_ref[...], preferred_element_type=jnp.float32)
        product = product.astype(jnp.bfloat16)
        for c in range(2):
            for j in range(states):
                first = (c * states + j) * rows
                for p in range(cuts):
                    slabs[j * cuts + p, :, c * piece : (c + 1) * piece] = product[
                        first : first + rows, p * piece : (p + 1) * piece
                    ]
        for s, out in enumerate(outs):
            out[n] = slabs[me ^ s]


def right_call(after, me, second, view, chosen, ranks, states, piece, limit):
    rows, _, _, group, _ = view.shape
    width = second.shape[1]
    block = rows // 2
    kinds = len(chosen)
    return pl.pallas_call(
        functools.partial(right_kernel, len(after), ranks, states),
        grid=(rows // block,),
        in_specs=[SMEM, pl.BlockSpec(second.shape, lambda i: (0, 0))]
        + [AFTER] * len(after)
        + [
            pl.BlockSpec((block, 2, None, group, LANES), lambda i, k=k: (i, 0, k, 0, 0))
            for k in chosen
        ],
        out_specs=[pl.BlockSpec((kinds, block, 2 * piece), lambda i: (0, i, 0))] * ranks,
        out_shape=[jax.ShapeDtypeStruct((kinds, rows, 2 * piece), jnp.bfloat16)] * ranks,
        scratch_shapes=[
            pltpu.VMEM((ranks, block, 2 * piece), jnp.bfloat16),
        ],
        compiler_params=params(limit),
        cost_estimate=cost(
            8 * kinds * states * rows * width * width, 8 * kinds * states * rows * width
        ),
        name="right",
    )(me, second, *after, *([view] * kinds))


def left_kernel(after, ranks, me_ref, first_ref, *refs):
    refs = refs[after:]
    ins, outs, lines, slabs = refs[:ranks], refs[ranks:-2], refs[-2], refs[-1]
    me = me_ref[0]
    rows, wide = ins[0].shape
    piece = wide // 2
    whole = ranks * rows
    for s, part in enumerate(ins):
        value = part[...]
        first = pl.multiple_of((me ^ s) * rows, rows)
        lines[pl.ds(first, rows), :] = value
        lines[pl.ds(first + whole, rows), :] = jnp.concatenate(
            [-value[:, piece:], value[:, :piece]], 1
        )
    product = jnp.dot(first_ref[...], lines[...], preferred_element_type=jnp.float32)
    slabs[...] = product.astype(jnp.bfloat16).reshape(ranks, rows, wide)
    for s, out in enumerate(outs):
        out[...] = slabs[me ^ s]


def left_call(after, me, first, slabs):
    ranks = len(slabs)
    kinds, rows, wide = slabs[0].shape
    whole = ranks * rows
    spec = pl.BlockSpec((None, rows, wide), lambda i: (i, 0, 0))
    return pl.pallas_call(
        functools.partial(left_kernel, len(after), ranks),
        grid=(kinds,),
        in_specs=[SMEM, pl.BlockSpec(first.shape, lambda i: (0, 0))]
        + [AFTER] * len(after)
        + [spec] * ranks,
        out_specs=[spec] * ranks,
        out_shape=[jax.ShapeDtypeStruct(slabs[0].shape, jnp.bfloat16)] * ranks,
        scratch_shapes=[
            pltpu.VMEM((2 * whole, wide), jnp.bfloat16),
            pltpu.VMEM((ranks, rows, wide), jnp.bfloat16),
        ],
        compiler_params=params(),
        cost_estimate=cost(
            4 * kinds * whole * whole * wide, 4 * whole * whole + 4 * kinds * whole * wide
        ),
        name="left",
    )(me, first, *after, *slabs)


def phased_product(me, n, second_ref, cosine_ref, sine_ref, ins, order, slabs):
    states, _, width = cosine_ref.shape
    piece = slabs.shape[2] // 2
    cuts = width // piece
    for s, part in zip(order, ins):
        slabs[me ^ s] = part[n]
    pairs = []
    for j in range(states):
        real, imag = (
            jnp.concatenate(
                [slabs[j * cuts + p, :, c * piece : (c + 1) * piece] for p in range(cuts)], 1
            ).astype(jnp.float32)
            for c in range(2)
        )
        cosine, sine = cosine_ref[j], sine_ref[j]
        pairs.append(
            complex_rows(
                (real * cosine + imag * sine).astype(jnp.bfloat16),
                (imag * cosine - real * sine).astype(jnp.bfloat16),
            )
        )
    left = jnp.concatenate([p[0] for p in pairs] + [p[1] for p in pairs], 0)
    product = jnp.dot(left, second_ref[...], preferred_element_type=jnp.float32)
    return product.astype(jnp.bfloat16)


def phase_kernel(after, ranks, me_ref, second_ref, cosine_ref, sine_ref, *refs):
    refs = refs[after:]
    ins, outs, slabs = refs[:ranks], refs[ranks:-1], refs[-1]
    states, rows, _ = cosine_ref.shape
    share = outs[0].shape[1]
    pieces = states // share
    for n in range(len(outs) // pieces):
        product = phased_product(
            me_ref[0], n, second_ref, cosine_ref, sine_ref, ins, range(ranks), slabs
        )
        for c in range(2):
            for j in range(states):
                first = (c * states + j) * rows
                outs[n * pieces + j // share][c, j % share] = product[first : first + rows]


def phase_call(after, me, second, cosine, sine, slabs):
    ranks = len(slabs)
    kinds, rows, wide = slabs[0].shape
    states, _, width = cosine.shape
    block = rows // 2
    share = states // PIECES
    count = kinds * PIECES
    table = pl.BlockSpec((states, block, width), lambda i: (0, i, 0))
    return pl.pallas_call(
        functools.partial(phase_kernel, len(after), ranks),
        grid=(rows // block,),
        in_specs=[SMEM, pl.BlockSpec(second.shape, lambda i: (0, 0)), table, table]
        + [AFTER] * len(after)
        + [pl.BlockSpec((kinds, block, wide), lambda i: (0, i, 0))] * ranks,
        out_specs=[pl.BlockSpec((2, share, block, width), lambda i: (0, 0, i, 0))] * count,
        out_shape=[jax.ShapeDtypeStruct((2, share, rows, width), jnp.bfloat16)] * count,
        scratch_shapes=[pltpu.VMEM((ranks, block, wide), jnp.bfloat16)],
        compiler_params=params(),
        cost_estimate=cost(
            8 * kinds * states * rows * width * width, 8 * kinds * states * rows * width
        ),
        name="phase",
    )(me, second, cosine, sine, *after, *slabs)


def mix_kernel(
    chosen, order, me_ref, up_ref, down_ref, second_ref, cosine_ref, sine_ref, weight_ref, *refs
):
    ranks = len(order)
    ins, known, (out, slabs, fresh) = refs[:ranks], refs[ranks:-3], refs[-3:]
    blocks, states = up_ref.shape
    rows, width = weight_ref.shape
    share = known[0].shape[1]
    pieces = states // share
    group = out.shape[3]
    weight = weight_ref[...]
    others = [k for k in range(-1, blocks + 1) if k not in chosen]
    for n in range(len(chosen)):
        product = phased_product(
            me_ref[0], n, second_ref, cosine_ref, sine_ref, ins, order, slabs
        )
        fresh[n] = product.reshape(2, states, rows, width)

    def kinetic(k, c, j):
        if k in chosen:
            value = fresh[chosen.index(k), c, j]
        else:
            value = known[others.index(k) * pieces + j // share][c, j % share]
        return value.astype(jnp.float32)

    for k in range(blocks):
        columns = [[None] * group for _ in range(2)]
        for j in range(states):
            up, down = up_ref[k, j], down_ref[k, j]
            mixed = [up * kinetic(k + 1, c, j) + down * kinetic(k - 1, c, j) for c in range(2)]
            parts = (
                kinetic(k, 0, j) + weight * mixed[1],
                kinetic(k, 1, j) - weight * mixed[0],
            )
            for c in range(2):
                for t in range(width // LANES):
                    columns[c][t * states + j] = parts[c][:, t * LANES : (t + 1) * LANES]
        for c in range(2):
            out[:, c, k] = jnp.stack(columns[c], 0).transpose(1, 0, 2).astype(jnp.bfloat16)


def mix_call(me, up, down, second, cosine, sine, weight, chosen, slabs, known):
    ranks = len(slabs)
    half = ranks // 2
    order = (*range(half, ranks), *range(half))
    kinds, rows, wide = slabs[0].shape
    _, share, _, width = known[0].shape
    blocks, states = up.shape
    group = width // LANES * states
    block = rows // 4
    table = pl.BlockSpec((states, block, width), lambda i: (0, i, 0))
    return pl.pallas_call(
        functools.partial(mix_kernel, tuple(chosen), order),
        grid=(rows // block,),
        in_specs=[SMEM] * 3
        + [pl.BlockSpec(second.shape, lambda i: (0, 0)), table, table]
        + [pl.BlockSpec((block, width), lambda i: (i, 0))]
        + [pl.BlockSpec((kinds, block, wide), lambda i: (0, i, 0))] * ranks
        + [pl.BlockSpec((2, share, block, width), lambda i: (0, 0, i, 0))] * len(known),
        out_specs=pl.BlockSpec((block, 2, blocks, group, LANES), lambda i: (i, 0, 0, 0, 0)),
        out_shape=jax.ShapeDtypeStruct((rows, 2, blocks, group, LANES), jnp.bfloat16),
        scratch_shapes=[
            pltpu.VMEM((ranks, block, wide), jnp.bfloat16),
            pltpu.VMEM((kinds, 2, states, block, width), jnp.bfloat16),
        ],
        compiler_params=params(),
        cost_estimate=cost(
            8 * kinds * states * rows * width * width, 10 * blocks * states * rows * width
        ),
        name="mix",
    )(me, up, down, second, cosine, sine, weight, *[slabs[s] for s in order], *known)


def exchanged(slabs, axis):
    count = lax.axis_size(axis)
    result = [slabs[0]] + [None] * (count - 1)
    for s in reversed(range(1, count)):
        result[s] = lax.ppermute(slabs[s], axis, [(i, i ^ s) for i in range(count)])
    return result


def neighbour(edge, axis, step):
    count = lax.axis_size(axis)
    pairs = [(i, i + step) for i in range(count) if 0 <= i + step < count]
    return lax.ppermute(edge, axis, pairs)


def per_device(packet, first_propagator, second_propagator, potential, coupling, radial_weight):
    rows, _, blocks, states, width = packet.shape
    ranks = lax.axis_size("rad")
    whole = first_propagator.shape[1]
    tiles = width // LANES
    piece = states * width // ranks
    me = lax.axis_index("rad").astype(jnp.int32).reshape(1)
    second = second_propagator.reshape(2 * width, width)
    first = first_propagator.reshape(2 * whole, whole).T
    view = packet.reshape(rows, 2, blocks, states, tiles, LANES).transpose(0, 1, 2, 4, 3, 5)
    view = view.reshape(rows, 2, blocks, tiles * states, LANES)
    edges = sorted({0, blocks - 1})
    chunks = [edges, [k for k in range(blocks) if k not in edges]]

    last = me
    lines = []
    for n, chosen in enumerate(chunks):
        limit = LIMIT if n else 2 * LIMIT + LIMIT // 2
        half = right_call([last], me, second, view, chosen, ranks, states, piece, limit)
        last = half[0]
        lines.append(exchanged(half, "rad"))
    backs = []
    for line in lines:
        moved = left_call([last], me, first, line)
        last = moved[0]
        backs.append(exchanged(moved, "rad"))

    angles = potential.transpose(1, 0, 2)
    cosine, sine = jnp.cos(angles), jnp.sin(angles)
    edge = phase_call([last], me, second, cosine, sine, backs[0])
    low, high = edge[:PIECES], edge[-PIECES:]
    below = [neighbour(x, "hel", 1) for x in high]
    above = [neighbour(x, "hel", -1) for x in low]

    count = coupling.shape[0]
    helicities = jnp.arange(count, dtype=jnp.int32)
    couple_up = jnp.where(helicities[:, None] < count - 1, coupling, 0.0)
    couple_down = jnp.concatenate(
        [jnp.zeros((1, coupling.shape[1]), jnp.float32), coupling[:-1]], axis=0
    )
    start = lax.axis_index("hel") * blocks
    up = lax.dynamic_slice_in_dim(couple_up, start, blocks, 0)
    down = lax.dynamic_slice_in_dim(couple_down, start, blocks, 0)
    known = [*below, *low, *high, *above]
    out = mix_call(
        me, up, down, second, cosine, sine, radial_weight, chunks[1], backs[1], known
    )
    out = out.reshape(rows, 2, blocks, tiles, states, LANES).transpose(0, 1, 2, 4, 3, 5)
    return out.reshape(rows, 2, blocks, states, width)


def solution(mesh):
    return jax.shard_map(
        per_device,
        mesh=mesh,
        in_specs=(
            P("rad", None, "hel", None, None),
            P(),
            P(),
            P("rad", None, None),
            P(),
            P("rad", None),
        ),
        out_specs=P("rad", None, "hel", None, None),
        check_vma=False,
    )
```

```python
import functools

import jax
import jax.numpy as jnp
from jax import lax
from jax.experimental import pallas as pl
from jax.experimental.pallas import tpu as pltpu
from jax.sharding import PartitionSpec as P

LANES = 128
PIECES = 2
LIMIT = 20 * 1024 * 1024
SMEM = pl.BlockSpec(memory_space=pltpu.SMEM)
AFTER = pl.BlockSpec(memory_space=pl.ANY)


def params(limit=LIMIT):
    return pltpu.CompilerParams(vmem_limit_bytes=limit)


def cost(flops, moved):
    return pl.CostEstimate(flops=flops, bytes_accessed=moved, transcendentals=0)


def complex_rows(real, imag):
    return jnp.concatenate([real, -imag], 1), jnp.concatenate([imag, real], 1)


def near_slabs(me, near):
    return pl.ds(me & -near, near)


def slab_specs(near, ranks, kinds, block, wide):
    return [pl.BlockSpec((near, kinds, block, wide), lambda i: (0, 0, i, 0))] + [
        pl.BlockSpec((kinds, block, wide), lambda i: (0, i, 0))
    ] * (ranks - near)


def sources(me, near, parts, n):
    for low in range(near):
        yield (me & -near) + low, parts[0][low, n]
    for s, part in enumerate(parts[1:], near):
        yield me ^ s, part[n]


def right_kernel(after, near, ranks, states, me_ref, second_ref, *refs):
    refs = refs[after:]
    kinds = len(refs) - 2 - (ranks - near)
    packets, outs, slabs = refs[:kinds], refs[kinds:-1], refs[-1]
    me = me_ref[0]
    rows = packets[0].shape[0]
    group = packets[0].shape[2]
    tiles = group // states
    piece = slabs.shape[2] // 2
    cuts = tiles * LANES // piece
    for n, packet in enumerate(packets):
        turned = [
            packet[:, c].astype(jnp.float32).transpose(1, 0, 2).astype(jnp.bfloat16)
            for c in range(2)
        ]

        def part(c, j):
            return jnp.concatenate([turned[c][t * states + j] for t in range(tiles)], 1)

        pairs = [complex_rows(part(0, j), part(1, j)) for j in range(states)]
        left = jnp.concatenate([p[0] for p in pairs] + [p[1] for p in pairs], 0)
        product = jnp.dot(left, second_ref[...], preferred_element_type=jnp.float32)
        product = product.astype(jnp.bfloat16)
        for c in range(2):
            for j in range(states):
                first = (c * states + j) * rows
                for p in range(cuts):
                    slabs[j * cuts + p, :, c * piece : (c + 1) * piece] = product[
                        first : first + rows, p * piece : (p + 1) * piece
                    ]
        outs[0][:, n] = slabs[near_slabs(me, near)]
        for s, out in enumerate(outs[1:], near):
            out[n] = slabs[me ^ s]


def right_call(after, near, me, second, view, chosen, ranks, states, piece, limit):
    rows, _, _, group, _ = view.shape
    width = second.shape[1]
    block = rows // 2
    kinds = len(chosen)
    return pl.pallas_call(
        functools.partial(right_kernel, len(after), near, ranks, states),
        grid=(rows // block,),
        in_specs=[SMEM, pl.BlockSpec(second.shape, lambda i: (0, 0))]
        + [AFTER] * len(after)
        + [
            pl.BlockSpec((block, 2, None, group, LANES), lambda i, k=k: (i, 0, k, 0, 0))
            for k in chosen
        ],
        out_specs=slab_specs(near, ranks, kinds, block, 2 * piece),
        out_shape=[jax.ShapeDtypeStruct((near, kinds, rows, 2 * piece), jnp.bfloat16)]
        + [jax.ShapeDtypeStruct((kinds, rows, 2 * piece), jnp.bfloat16)] * (ranks - near),
        scratch_shapes=[
            pltpu.VMEM((ranks, block, 2 * piece), jnp.bfloat16),
        ],
        compiler_params=params(limit),
        cost_estimate=cost(
            8 * kinds * states * rows * width * width, 8 * kinds * states * rows * width
        ),
        name="right",
    )(me, second, *after, *([view] * kinds))


def left_kernel(after, near, ranks, me_ref, first_ref, *refs):
    refs = refs[after:]
    count = 1 + ranks - near
    ins, outs, lines, slabs = refs[:count], refs[count:-2], refs[-2], refs[-1]
    me = me_ref[0]
    _, _, rows, wide = ins[0].shape
    piece = wide // 2
    whole = ranks * rows
    for source, value in sources(me, near, ins, 0):
        first = pl.multiple_of(source * rows, rows)
        lines[pl.ds(first, rows), :] = value
        lines[pl.ds(first + whole, rows), :] = jnp.concatenate(
            [-value[:, piece:], value[:, :piece]], 1
        )
    product = jnp.dot(first_ref[...], lines[...], preferred_element_type=jnp.float32)
    slabs[...] = product.astype(jnp.bfloat16).reshape(ranks, rows, wide)
    outs[0][:, 0] = slabs[near_slabs(me, near)]
    for s, out in enumerate(outs[1:], near):
        out[0] = slabs[me ^ s]


def left_call(after, me, first, slabs):
    near, kinds, rows, wide = slabs[0].shape
    ranks = len(slabs) - 1 + near
    whole = ranks * rows
    specs = [pl.BlockSpec((near, 1, rows, wide), lambda i: (0, i, 0, 0))] + [
        pl.BlockSpec((1, rows, wide), lambda i: (i, 0, 0))
    ] * (ranks - near)
    return pl.pallas_call(
        functools.partial(left_kernel, len(after), near, ranks),
        grid=(kinds,),
        in_specs=[SMEM, pl.BlockSpec(first.shape, lambda i: (0, 0))]
        + [AFTER] * len(after)
        + specs,
        out_specs=specs,
        out_shape=[jax.ShapeDtypeStruct(x.shape, jnp.bfloat16) for x in slabs],
        scratch_shapes=[
            pltpu.VMEM((2 * whole, wide), jnp.bfloat16),
            pltpu.VMEM((ranks, rows, wide), jnp.bfloat16),
        ],
        compiler_params=params(),
        cost_estimate=cost(
            4 * kinds * whole * whole * wide, 4 * whole * whole + 4 * kinds * whole * wide
        ),
        name="left",
    )(me, first, *after, *slabs)


def phased_product(me, n, near, second_ref, cosine_ref, sine_ref, ins, slabs):
    states, _, width = cosine_ref.shape
    piece = slabs.shape[2] // 2
    cuts = width // piece
    for source, value in sources(me, near, ins, n):
        slabs[source] = value
    pairs = []
    for j in range(states):
        real, imag = (
            jnp.concatenate(
                [slabs[j * cuts + p, :, c * piece : (c + 1) * piece] for p in range(cuts)], 1
            ).astype(jnp.float32)
            for c in range(2)
        )
        cosine, sine = cosine_ref[j], sine_ref[j]
        pairs.append(
            complex_rows(
                (real * cosine + imag * sine).astype(jnp.bfloat16),
                (imag * cosine - real * sine).astype(jnp.bfloat16),
            )
        )
    left = jnp.concatenate([p[0] for p in pairs] + [p[1] for p in pairs], 0)
    product = jnp.dot(left, second_ref[...], preferred_element_type=jnp.float32)
    return product.astype(jnp.bfloat16)


def phase_kernel(after, near, ranks, me_ref, second_ref, cosine_ref, sine_ref, *refs):
    refs = refs[after:]
    count = 1 + ranks - near
    ins, outs, slabs = refs[:count], refs[count:-1], refs[-1]
    states, rows, _ = cosine_ref.shape
    share = outs[0].shape[1]
    pieces = states // share
    for n in range(len(outs) // pieces):
        product = phased_product(
            me_ref[0], n, near, second_ref, cosine_ref, sine_ref, ins, slabs
        )
        for c in range(2):
            for j in range(states):
                first = (c * states + j) * rows
                outs[n * pieces + j // share][c, j % share] = product[first : first + rows]


def phase_call(after, me, second, cosine, sine, slabs):
    near, kinds, rows, wide = slabs[0].shape
    ranks = len(slabs) - 1 + near
    states, _, width = cosine.shape
    block = rows // 2
    share = states // PIECES
    count = kinds * PIECES
    table = pl.BlockSpec((states, block, width), lambda i: (0, i, 0))
    return pl.pallas_call(
        functools.partial(phase_kernel, len(after), near, ranks),
        grid=(rows // block,),
        in_specs=[SMEM, pl.BlockSpec(second.shape, lambda i: (0, 0)), table, table]
        + [AFTER] * len(after)
        + slab_specs(near, ranks, kinds, block, wide),
        out_specs=[pl.BlockSpec((2, share, block, width), lambda i: (0, 0, i, 0))] * count,
        out_shape=[jax.ShapeDtypeStruct((2, share, rows, width), jnp.bfloat16)] * count,
        scratch_shapes=[pltpu.VMEM((ranks, block, wide), jnp.bfloat16)],
        compiler_params=params(),
        cost_estimate=cost(
            8 * kinds * states * rows * width * width, 8 * kinds * states * rows * width
        ),
        name="phase",
    )(me, second, cosine, sine, *after, *slabs)


def mix_kernel(
    chosen, near, ranks, me_ref, up_ref, down_ref, second_ref, cosine_ref, sine_ref, weight_ref, *refs
):
    count = 1 + ranks - near
    ins, known, (out, slabs, fresh) = refs[:count], refs[count:-3], refs[-3:]
    blocks, states = up_ref.shape
    rows, width = weight_ref.shape
    share = known[0].shape[1]
    pieces = states // share
    group = out.shape[3]
    weight = weight_ref[...]
    others = [k for k in range(-1, blocks + 1) if k not in chosen]
    for n in range(len(chosen)):
        product = phased_product(
            me_ref[0], n, near, second_ref, cosine_ref, sine_ref, ins, slabs
        )
        fresh[n] = product.reshape(2, states, rows, width)

    def kinetic(k, c, j):
        if k in chosen:
            value = fresh[chosen.index(k), c, j]
        else:
            value = known[others.index(k) * pieces + j // share][c, j % share]
        return value.astype(jnp.float32)

    for k in range(blocks):
        columns = [[None] * group for _ in range(2)]
        for j in range(states):
            up, down = up_ref[k, j], down_ref[k, j]
            mixed = [up * kinetic(k + 1, c, j) + down * kinetic(k - 1, c, j) for c in range(2)]
            parts = (
                kinetic(k, 0, j) + weight * mixed[1],
                kinetic(k, 1, j) - weight * mixed[0],
            )
            for c in range(2):
                for t in range(width // LANES):
                    columns[c][t * states + j] = parts[c][:, t * LANES : (t + 1) * LANES]
        for c in range(2):
            out[:, c, k] = jnp.stack(columns[c], 0).transpose(1, 0, 2).astype(jnp.bfloat16)


def mix_call(me, up, down, second, cosine, sine, weight, chosen, slabs, known):
    near, kinds, rows, wide = slabs[0].shape
    ranks = len(slabs) - 1 + near
    _, share, _, width = known[0].shape
    blocks, states = up.shape
    group = width // LANES * states
    block = rows // 4
    table = pl.BlockSpec((states, block, width), lambda i: (0, i, 0))
    return pl.pallas_call(
        functools.partial(mix_kernel, tuple(chosen), near, ranks),
        grid=(rows // block,),
        in_specs=[SMEM] * 3
        + [pl.BlockSpec(second.shape, lambda i: (0, 0)), table, table]
        + [pl.BlockSpec((block, width), lambda i: (i, 0))]
        + slab_specs(near, ranks, kinds, block, wide)
        + [pl.BlockSpec((2, share, block, width), lambda i: (0, 0, i, 0))] * len(known),
        out_specs=pl.BlockSpec((block, 2, blocks, group, LANES), lambda i: (i, 0, 0, 0, 0)),
        out_shape=jax.ShapeDtypeStruct((rows, 2, blocks, group, LANES), jnp.bfloat16),
        scratch_shapes=[
            pltpu.VMEM((ranks, block, wide), jnp.bfloat16),
            pltpu.VMEM((kinds, 2, states, block, width), jnp.bfloat16),
        ],
        compiler_params=params(),
        cost_estimate=cost(
            8 * kinds * states * rows * width * width, 10 * blocks * states * rows * width
        ),
        name="mix",
    )(me, up, down, second, cosine, sine, weight, *slabs, *known)


def exchanged(slabs, axis):
    count = lax.axis_size(axis)
    near = slabs[0].shape[0]
    result = [slabs[0]]
    if near == count:
        result = [lax.all_to_all(slabs[0], axis, 0, 0, tiled=True)]
    elif near > 1:
        groups = [list(range(i, i + near)) for i in range(0, count, near)]
        result = [lax.all_to_all(slabs[0], axis, 0, 0, axis_index_groups=groups, tiled=True)]
    for s, slab in enumerate(slabs[1:], near):
        result.append(lax.ppermute(slab, axis, [(i, i ^ s) for i in range(count)]))
    return result


def neighbour(edge, axis, step):
    count = lax.axis_size(axis)
    pairs = [(i, i + step) for i in range(count) if 0 <= i + step < count]
    return lax.ppermute(edge, axis, pairs)


def per_device(packet, first_propagator, second_propagator, potential, coupling, radial_weight):
    rows, _, blocks, states, width = packet.shape
    ranks = lax.axis_size("rad")
    whole = first_propagator.shape[1]
    tiles = width // LANES
    piece = states * width // ranks
    me = lax.axis_index("rad").astype(jnp.int32).reshape(1)
    second = second_propagator.reshape(2 * width, width)
    first = first_propagator.reshape(2 * whole, whole).T
    view = packet.reshape(rows, 2, blocks, states, tiles, LANES).transpose(0, 1, 2, 4, 3, 5)
    view = view.reshape(rows, 2, blocks, tiles * states, LANES)
    edges = sorted({0, blocks - 1})
    chunks = [edges, [k for k in range(blocks) if k not in edges]]

    nears = (ranks, ranks)
    last = me
    lines = []
    for n, chosen in enumerate(chunks):
        limit = LIMIT if n else 2 * LIMIT + LIMIT // 2
        half = right_call([last], nears[n], me, second, view, chosen, ranks, states, piece, limit)
        last = half[0]
        lines.append(exchanged(half, "rad"))
    backs = []
    for line in lines:
        moved = left_call([last], me, first, line)
        last = moved[0]
        backs.append(exchanged(moved, "rad"))

    angles = potential.transpose(1, 0, 2)
    cosine, sine = jnp.cos(angles), jnp.sin(angles)
    edge = phase_call([last], me, second, cosine, sine, backs[0])
    low, high = edge[:PIECES], edge[-PIECES:]
    below = [neighbour(x, "hel", 1) for x in high]
    above = [neighbour(x, "hel", -1) for x in low]

    count = coupling.shape[0]
    helicities = jnp.arange(count, dtype=jnp.int32)
    couple_up = jnp.where(helicities[:, None] < count - 1, coupling, 0.0)
    couple_down = jnp.concatenate(
        [jnp.zeros((1, coupling.shape[1]), jnp.float32), coupling[:-1]], axis=0
    )
    start = lax.axis_index("hel") * blocks
    up = lax.dynamic_slice_in_dim(couple_up, start, blocks, 0)
    down = lax.dynamic_slice_in_dim(couple_down, start, blocks, 0)
    known = [*below, *low, *high, *above]
    out = mix_call(
        me, up, down, second, cosine, sine, radial_weight, chunks[1], backs[1], known
    )
    out = out.reshape(rows, 2, blocks, tiles, states, LANES).transpose(0, 1, 2, 4, 3, 5)
    return out.reshape(rows, 2, blocks, states, width)


def solution(mesh):
    return jax.shard_map(
        per_device,
        mesh=mesh,
        in_specs=(
            P("rad", None, "hel", None, None),
            P(),
            P(),
            P("rad", None, None),
            P(),
            P("rad", None),
        ),
        out_specs=P("rad", None, "hel", None, None),
        check_vma=False,
    )
```

```python
import functools

import jax
import jax.numpy as jnp
from jax import lax
from jax.experimental import pallas as pl
from jax.experimental.pallas import tpu as pltpu
from jax.sharding import PartitionSpec as P

LANES = 128
PIECES = 2
LIMIT = 20 * 1024 * 1024
SMEM = pl.BlockSpec(memory_space=pltpu.SMEM)
AFTER = pl.BlockSpec(memory_space=pl.ANY)


def params(limit=LIMIT):
    return pltpu.CompilerParams(vmem_limit_bytes=limit)


def cost(flops, moved):
    return pl.CostEstimate(flops=flops, bytes_accessed=moved, transcendentals=0)


def complex_rows(real, imag):
    return jnp.concatenate([real, -imag], 1), jnp.concatenate([imag, real], 1)


def near_slabs(me, near):
    return pl.ds(me & -near, near)


def slab_specs(near, ranks, kinds, block, wide):
    return [pl.BlockSpec((near, kinds, block, wide), lambda i: (0, 0, i, 0))] + [
        pl.BlockSpec((kinds, block, wide), lambda i: (0, i, 0))
    ] * (ranks - near)


def sources(me, near, parts, n):
    for low in range(near):
        yield (me & -near) + low, parts[0][low, n]
    for s, part in enumerate(parts[1:], near):
        yield me ^ s, part[n]


def right_kernel(after, near, ranks, states, me_ref, second_ref, *refs):
    refs = refs[after:]
    kinds = len(refs) - 2 - (ranks - near)
    packets, outs, slabs = refs[:kinds], refs[kinds:-1], refs[-1]
    me = me_ref[0]
    rows = packets[0].shape[0]
    group = packets[0].shape[2]
    tiles = group // states
    piece = slabs.shape[2] // 2
    cuts = tiles * LANES // piece
    for n, packet in enumerate(packets):
        turned = [
            packet[:, c].astype(jnp.float32).transpose(1, 0, 2).astype(jnp.bfloat16)
            for c in range(2)
        ]

        def part(c, j):
            return jnp.concatenate([turned[c][t * states + j] for t in range(tiles)], 1)

        pairs = [complex_rows(part(0, j), part(1, j)) for j in range(states)]
        left = jnp.concatenate([p[0] for p in pairs] + [p[1] for p in pairs], 0)
        product = jnp.dot(left, second_ref[...], preferred_element_type=jnp.float32)
        product = product.astype(jnp.bfloat16)
        for c in range(2):
            for j in range(states):
                first = (c * states + j) * rows
                for p in range(cuts):
                    slabs[j * cuts + p, :, c * piece : (c + 1) * piece] = product[
                        first : first + rows, p * piece : (p + 1) * piece
                    ]
        outs[0][:, n] = slabs[near_slabs(me, near)]
        for s, out in enumerate(outs[1:], near):
            out[n] = slabs[me ^ s]


def right_call(after, near, me, second, view, chosen, ranks, states, piece, limit):
    rows, _, _, group, _ = view.shape
    width = second.shape[1]
    block = rows // 2
    kinds = len(chosen)
    return pl.pallas_call(
        functools.partial(right_kernel, len(after), near, ranks, states),
        grid=(rows // block,),
        in_specs=[SMEM, pl.BlockSpec(second.shape, lambda i: (0, 0))]
        + [AFTER] * len(after)
        + [
            pl.BlockSpec((block, 2, None, group, LANES), lambda i, k=k: (i, 0, k, 0, 0))
            for k in chosen
        ],
        out_specs=slab_specs(near, ranks, kinds, block, 2 * piece),
        out_shape=[jax.ShapeDtypeStruct((near, kinds, rows, 2 * piece), jnp.bfloat16)]
        + [jax.ShapeDtypeStruct((kinds, rows, 2 * piece), jnp.bfloat16)] * (ranks - near),
        scratch_shapes=[
            pltpu.VMEM((ranks, block, 2 * piece), jnp.bfloat16),
        ],
        compiler_params=params(limit),
        cost_estimate=cost(
            8 * kinds * states * rows * width * width, 8 * kinds * states * rows * width
        ),
        name="right",
    )(me, second, *after, *([view] * kinds))


def left_kernel(after, near, ranks, me_ref, first_ref, *refs):
    refs = refs[after:]
    count = 1 + ranks - near
    ins, outs, lines, slabs = refs[:count], refs[count:-2], refs[-2], refs[-1]
    me = me_ref[0]
    _, _, rows, wide = ins[0].shape
    piece = wide // 2
    whole = ranks * rows
    for source, value in sources(me, near, ins, 0):
        first = pl.multiple_of(source * rows, rows)
        lines[pl.ds(first, rows), :] = value
        lines[pl.ds(first + whole, rows), :] = jnp.concatenate(
            [-value[:, piece:], value[:, :piece]], 1
        )
    product = jnp.dot(first_ref[...], lines[...], preferred_element_type=jnp.float32)
    slabs[...] = product.astype(jnp.bfloat16).reshape(ranks, rows, wide)
    outs[0][:, 0] = slabs[near_slabs(me, near)]
    for s, out in enumerate(outs[1:], near):
        out[0] = slabs[me ^ s]


def left_call(after, me, first, slabs):
    near, kinds, rows, wide = slabs[0].shape
    ranks = len(slabs) - 1 + near
    whole = ranks * rows
    specs = [pl.BlockSpec((near, 1, rows, wide), lambda i: (0, i, 0, 0))] + [
        pl.BlockSpec((1, rows, wide), lambda i: (i, 0, 0))
    ] * (ranks - near)
    return pl.pallas_call(
        functools.partial(left_kernel, len(after), near, ranks),
        grid=(kinds,),
        in_specs=[SMEM, pl.BlockSpec(first.shape, lambda i: (0, 0))]
        + [AFTER] * len(after)
        + specs,
        out_specs=specs,
        out_shape=[jax.ShapeDtypeStruct(x.shape, jnp.bfloat16) for x in slabs],
        scratch_shapes=[
            pltpu.VMEM((2 * whole, wide), jnp.bfloat16),
            pltpu.VMEM((ranks, rows, wide), jnp.bfloat16),
        ],
        compiler_params=params(),
        cost_estimate=cost(
            4 * kinds * whole * whole * wide, 4 * whole * whole + 4 * kinds * whole * wide
        ),
        name="left",
    )(me, first, *after, *slabs)


def phased_product(me, n, near, second_ref, cosine_ref, sine_ref, ins, slabs):
    states, _, width = cosine_ref.shape
    piece = slabs.shape[2] // 2
    cuts = width // piece
    for source, value in sources(me, near, ins, n):
        slabs[source] = value
    pairs = []
    for j in range(states):
        real, imag = (
            jnp.concatenate(
                [slabs[j * cuts + p, :, c * piece : (c + 1) * piece] for p in range(cuts)], 1
            ).astype(jnp.float32)
            for c in range(2)
        )
        cosine, sine = cosine_ref[j], sine_ref[j]
        pairs.append(
            complex_rows(
                (real * cosine + imag * sine).astype(jnp.bfloat16),
                (imag * cosine - real * sine).astype(jnp.bfloat16),
            )
        )
    left = jnp.concatenate([p[0] for p in pairs] + [p[1] for p in pairs], 0)
    product = jnp.dot(left, second_ref[...], preferred_element_type=jnp.float32)
    return product.astype(jnp.bfloat16)


def phase_kernel(after, near, ranks, me_ref, second_ref, cosine_ref, sine_ref, *refs):
    refs = refs[after:]
    count = 1 + ranks - near
    ins, outs, slabs = refs[:count], refs[count:-1], refs[-1]
    states, rows, _ = cosine_ref.shape
    share = outs[0].shape[1]
    pieces = states // share
    for n in range(len(outs) // pieces):
        product = phased_product(
            me_ref[0], n, near, second_ref, cosine_ref, sine_ref, ins, slabs
        )
        for c in range(2):
            for j in range(states):
                first = (c * states + j) * rows
                outs[n * pieces + j // share][c, j % share] = product[first : first + rows]


def phase_call(after, me, second, cosine, sine, slabs):
    near, kinds, rows, wide = slabs[0].shape
    ranks = len(slabs) - 1 + near
    states, _, width = cosine.shape
    block = rows // 2
    share = states // PIECES
    count = kinds * PIECES
    table = pl.BlockSpec((states, block, width), lambda i: (0, i, 0))
    return pl.pallas_call(
        functools.partial(phase_kernel, len(after), near, ranks),
        grid=(rows // block,),
        in_specs=[SMEM, pl.BlockSpec(second.shape, lambda i: (0, 0)), table, table]
        + [AFTER] * len(after)
        + slab_specs(near, ranks, kinds, block, wide),
        out_specs=[pl.BlockSpec((2, share, block, width), lambda i: (0, 0, i, 0))] * count,
        out_shape=[jax.ShapeDtypeStruct((2, share, rows, width), jnp.bfloat16)] * count,
        scratch_shapes=[pltpu.VMEM((ranks, block, wide), jnp.bfloat16)],
        compiler_params=params(),
        cost_estimate=cost(
            8 * kinds * states * rows * width * width, 8 * kinds * states * rows * width
        ),
        name="phase",
    )(me, second, cosine, sine, *after, *slabs)


def mix_kernel(
    chosen, near, ranks, me_ref, up_ref, down_ref, second_ref, cosine_ref, sine_ref, weight_ref, *refs
):
    count = 1 + ranks - near
    ins, known, (out, slabs, fresh) = refs[:count], refs[count:-3], refs[-3:]
    blocks, states = up_ref.shape
    rows, width = weight_ref.shape
    share = known[0].shape[1]
    pieces = states // share
    group = out.shape[3]
    weight = weight_ref[...]
    others = [k for k in range(-1, blocks + 1) if k not in chosen]
    for n in range(len(chosen)):
        product = phased_product(
            me_ref[0], n, near, second_ref, cosine_ref, sine_ref, ins, slabs
        )
        fresh[n] = product.reshape(2, states, rows, width)

    def kinetic(k, c, j):
        if k in chosen:
            value = fresh[chosen.index(k), c, j]
        else:
            value = known[others.index(k) * pieces + j // share][c, j % share]
        return value.astype(jnp.float32)

    for k in range(blocks):
        columns = [[None] * group for _ in range(2)]
        for j in range(states):
            up, down = up_ref[k, j], down_ref[k, j]
            mixed = [up * kinetic(k + 1, c, j) + down * kinetic(k - 1, c, j) for c in range(2)]
            parts = (
                kinetic(k, 0, j) + weight * mixed[1],
                kinetic(k, 1, j) - weight * mixed[0],
            )
            for c in range(2):
                for t in range(width // LANES):
                    columns[c][t * states + j] = parts[c][:, t * LANES : (t + 1) * LANES]
        for c in range(2):
            out[:, c, k] = jnp.stack(columns[c], 0).transpose(1, 0, 2).astype(jnp.bfloat16)


def mix_call(me, up, down, second, cosine, sine, weight, chosen, slabs, known):
    near, kinds, rows, wide = slabs[0].shape
    ranks = len(slabs) - 1 + near
    _, share, _, width = known[0].shape
    blocks, states = up.shape
    group = width // LANES * states
    block = rows // 4
    table = pl.BlockSpec((states, block, width), lambda i: (0, i, 0))
    return pl.pallas_call(
        functools.partial(mix_kernel, tuple(chosen), near, ranks),
        grid=(rows // block,),
        in_specs=[SMEM] * 3
        + [pl.BlockSpec(second.shape, lambda i: (0, 0)), table, table]
        + [pl.BlockSpec((block, width), lambda i: (i, 0))]
        + slab_specs(near, ranks, kinds, block, wide)
        + [pl.BlockSpec((2, share, block, width), lambda i: (0, 0, i, 0))] * len(known),
        out_specs=pl.BlockSpec((block, 2, blocks, group, LANES), lambda i: (i, 0, 0, 0, 0)),
        out_shape=jax.ShapeDtypeStruct((rows, 2, blocks, group, LANES), jnp.bfloat16),
        scratch_shapes=[
            pltpu.VMEM((ranks, block, wide), jnp.bfloat16),
            pltpu.VMEM((kinds, 2, states, block, width), jnp.bfloat16),
        ],
        compiler_params=params(),
        cost_estimate=cost(
            8 * kinds * states * rows * width * width, 10 * blocks * states * rows * width
        ),
        name="mix",
    )(me, up, down, second, cosine, sine, weight, *slabs, *known)


def exchanged(slabs, axis):
    count = lax.axis_size(axis)
    near = slabs[0].shape[0]
    result = [slabs[0]]
    if near == count:
        result = [lax.all_to_all(slabs[0], axis, 0, 0, tiled=True)]
    elif near > 1:
        groups = [list(range(i, i + near)) for i in range(0, count, near)]
        result = [lax.all_to_all(slabs[0], axis, 0, 0, axis_index_groups=groups, tiled=True)]
    for s, slab in enumerate(slabs[1:], near):
        result.append(lax.ppermute(slab, axis, [(i, i ^ s) for i in range(count)]))
    return result


def neighbour(edge, axis, step):
    count = lax.axis_size(axis)
    pairs = [(i, i + step) for i in range(count) if 0 <= i + step < count]
    return lax.ppermute(edge, axis, pairs)


def per_device(packet, first_propagator, second_propagator, potential, coupling, radial_weight):
    rows, _, blocks, states, width = packet.shape
    ranks = lax.axis_size("rad")
    whole = first_propagator.shape[1]
    tiles = width // LANES
    piece = states * width // ranks
    me = lax.axis_index("rad").astype(jnp.int32).reshape(1)
    second = second_propagator.reshape(2 * width, width)
    first = first_propagator.reshape(2 * whole, whole).T
    view = packet.reshape(rows, 2, blocks, states, tiles, LANES).transpose(0, 1, 2, 4, 3, 5)
    view = view.reshape(rows, 2, blocks, tiles * states, LANES)
    edges = sorted({0, blocks - 1})
    chunks = [edges, [k for k in range(blocks) if k not in edges]]

    nears = (ranks, 1)
    last = me
    lines = []
    for n, chosen in enumerate(chunks):
        limit = LIMIT if n else 2 * LIMIT + LIMIT // 2
        half = right_call([last], nears[n], me, second, view, chosen, ranks, states, piece, limit)
        last = half[0]
        lines.append(exchanged(half, "rad"))
    backs = []
    for line in lines:
        moved = left_call([last], me, first, line)
        last = moved[0]
        backs.append(exchanged(moved, "rad"))

    angles = potential.transpose(1, 0, 2)
    cosine, sine = jnp.cos(angles), jnp.sin(angles)
    edge = phase_call([last], me, second, cosine, sine, backs[0])
    low, high = edge[:PIECES], edge[-PIECES:]
    below = [neighbour(x, "hel", 1) for x in high]
    above = [neighbour(x, "hel", -1) for x in low]

    count = coupling.shape[0]
    helicities = jnp.arange(count, dtype=jnp.int32)
    couple_up = jnp.where(helicities[:, None] < count - 1, coupling, 0.0)
    couple_down = jnp.concatenate(
        [jnp.zeros((1, coupling.shape[1]), jnp.float32), coupling[:-1]], axis=0
    )
    start = lax.axis_index("hel") * blocks
    up = lax.dynamic_slice_in_dim(couple_up, start, blocks, 0)
    down = lax.dynamic_slice_in_dim(couple_down, start, blocks, 0)
    known = [*below, *low, *high, *above]
    out = mix_call(
        me, up, down, second, cosine, sine, radial_weight, chunks[1], backs[1], known
    )
    out = out.reshape(rows, 2, blocks, tiles, states, LANES).transpose(0, 1, 2, 4, 3, 5)
    return out.reshape(rows, 2, blocks, states, width)


def solution(mesh):
    return jax.shard_map(
        per_device,
        mesh=mesh,
        in_specs=(
            P("rad", None, "hel", None, None),
            P(),
            P(),
            P("rad", None, None),
            P(),
            P("rad", None),
        ),
        out_specs=P("rad", None, "hel", None, None),
        check_vma=False,
    )
```

```python
import functools

import jax
import jax.numpy as jnp
from jax import lax
from jax.experimental import pallas as pl
from jax.experimental.pallas import tpu as pltpu
from jax.sharding import PartitionSpec as P

LANES = 128
ROWS = 16
PIECES = 4
LIMIT = 18 * 1024 * 1024
WHOLE = 3 * LIMIT
SMEM = pl.BlockSpec(memory_space=pltpu.SMEM)
AFTER = pl.BlockSpec(memory_space=pl.ANY)


def params(limit=LIMIT):
    return pltpu.CompilerParams(vmem_limit_bytes=limit)


def in_place(arrays):
    return [pltpu.with_memory_space_constraint(x, pltpu.VMEM) for x in arrays]


def cost(flops, moved):
    return pl.CostEstimate(flops=flops, bytes_accessed=moved, transcendentals=0)


def complex_rows(real, imag):
    return jnp.concatenate([real, -imag], 1), jnp.concatenate([imag, real], 1)


def right_kernel(after, ranks, states, me_ref, second_ref, *refs):
    refs = refs[after:]
    kinds = len(refs) - 1 - ranks
    packets, outs, slabs = refs[:kinds], refs[kinds:-1], refs[-1]
    me = me_ref[0]
    rows = packets[0].shape[0]
    group = packets[0].shape[2]
    tiles = group // states
    piece = slabs.shape[2] // 2
    cuts = tiles * LANES // piece
    for n, packet in enumerate(packets):
        turned = [
            packet[:, c].astype(jnp.float32).transpose(1, 0, 2).astype(jnp.bfloat16)
            for c in range(2)
        ]

        def part(c, j):
            return jnp.concatenate([turned[c][t * states + j] for t in range(tiles)], 1)

        pairs = [complex_rows(part(0, j), part(1, j)) for j in range(states)]
        left = jnp.concatenate([p[0] for p in pairs] + [p[1] for p in pairs], 0)
        product = jnp.dot(left, second_ref[...], preferred_element_type=jnp.float32)
        product = product.astype(jnp.bfloat16)
        for c in range(2):
            for j in range(states):
                first = (c * states + j) * rows
                for p in range(cuts):
                    slabs[j * cuts + p, :, c * piece : (c + 1) * piece] = product[
                        first : first + rows, p * piece : (p + 1) * piece
                    ]
        for s, out in enumerate(outs):
            out[n] = slabs[me ^ s]


def right_call(after, me, second, view, chosen, ranks, states, piece, limit):
    rows, _, _, group, _ = view.shape
    width = second.shape[1]
    block = rows // 2
    kinds = len(chosen)
    return pl.pallas_call(
        functools.partial(right_kernel, len(after), ranks, states),
        grid=(rows // block,),
        in_specs=[SMEM, pl.BlockSpec(second.shape, lambda i: (0, 0))]
        + [AFTER] * len(after)
        + [
            pl.BlockSpec((block, 2, None, group, LANES), lambda i, k=k: (i, 0, k, 0, 0))
            for k in chosen
        ],
        out_specs=[pl.BlockSpec((kinds, block, 2 * piece), lambda i: (0, i, 0))] * ranks,
        out_shape=[jax.ShapeDtypeStruct((kinds, rows, 2 * piece), jnp.bfloat16)] * ranks,
        scratch_shapes=[
            pltpu.VMEM((ranks, block, 2 * piece), jnp.bfloat16),
        ],
        compiler_params=params(limit),
        cost_estimate=cost(
            8 * kinds * states * rows * width * width, 8 * kinds * states * rows * width
        ),
        name="right",
    )(me, second, *after, *([view] * kinds))


def left_kernel(after, ranks, me_ref, first_ref, *refs):
    refs = refs[after:]
    ins, outs, lines, slabs = refs[:ranks], refs[ranks:-2], refs[-2], refs[-1]
    me = me_ref[0]
    rows, wide = ins[0].shape
    piece = wide // 2
    whole = ranks * rows
    for s, part in enumerate(ins):
        value = part[...]
        first = pl.multiple_of((me ^ s) * rows, rows)
        lines[pl.ds(first, rows), :] = value
        lines[pl.ds(first + whole, rows), :] = jnp.concatenate(
            [-value[:, piece:], value[:, :piece]], 1
        )
    product = jnp.dot(first_ref[...], lines[...], preferred_element_type=jnp.float32)
    slabs[...] = product.astype(jnp.bfloat16).reshape(ranks, rows, wide)
    for s, out in enumerate(outs):
        out[...] = slabs[me ^ s]


def left_call(after, me, first, slabs):
    ranks = len(slabs)
    kinds, rows, wide = slabs[0].shape
    whole = ranks * rows
    spec = pl.BlockSpec((None, rows, wide), lambda i: (i, 0, 0))
    return pl.pallas_call(
        functools.partial(left_kernel, len(after), ranks),
        grid=(kinds,),
        in_specs=[SMEM, pl.BlockSpec(first.shape, lambda i: (0, 0))]
        + [AFTER] * len(after)
        + [spec] * ranks,
        out_specs=[spec] * ranks,
        out_shape=[jax.ShapeDtypeStruct(slabs[0].shape, jnp.bfloat16)] * ranks,
        scratch_shapes=[
            pltpu.VMEM((2 * whole, wide), jnp.bfloat16),
            pltpu.VMEM((ranks, rows, wide), jnp.bfloat16),
        ],
        compiler_params=params(),
        cost_estimate=cost(
            4 * kinds * whole * whole * wide, 4 * whole * whole + 4 * kinds * whole * wide
        ),
        name="left",
    )(me, first, *after, *slabs)


def phased_product(me, n, second_ref, cosine_ref, sine_ref, ins, order, slabs):
    states, _, width = cosine_ref.shape
    piece = slabs.shape[2] // 2
    cuts = width // piece
    for s, part in zip(order, ins):
        slabs[me ^ s] = part[n]
    pairs = []
    for j in range(states):
        real, imag = (
            jnp.concatenate(
                [slabs[j * cuts + p, :, c * piece : (c + 1) * piece] for p in range(cuts)], 1
            ).astype(jnp.float32)
            for c in range(2)
        )
        cosine, sine = cosine_ref[j], sine_ref[j]
        pairs.append(
            complex_rows(
                (real * cosine + imag * sine).astype(jnp.bfloat16),
                (imag * cosine - real * sine).astype(jnp.bfloat16),
            )
        )
    left = jnp.concatenate([p[0] for p in pairs] + [p[1] for p in pairs], 0)
    product = jnp.dot(left, second_ref[...], preferred_element_type=jnp.float32)
    return product.astype(jnp.bfloat16)


def phase_kernel(after, ranks, me_ref, second_ref, cosine_ref, sine_ref, *refs):
    refs = refs[after:]
    ins, outs, slabs = refs[:ranks], refs[ranks:-1], refs[-1]
    states, rows, _ = cosine_ref.shape
    share = outs[0].shape[1]
    pieces = states // share
    for n in range(len(outs) // pieces):
        product = phased_product(
            me_ref[0], n, second_ref, cosine_ref, sine_ref, ins, range(ranks), slabs
        )
        for c in range(2):
            for j in range(states):
                first = (c * states + j) * rows
                outs[n * pieces + j // share][c, j % share] = product[first : first + rows]


def phase_call(after, me, second, cosine, sine, slabs):
    ranks = len(slabs)
    kinds, rows, wide = slabs[0].shape
    states, _, width = cosine.shape
    block = rows // 2
    share = states // PIECES
    count = kinds * PIECES
    table = pl.BlockSpec((states, block, width), lambda i: (0, i, 0))
    return pl.pallas_call(
        functools.partial(phase_kernel, len(after), ranks),
        grid=(rows // block,),
        in_specs=[SMEM, pl.BlockSpec(second.shape, lambda i: (0, 0)), table, table]
        + [AFTER] * len(after)
        + [pl.BlockSpec((kinds, block, wide), lambda i: (0, i, 0))] * ranks,
        out_specs=[pl.BlockSpec((2, share, block, width), lambda i: (0, 0, i, 0))] * count,
        out_shape=[jax.ShapeDtypeStruct((2, share, rows, width), jnp.bfloat16)] * count,
        scratch_shapes=[pltpu.VMEM((ranks, block, wide), jnp.bfloat16)],
        compiler_params=params(),
        cost_estimate=cost(
            8 * kinds * states * rows * width * width, 8 * kinds * states * rows * width
        ),
        name="phase",
    )(me, second, cosine, sine, *after, *slabs)


def mix_kernel(
    chosen, order, me_ref, up_ref, down_ref, second_ref, cosine_ref, sine_ref, weight_ref, *refs
):
    ranks = len(order)
    ins, known, (out, slabs, fresh) = refs[:ranks], refs[ranks:-3], refs[-3:]
    blocks, states = up_ref.shape
    rows, width = weight_ref.shape
    share = known[0].shape[1]
    pieces = states // share
    group = out.shape[3]
    others = [k for k in range(-1, blocks + 1) if k not in chosen]
    for n in range(len(chosen)):
        product = phased_product(
            me_ref[0], n, second_ref, cosine_ref, sine_ref, ins, order, slabs
        )
        fresh[n] = product.reshape(2, states, rows, width)

    def kinetic(k, c, j, span):
        if k in chosen:
            value = fresh[chosen.index(k), c, j, span]
        else:
            value = known[others.index(k) * pieces + j // share][c, j % share, span]
        return value.astype(jnp.float32)

    for first in range(0, rows, ROWS):
        span = slice(first, first + ROWS)
        weight = weight_ref[span]
        for k in range(blocks):
            columns = [[None] * group for _ in range(2)]
            for j in range(states):
                up, down = up_ref[k, j], down_ref[k, j]
                mixed = [
                    up * kinetic(k + 1, c, j, span) + down * kinetic(k - 1, c, j, span)
                    for c in range(2)
                ]
                parts = (
                    kinetic(k, 0, j, span) + weight * mixed[1],
                    kinetic(k, 1, j, span) - weight * mixed[0],
                )
                for c in range(2):
                    for t in range(width // LANES):
                        columns[c][t * states + j] = parts[c][:, t * LANES : (t + 1) * LANES]
            for c in range(2):
                out[span, c, k] = jnp.stack(columns[c], 0).transpose(1, 0, 2).astype(jnp.bfloat16)


def mix_call(me, up, down, second, cosine, sine, weight, chosen, slabs, known):
    ranks = len(slabs)
    order = tuple(range(ranks))
    kinds, rows, wide = slabs[0].shape
    _, share, _, width = known[0].shape
    blocks, states = up.shape
    group = width // LANES * states
    block = rows // 4
    table = pl.BlockSpec((states, block, width), lambda i: (0, i, 0))
    return pl.pallas_call(
        functools.partial(mix_kernel, tuple(chosen), order),
        grid=(rows // block,),
        in_specs=[SMEM] * 3
        + [pl.BlockSpec(second.shape, lambda i: (0, 0)), table, table]
        + [pl.BlockSpec((block, width), lambda i: (i, 0))]
        + [pl.BlockSpec((kinds, block, wide), lambda i: (0, i, 0))] * ranks
        + [pl.BlockSpec((2, share, block, width), lambda i: (0, 0, i, 0))] * len(known),
        out_specs=pl.BlockSpec((block, 2, blocks, group, LANES), lambda i: (i, 0, 0, 0, 0)),
        out_shape=jax.ShapeDtypeStruct((rows, 2, blocks, group, LANES), jnp.bfloat16),
        scratch_shapes=[
            pltpu.VMEM((ranks, block, wide), jnp.bfloat16),
            pltpu.VMEM((kinds, 2, states, block, width), jnp.bfloat16),
        ],
        compiler_params=params(),
        cost_estimate=cost(
            8 * kinds * states * rows * width * width, 10 * blocks * states * rows * width
        ),
        name="mix",
    )(me, up, down, second, cosine, sine, weight, *in_place([slabs[s] for s in order] + known))


def exchanged(slabs, axis):
    count = lax.axis_size(axis)
    result = [slabs[0]] + [None] * (count - 1)
    for s in reversed(range(1, count)):
        result[s] = lax.ppermute(slabs[s], axis, [(i, i ^ s) for i in range(count)])
    return result


def neighbour(edge, axis, step):
    count = lax.axis_size(axis)
    pairs = [(i, i + step) for i in range(count) if 0 <= i + step < count]
    return lax.ppermute(edge, axis, pairs)


def per_device(packet, first_propagator, second_propagator, potential, coupling, radial_weight):
    rows, _, blocks, states, width = packet.shape
    ranks = lax.axis_size("rad")
    whole = first_propagator.shape[1]
    tiles = width // LANES
    piece = states * width // ranks
    me = lax.axis_index("rad").astype(jnp.int32).reshape(1)
    second = second_propagator.reshape(2 * width, width)
    first = first_propagator.reshape(2 * whole, whole).T
    view = packet.reshape(rows, 2, blocks, states, tiles, LANES).transpose(0, 1, 2, 4, 3, 5)
    view = view.reshape(rows, 2, blocks, tiles * states, LANES)
    edges = sorted({0, blocks - 1})
    chunks = [edges, [k for k in range(blocks) if k not in edges]]

    last = me
    lines = []
    for n, chosen in enumerate(chunks):
        limit = LIMIT if n else WHOLE
        half = right_call([last], me, second, view, chosen, ranks, states, piece, limit)
        last = half[0]
        lines.append(exchanged(half, "rad"))
    backs = []
    for line in lines:
        moved = left_call([last], me, first, line)
        last = moved[0]
        backs.append(exchanged(moved, "rad"))

    angles = potential.transpose(1, 0, 2)
    cosine, sine = jnp.cos(angles), jnp.sin(angles)
    edge = phase_call([last], me, second, cosine, sine, backs[0])
    low, high = edge[:PIECES], edge[-PIECES:]
    below = [neighbour(x, "hel", 1) for x in high]
    above = [neighbour(x, "hel", -1) for x in low]

    count = coupling.shape[0]
    helicities = jnp.arange(count, dtype=jnp.int32)
    couple_up = jnp.where(helicities[:, None] < count - 1, coupling, 0.0)
    couple_down = jnp.concatenate(
        [jnp.zeros((1, coupling.shape[1]), jnp.float32), coupling[:-1]], axis=0
    )
    start = lax.axis_index("hel") * blocks
    up = lax.dynamic_slice_in_dim(couple_up, start, blocks, 0)
    down = lax.dynamic_slice_in_dim(couple_down, start, blocks, 0)
    known = [*below, *low, *high, *above]
    out = mix_call(
        me, up, down, second, cosine, sine, radial_weight, chunks[1], backs[1], known
    )
    out = out.reshape(rows, 2, blocks, tiles, states, LANES).transpose(0, 1, 2, 4, 3, 5)
    return out.reshape(rows, 2, blocks, states, width)


def solution(mesh):
    return jax.shard_map(
        per_device,
        mesh=mesh,
        in_specs=(
            P("rad", None, "hel", None, None),
            P(),
            P(),
            P("rad", None, None),
            P(),
            P("rad", None),
        ),
        out_specs=P("rad", None, "hel", None, None),
        check_vma=False,
    )
```

```python
import functools

import jax
import jax.numpy as jnp
from jax import lax
from jax.experimental import pallas as pl
from jax.experimental.pallas import tpu as pltpu
from jax.sharding import PartitionSpec as P

LANES = 128
ROWS = 16
PIECES = 4
LIMIT = 18 * 1024 * 1024
WHOLE = 3 * LIMIT
SMEM = pl.BlockSpec(memory_space=pltpu.SMEM)
AFTER = pl.BlockSpec(memory_space=pl.ANY)


def params(limit=LIMIT):
    return pltpu.CompilerParams(vmem_limit_bytes=limit)


def in_place(arrays):
    return [pltpu.with_memory_space_constraint(x, pltpu.HBM) for x in arrays]


def cost(flops, moved):
    return pl.CostEstimate(flops=flops, bytes_accessed=moved, transcendentals=0)


def complex_rows(real, imag):
    return jnp.concatenate([real, -imag], 1), jnp.concatenate([imag, real], 1)


def right_kernel(after, ranks, states, me_ref, second_ref, *refs):
    refs = refs[after:]
    kinds = len(refs) - 1 - ranks
    packets, outs, slabs = refs[:kinds], refs[kinds:-1], refs[-1]
    me = me_ref[0]
    rows = packets[0].shape[0]
    group = packets[0].shape[2]
    tiles = group // states
    piece = slabs.shape[2] // 2
    cuts = tiles * LANES // piece
    for n, packet in enumerate(packets):
        turned = [
            packet[:, c].astype(jnp.float32).transpose(1, 0, 2).astype(jnp.bfloat16)
            for c in range(2)
        ]

        def part(c, j):
            return jnp.concatenate([turned[c][t * states + j] for t in range(tiles)], 1)

        pairs = [complex_rows(part(0, j), part(1, j)) for j in range(states)]
        left = jnp.concatenate([p[0] for p in pairs] + [p[1] for p in pairs], 0)
        product = jnp.dot(left, second_ref[...], preferred_element_type=jnp.float32)
        product = product.astype(jnp.bfloat16)
        for c in range(2):
            for j in range(states):
                first = (c * states + j) * rows
                for p in range(cuts):
                    slabs[j * cuts + p, :, c * piece : (c + 1) * piece] = product[
                        first : first + rows, p * piece : (p + 1) * piece
                    ]
        for s, out in enumerate(outs):
            out[n] = slabs[me ^ s]


def right_call(after, me, second, view, chosen, ranks, states, piece, limit):
    rows, _, _, group, _ = view.shape
    width = second.shape[1]
    block = rows // 2
    kinds = len(chosen)
    return pl.pallas_call(
        functools.partial(right_kernel, len(after), ranks, states),
        grid=(rows // block,),
        in_specs=[SMEM, pl.BlockSpec(second.shape, lambda i: (0, 0))]
        + [AFTER] * len(after)
        + [
            pl.BlockSpec((block, 2, None, group, LANES), lambda i, k=k: (i, 0, k, 0, 0))
            for k in chosen
        ],
        out_specs=[pl.BlockSpec((kinds, block, 2 * piece), lambda i: (0, i, 0))] * ranks,
        out_shape=[jax.ShapeDtypeStruct((kinds, rows, 2 * piece), jnp.bfloat16)] * ranks,
        scratch_shapes=[
            pltpu.VMEM((ranks, block, 2 * piece), jnp.bfloat16),
        ],
        compiler_params=params(limit),
        cost_estimate=cost(
            8 * kinds * states * rows * width * width, 8 * kinds * states * rows * width
        ),
        name="right",
    )(me, second, *after, *([view] * kinds))


def left_kernel(after, ranks, me_ref, first_ref, *refs):
    refs = refs[after:]
    ins, outs, lines, slabs = refs[:ranks], refs[ranks:-2], refs[-2], refs[-1]
    me = me_ref[0]
    rows, wide = ins[0].shape
    piece = wide // 2
    whole = ranks * rows
    for s, part in enumerate(ins):
        value = part[...]
        first = pl.multiple_of((me ^ s) * rows, rows)
        lines[pl.ds(first, rows), :] = value
        lines[pl.ds(first + whole, rows), :] = jnp.concatenate(
            [-value[:, piece:], value[:, :piece]], 1
        )
    product = jnp.dot(first_ref[...], lines[...], preferred_element_type=jnp.float32)
    slabs[...] = product.astype(jnp.bfloat16).reshape(ranks, rows, wide)
    for s, out in enumerate(outs):
        out[...] = slabs[me ^ s]


def left_call(after, me, first, slabs):
    ranks = len(slabs)
    kinds, rows, wide = slabs[0].shape
    whole = ranks * rows
    spec = pl.BlockSpec((None, rows, wide), lambda i: (i, 0, 0))
    return pl.pallas_call(
        functools.partial(left_kernel, len(after), ranks),
        grid=(kinds,),
        in_specs=[SMEM, pl.BlockSpec(first.shape, lambda i: (0, 0))]
        + [AFTER] * len(after)
        + [spec] * ranks,
        out_specs=[spec] * ranks,
        out_shape=[jax.ShapeDtypeStruct(slabs[0].shape, jnp.bfloat16)] * ranks,
        scratch_shapes=[
            pltpu.VMEM((2 * whole, wide), jnp.bfloat16),
            pltpu.VMEM((ranks, rows, wide), jnp.bfloat16),
        ],
        compiler_params=params(),
        cost_estimate=cost(
            4 * kinds * whole * whole * wide, 4 * whole * whole + 4 * kinds * whole * wide
        ),
        name="left",
    )(me, first, *after, *slabs)


def phased_product(me, n, second_ref, cosine_ref, sine_ref, ins, order, slabs):
    states, _, width = cosine_ref.shape
    piece = slabs.shape[2] // 2
    cuts = width // piece
    for s, part in zip(order, ins):
        slabs[me ^ s] = part[n]
    pairs = []
    for j in range(states):
        real, imag = (
            jnp.concatenate(
                [slabs[j * cuts + p, :, c * piece : (c + 1) * piece] for p in range(cuts)], 1
            ).astype(jnp.float32)
            for c in range(2)
        )
        cosine, sine = cosine_ref[j], sine_ref[j]
        pairs.append(
            complex_rows(
                (real * cosine + imag * sine).astype(jnp.bfloat16),
                (imag * cosine - real * sine).astype(jnp.bfloat16),
            )
        )
    left = jnp.concatenate([p[0] for p in pairs] + [p[1] for p in pairs], 0)
    product = jnp.dot(left, second_ref[...], preferred_element_type=jnp.float32)
    return product.astype(jnp.bfloat16)


def phase_kernel(after, ranks, me_ref, second_ref, cosine_ref, sine_ref, *refs):
    refs = refs[after:]
    ins, outs, slabs = refs[:ranks], refs[ranks:-1], refs[-1]
    states, rows, _ = cosine_ref.shape
    share = outs[0].shape[1]
    pieces = states // share
    for n in range(len(outs) // pieces):
        product = phased_product(
            me_ref[0], n, second_ref, cosine_ref, sine_ref, ins, range(ranks), slabs
        )
        for c in range(2):
            for j in range(states):
                first = (c * states + j) * rows
                outs[n * pieces + j // share][c, j % share] = product[first : first + rows]


def phase_call(after, me, second, cosine, sine, slabs):
    ranks = len(slabs)
    kinds, rows, wide = slabs[0].shape
    states, _, width = cosine.shape
    block = rows // 2
    share = states // PIECES
    count = kinds * PIECES
    table = pl.BlockSpec((states, block, width), lambda i: (0, i, 0))
    return pl.pallas_call(
        functools.partial(phase_kernel, len(after), ranks),
        grid=(rows // block,),
        in_specs=[SMEM, pl.BlockSpec(second.shape, lambda i: (0, 0)), table, table]
        + [AFTER] * len(after)
        + [pl.BlockSpec((kinds, block, wide), lambda i: (0, i, 0))] * ranks,
        out_specs=[pl.BlockSpec((2, share, block, width), lambda i: (0, 0, i, 0))] * count,
        out_shape=[pltpu.HBM((2, share, rows, width), jnp.bfloat16)] * count,
        scratch_shapes=[pltpu.VMEM((ranks, block, wide), jnp.bfloat16)],
        compiler_params=params(),
        cost_estimate=cost(
            8 * kinds * states * rows * width * width, 8 * kinds * states * rows * width
        ),
        name="phase",
    )(me, second, cosine, sine, *after, *slabs)


def mix_kernel(
    chosen, order, me_ref, up_ref, down_ref, second_ref, cosine_ref, sine_ref, weight_ref, *refs
):
    ranks = len(order)
    ins, known, (out, slabs, fresh) = refs[:ranks], refs[ranks:-3], refs[-3:]
    blocks, states = up_ref.shape
    rows, width = weight_ref.shape
    share = known[0].shape[1]
    pieces = states // share
    group = out.shape[3]
    others = [k for k in range(-1, blocks + 1) if k not in chosen]
    for n in range(len(chosen)):
        product = phased_product(
            me_ref[0], n, second_ref, cosine_ref, sine_ref, ins, order, slabs
        )
        fresh[n] = product.reshape(2, states, rows, width)

    def kinetic(k, c, j, span):
        if k in chosen:
            value = fresh[chosen.index(k), c, j, span]
        else:
            value = known[others.index(k) * pieces + j // share][c, j % share, span]
        return value.astype(jnp.float32)

    for first in range(0, rows, ROWS):
        span = slice(first, first + ROWS)
        weight = weight_ref[span]
        for k in range(blocks):
            columns = [[None] * group for _ in range(2)]
            for j in range(states):
                up, down = up_ref[k, j], down_ref[k, j]
                mixed = [
                    up * kinetic(k + 1, c, j, span) + down * kinetic(k - 1, c, j, span)
                    for c in range(2)
                ]
                parts = (
                    kinetic(k, 0, j, span) + weight * mixed[1],
                    kinetic(k, 1, j, span) - weight * mixed[0],
                )
                for c in range(2):
                    for t in range(width // LANES):
                        columns[c][t * states + j] = parts[c][:, t * LANES : (t + 1) * LANES]
            for c in range(2):
                out[span, c, k] = jnp.stack(columns[c], 0).transpose(1, 0, 2).astype(jnp.bfloat16)


def mix_call(me, up, down, second, cosine, sine, weight, chosen, slabs, known):
    ranks = len(slabs)
    order = tuple(range(ranks))
    kinds, rows, wide = slabs[0].shape
    _, share, _, width = known[0].shape
    blocks, states = up.shape
    group = width // LANES * states
    block = rows // 4
    table = pl.BlockSpec((states, block, width), lambda i: (0, i, 0))
    return pl.pallas_call(
        functools.partial(mix_kernel, tuple(chosen), order),
        grid=(rows // block,),
        in_specs=[SMEM] * 3
        + [pl.BlockSpec(second.shape, lambda i: (0, 0)), table, table]
        + [pl.BlockSpec((block, width), lambda i: (i, 0))]
        + [pl.BlockSpec((kinds, block, wide), lambda i: (0, i, 0))] * ranks
        + [pl.BlockSpec((2, share, block, width), lambda i: (0, 0, i, 0))] * len(known),
        out_specs=pl.BlockSpec((block, 2, blocks, group, LANES), lambda i: (i, 0, 0, 0, 0)),
        out_shape=jax.ShapeDtypeStruct((rows, 2, blocks, group, LANES), jnp.bfloat16),
        scratch_shapes=[
            pltpu.VMEM((ranks, block, wide), jnp.bfloat16),
            pltpu.VMEM((kinds, 2, states, block, width), jnp.bfloat16),
        ],
        compiler_params=params(),
        cost_estimate=cost(
            8 * kinds * states * rows * width * width, 10 * blocks * states * rows * width
        ),
        name="mix",
    )(me, up, down, second, cosine, sine, weight, *in_place([slabs[s] for s in order] + known))


def exchanged(slabs, axis):
    count = lax.axis_size(axis)
    result = [slabs[0]] + [None] * (count - 1)
    for s in reversed(range(1, count)):
        result[s] = lax.ppermute(slabs[s], axis, [(i, i ^ s) for i in range(count)])
    return result


def neighbour(edge, axis, step):
    count = lax.axis_size(axis)
    pairs = [(i, i + step) for i in range(count) if 0 <= i + step < count]
    return lax.ppermute(edge, axis, pairs)


def per_device(packet, first_propagator, second_propagator, potential, coupling, radial_weight):
    rows, _, blocks, states, width = packet.shape
    ranks = lax.axis_size("rad")
    whole = first_propagator.shape[1]
    tiles = width // LANES
    piece = states * width // ranks
    me = lax.axis_index("rad").astype(jnp.int32).reshape(1)
    second = second_propagator.reshape(2 * width, width)
    first = first_propagator.reshape(2 * whole, whole).T
    view = packet.reshape(rows, 2, blocks, states, tiles, LANES).transpose(0, 1, 2, 4, 3, 5)
    view = view.reshape(rows, 2, blocks, tiles * states, LANES)
    edges = sorted({0, blocks - 1})
    chunks = [edges, [k for k in range(blocks) if k not in edges]]

    last = me
    lines = []
    for n, chosen in enumerate(chunks):
        limit = LIMIT if n else WHOLE
        half = right_call([last], me, second, view, chosen, ranks, states, piece, limit)
        last = half[0]
        lines.append(exchanged(half, "rad"))
    backs = []
    for line in lines:
        moved = left_call([last], me, first, line)
        last = moved[0]
        backs.append(exchanged(moved, "rad"))

    angles = potential.transpose(1, 0, 2)
    cosine, sine = jnp.cos(angles), jnp.sin(angles)
    edge = phase_call([last], me, second, cosine, sine, backs[0])
    low, high = edge[:PIECES], edge[-PIECES:]
    below = [neighbour(x, "hel", 1) for x in high]
    above = [neighbour(x, "hel", -1) for x in low]

    count = coupling.shape[0]
    helicities = jnp.arange(count, dtype=jnp.int32)
    couple_up = jnp.where(helicities[:, None] < count - 1, coupling, 0.0)
    couple_down = jnp.concatenate(
        [jnp.zeros((1, coupling.shape[1]), jnp.float32), coupling[:-1]], axis=0
    )
    start = lax.axis_index("hel") * blocks
    up = lax.dynamic_slice_in_dim(couple_up, start, blocks, 0)
    down = lax.dynamic_slice_in_dim(couple_down, start, blocks, 0)
    known = [*below, *low, *high, *above]
    out = mix_call(
        me, up, down, second, cosine, sine, radial_weight, chunks[1], backs[1], known
    )
    out = out.reshape(rows, 2, blocks, tiles, states, LANES).transpose(0, 1, 2, 4, 3, 5)
    return out.reshape(rows, 2, blocks, states, width)


def solution(mesh):
    return jax.shard_map(
        per_device,
        mesh=mesh,
        in_specs=(
            P("rad", None, "hel", None, None),
            P(),
            P(),
            P("rad", None, None),
            P(),
            P("rad", None),
        ),
        out_specs=P("rad", None, "hel", None, None),
        check_vma=False,
    )
```

```python
import functools

import jax
import jax.numpy as jnp
from jax import lax
from jax.experimental import pallas as pl
from jax.experimental.pallas import tpu as pltpu
from jax.sharding import PartitionSpec as P

LANES = 128
ROWS = 16
PIECES = 2
LIMIT = 18 * 1024 * 1024
WHOLE = 3 * LIMIT
SMEM = pl.BlockSpec(memory_space=pltpu.SMEM)
AFTER = pl.BlockSpec(memory_space=pl.ANY)


def params(limit=LIMIT):
    return pltpu.CompilerParams(vmem_limit_bytes=limit)


def in_place(arrays):
    return [pltpu.with_memory_space_constraint(x, pltpu.HBM) for x in arrays]


def cost(flops, moved):
    return pl.CostEstimate(flops=flops, bytes_accessed=moved, transcendentals=0)


def complex_rows(real, imag):
    return jnp.concatenate([real, -imag], 1), jnp.concatenate([imag, real], 1)


def near_slabs(me, near):
    return pl.ds(me & -near, near)


def slab_specs(near, ranks, kinds, block, wide):
    return [pl.BlockSpec((near, kinds, block, wide), lambda i: (0, 0, i, 0))] + [
        pl.BlockSpec((kinds, block, wide), lambda i: (0, i, 0))
    ] * (ranks - near)


def sources(me, near, parts, n):
    for low in range(near):
        yield (me & -near) + low, parts[0][low, n]
    for s, part in enumerate(parts[1:], near):
        yield me ^ s, part[n]


def right_kernel(after, near, ranks, states, me_ref, second_ref, *refs):
    refs = refs[after:]
    kinds = len(refs) - 2 - (ranks - near)
    packets, outs, slabs = refs[:kinds], refs[kinds:-1], refs[-1]
    me = me_ref[0]
    rows = packets[0].shape[0]
    group = packets[0].shape[2]
    tiles = group // states
    piece = slabs.shape[2] // 2
    cuts = tiles * LANES // piece
    for n, packet in enumerate(packets):
        turned = [
            packet[:, c].astype(jnp.float32).transpose(1, 0, 2).astype(jnp.bfloat16)
            for c in range(2)
        ]

        def part(c, j):
            return jnp.concatenate([turned[c][t * states + j] for t in range(tiles)], 1)

        pairs = [complex_rows(part(0, j), part(1, j)) for j in range(states)]
        left = jnp.concatenate([p[0] for p in pairs] + [p[1] for p in pairs], 0)
        product = jnp.dot(left, second_ref[...], preferred_element_type=jnp.float32)
        product = product.astype(jnp.bfloat16)
        for c in range(2):
            for j in range(states):
                first = (c * states + j) * rows
                for p in range(cuts):
                    slabs[j * cuts + p, :, c * piece : (c + 1) * piece] = product[
                        first : first + rows, p * piece : (p + 1) * piece
                    ]
        outs[0][:, n] = slabs[near_slabs(me, near)]
        for s, out in enumerate(outs[1:], near):
            out[n] = slabs[me ^ s]


def right_call(after, near, me, second, view, chosen, ranks, states, piece, limit):
    rows, _, _, group, _ = view.shape
    width = second.shape[1]
    block = rows // 2
    kinds = len(chosen)
    return pl.pallas_call(
        functools.partial(right_kernel, len(after), near, ranks, states),
        grid=(rows // block,),
        in_specs=[SMEM, pl.BlockSpec(second.shape, lambda i: (0, 0))]
        + [AFTER] * len(after)
        + [
            pl.BlockSpec((block, 2, None, group, LANES), lambda i, k=k: (i, 0, k, 0, 0))
            for k in chosen
        ],
        out_specs=slab_specs(near, ranks, kinds, block, 2 * piece),
        out_shape=[jax.ShapeDtypeStruct((near, kinds, rows, 2 * piece), jnp.bfloat16)]
        + [jax.ShapeDtypeStruct((kinds, rows, 2 * piece), jnp.bfloat16)] * (ranks - near),
        scratch_shapes=[
            pltpu.VMEM((ranks, block, 2 * piece), jnp.bfloat16),
        ],
        compiler_params=params(limit),
        cost_estimate=cost(
            8 * kinds * states * rows * width * width, 8 * kinds * states * rows * width
        ),
        name="right",
    )(me, second, *after, *([view] * kinds))


def left_kernel(after, near, ranks, me_ref, first_ref, *refs):
    refs = refs[after:]
    count = 1 + ranks - near
    ins, outs, lines, slabs = refs[:count], refs[count:-2], refs[-2], refs[-1]
    me = me_ref[0]
    _, _, rows, wide = ins[0].shape
    piece = wide // 2
    whole = ranks * rows
    for source, value in sources(me, near, ins, 0):
        first = pl.multiple_of(source * rows, rows)
        lines[pl.ds(first, rows), :] = value
        lines[pl.ds(first + whole, rows), :] = jnp.concatenate(
            [-value[:, piece:], value[:, :piece]], 1
        )
    product = jnp.dot(first_ref[...], lines[...], preferred_element_type=jnp.float32)
    slabs[...] = product.astype(jnp.bfloat16).reshape(ranks, rows, wide)
    outs[0][:, 0] = slabs[near_slabs(me, near)]
    for s, out in enumerate(outs[1:], near):
        out[0] = slabs[me ^ s]


def left_call(after, me, first, slabs):
    near, kinds, rows, wide = slabs[0].shape
    ranks = len(slabs) - 1 + near
    whole = ranks * rows
    specs = [pl.BlockSpec((near, 1, rows, wide), lambda i: (0, i, 0, 0))] + [
        pl.BlockSpec((1, rows, wide), lambda i: (i, 0, 0))
    ] * (ranks - near)
    return pl.pallas_call(
        functools.partial(left_kernel, len(after), near, ranks),
        grid=(kinds,),
        in_specs=[SMEM, pl.BlockSpec(first.shape, lambda i: (0, 0))]
        + [AFTER] * len(after)
        + specs,
        out_specs=specs,
        out_shape=[jax.ShapeDtypeStruct(x.shape, jnp.bfloat16) for x in slabs],
        scratch_shapes=[
            pltpu.VMEM((2 * whole, wide), jnp.bfloat16),
            pltpu.VMEM((ranks, rows, wide), jnp.bfloat16),
        ],
        compiler_params=params(),
        cost_estimate=cost(
            4 * kinds * whole * whole * wide, 4 * whole * whole + 4 * kinds * whole * wide
        ),
        name="left",
    )(me, first, *after, *slabs)


def phased_product(me, n, near, second_ref, cosine_ref, sine_ref, ins, slabs):
    states, _, width = cosine_ref.shape
    piece = slabs.shape[2] // 2
    cuts = width // piece
    for source, value in sources(me, near, ins, n):
        slabs[source] = value
    pairs = []
    for j in range(states):
        real, imag = (
            jnp.concatenate(
                [slabs[j * cuts + p, :, c * piece : (c + 1) * piece] for p in range(cuts)], 1
            ).astype(jnp.float32)
            for c in range(2)
        )
        cosine, sine = cosine_ref[j], sine_ref[j]
        pairs.append(
            complex_rows(
                (real * cosine + imag * sine).astype(jnp.bfloat16),
                (imag * cosine - real * sine).astype(jnp.bfloat16),
            )
        )
    left = jnp.concatenate([p[0] for p in pairs] + [p[1] for p in pairs], 0)
    product = jnp.dot(left, second_ref[...], preferred_element_type=jnp.float32)
    return product.astype(jnp.bfloat16)


def phase_kernel(after, near, ranks, me_ref, second_ref, cosine_ref, sine_ref, *refs):
    refs = refs[after:]
    count = 1 + ranks - near
    ins, outs, slabs = refs[:count], refs[count:-1], refs[-1]
    states, rows, _ = cosine_ref.shape
    share = outs[0].shape[1]
    pieces = states // share
    for n in range(len(outs) // pieces):
        product = phased_product(
            me_ref[0], n, near, second_ref, cosine_ref, sine_ref, ins, slabs
        )
        for c in range(2):
            for j in range(states):
                first = (c * states + j) * rows
                outs[n * pieces + j // share][c, j % share] = product[first : first + rows]


def phase_call(after, me, second, cosine, sine, slabs):
    near, kinds, rows, wide = slabs[0].shape
    ranks = len(slabs) - 1 + near
    states, _, width = cosine.shape
    block = rows // 2
    share = states // PIECES
    count = kinds * PIECES
    table = pl.BlockSpec((states, block, width), lambda i: (0, i, 0))
    return pl.pallas_call(
        functools.partial(phase_kernel, len(after), near, ranks),
        grid=(rows // block,),
        in_specs=[SMEM, pl.BlockSpec(second.shape, lambda i: (0, 0)), table, table]
        + [AFTER] * len(after)
        + slab_specs(near, ranks, kinds, block, wide),
        out_specs=[pl.BlockSpec((2, share, block, width), lambda i: (0, 0, i, 0))] * count,
        out_shape=[pltpu.HBM((2, share, rows, width), jnp.bfloat16)] * count,
        scratch_shapes=[pltpu.VMEM((ranks, block, wide), jnp.bfloat16)],
        compiler_params=params(),
        cost_estimate=cost(
            8 * kinds * states * rows * width * width, 8 * kinds * states * rows * width
        ),
        name="phase",
    )(me, second, cosine, sine, *after, *slabs)


def mix_kernel(
    chosen, near, ranks, me_ref, up_ref, down_ref, second_ref, cosine_ref, sine_ref, weight_ref, *refs
):
    count = 1 + ranks - near
    ins, known, (out, slabs, fresh) = refs[:count], refs[count:-3], refs[-3:]
    blocks, states = up_ref.shape
    rows, width = weight_ref.shape
    share = known[0].shape[1]
    pieces = states // share
    group = out.shape[3]
    others = [k for k in range(-1, blocks + 1) if k not in chosen]
    for n in range(len(chosen)):
        product = phased_product(
            me_ref[0], n, near, second_ref, cosine_ref, sine_ref, ins, slabs
        )
        fresh[n] = product.reshape(2, states, rows, width)

    def kinetic(k, c, j, span):
        if k in chosen:
            value = fresh[chosen.index(k), c, j, span]
        else:
            value = known[others.index(k) * pieces + j // share][c, j % share, span]
        return value.astype(jnp.float32)

    for first in range(0, rows, ROWS):
        span = slice(first, first + ROWS)
        weight = weight_ref[span]
        for k in range(blocks):
            columns = [[None] * group for _ in range(2)]
            for j in range(states):
                up, down = up_ref[k, j], down_ref[k, j]
                mixed = [
                    up * kinetic(k + 1, c, j, span) + down * kinetic(k - 1, c, j, span)
                    for c in range(2)
                ]
                parts = (
                    kinetic(k, 0, j, span) + weight * mixed[1],
                    kinetic(k, 1, j, span) - weight * mixed[0],
                )
                for c in range(2):
                    for t in range(width // LANES):
                        columns[c][t * states + j] = parts[c][:, t * LANES : (t + 1) * LANES]
            for c in range(2):
                out[span, c, k] = jnp.stack(columns[c], 0).transpose(1, 0, 2).astype(jnp.bfloat16)


def mix_call(me, up, down, second, cosine, sine, weight, chosen, slabs, known):
    near, kinds, rows, wide = slabs[0].shape
    ranks = len(slabs) - 1 + near
    _, share, _, width = known[0].shape
    blocks, states = up.shape
    group = width // LANES * states
    block = rows // 4
    table = pl.BlockSpec((states, block, width), lambda i: (0, i, 0))
    return pl.pallas_call(
        functools.partial(mix_kernel, tuple(chosen), near, ranks),
        grid=(rows // block,),
        in_specs=[SMEM] * 3
        + [pl.BlockSpec(second.shape, lambda i: (0, 0)), table, table]
        + [pl.BlockSpec((block, width), lambda i: (i, 0))]
        + slab_specs(near, ranks, kinds, block, wide)
        + [pl.BlockSpec((2, share, block, width), lambda i: (0, 0, i, 0))] * len(known),
        out_specs=pl.BlockSpec((block, 2, blocks, group, LANES), lambda i: (i, 0, 0, 0, 0)),
        out_shape=jax.ShapeDtypeStruct((rows, 2, blocks, group, LANES), jnp.bfloat16),
        scratch_shapes=[
            pltpu.VMEM((ranks, block, wide), jnp.bfloat16),
            pltpu.VMEM((kinds, 2, states, block, width), jnp.bfloat16),
        ],
        compiler_params=params(),
        cost_estimate=cost(
            8 * kinds * states * rows * width * width, 10 * blocks * states * rows * width
        ),
        name="mix",
    )(me, up, down, second, cosine, sine, weight, *in_place([*slabs, *known]))


def exchanged(slabs, axis):
    count = lax.axis_size(axis)
    near = slabs[0].shape[0]
    result = [slabs[0]]
    if near == count:
        result = [lax.all_to_all(slabs[0], axis, 0, 0, tiled=True)]
    elif near > 1:
        groups = [list(range(i, i + near)) for i in range(0, count, near)]
        result = [lax.all_to_all(slabs[0], axis, 0, 0, axis_index_groups=groups, tiled=True)]
    for s, slab in enumerate(slabs[1:], near):
        result.append(lax.ppermute(slab, axis, [(i, i ^ s) for i in range(count)]))
    return result


def neighbour(edge, axis, step):
    count = lax.axis_size(axis)
    pairs = [(i, i + step) for i in range(count) if 0 <= i + step < count]
    return lax.ppermute(edge, axis, pairs)


def per_device(packet, first_propagator, second_propagator, potential, coupling, radial_weight):
    rows, _, blocks, states, width = packet.shape
    ranks = lax.axis_size("rad")
    whole = first_propagator.shape[1]
    tiles = width // LANES
    piece = states * width // ranks
    me = lax.axis_index("rad").astype(jnp.int32).reshape(1)
    second = second_propagator.reshape(2 * width, width)
    first = first_propagator.reshape(2 * whole, whole).T
    view = packet.reshape(rows, 2, blocks, states, tiles, LANES).transpose(0, 1, 2, 4, 3, 5)
    view = view.reshape(rows, 2, blocks, tiles * states, LANES)
    edges = sorted({0, blocks - 1})
    chunks = [edges, [k for k in range(blocks) if k not in edges]]

    nears = (1, ranks // 2)
    last = me
    lines = []
    for n, chosen in enumerate(chunks):
        limit = LIMIT if n else WHOLE
        half = right_call([last], nears[n], me, second, view, chosen, ranks, states, piece, limit)
        last = half[0]
        lines.append(exchanged(half, "rad"))
    backs = []
    for line in lines:
        moved = left_call([last], me, first, line)
        last = moved[0]
        backs.append(exchanged(moved, "rad"))

    angles = potential.transpose(1, 0, 2)
    cosine, sine = jnp.cos(angles), jnp.sin(angles)
    edge = phase_call([last], me, second, cosine, sine, backs[0])
    low, high = edge[:PIECES], edge[-PIECES:]
    below = [neighbour(x, "hel", 1) for x in high]
    above = [neighbour(x, "hel", -1) for x in low]

    count = coupling.shape[0]
    helicities = jnp.arange(count, dtype=jnp.int32)
    couple_up = jnp.where(helicities[:, None] < count - 1, coupling, 0.0)
    couple_down = jnp.concatenate(
        [jnp.zeros((1, coupling.shape[1]), jnp.float32), coupling[:-1]], axis=0
    )
    start = lax.axis_index("hel") * blocks
    up = lax.dynamic_slice_in_dim(couple_up, start, blocks, 0)
    down = lax.dynamic_slice_in_dim(couple_down, start, blocks, 0)
    known = [*below, *low, *high, *above]
    out = mix_call(
        me, up, down, second, cosine, sine, radial_weight, chunks[1], backs[1], known
    )
    out = out.reshape(rows, 2, blocks, tiles, states, LANES).transpose(0, 1, 2, 4, 3, 5)
    return out.reshape(rows, 2, blocks, states, width)


def solution(mesh):
    return jax.shard_map(
        per_device,
        mesh=mesh,
        in_specs=(
            P("rad", None, "hel", None, None),
            P(),
            P(),
            P("rad", None, None),
            P(),
            P("rad", None),
        ),
        out_specs=P("rad", None, "hel", None, None),
        check_vma=False,
    )
```

```python
import functools

import jax
import jax.numpy as jnp
from jax import lax
from jax.experimental import pallas as pl
from jax.experimental.pallas import tpu as pltpu
from jax.sharding import PartitionSpec as P

LANES = 128
ROWS = 16
PIECES = 4
LIMIT = 18 * 1024 * 1024
WHOLE = 3 * LIMIT
SMEM = pl.BlockSpec(memory_space=pltpu.SMEM)
AFTER = pl.BlockSpec(memory_space=pl.ANY)


def params(limit=LIMIT):
    return pltpu.CompilerParams(vmem_limit_bytes=limit)


def in_place(arrays):
    return [pltpu.with_memory_space_constraint(x, pltpu.HBM) for x in arrays]


def cost(flops, moved):
    return pl.CostEstimate(flops=flops, bytes_accessed=moved, transcendentals=0)


def complex_rows(real, imag):
    return jnp.concatenate([real, -imag], 1), jnp.concatenate([imag, real], 1)


def right_kernel(after, ranks, states, me_ref, second_ref, *refs):
    refs = refs[after:]
    kinds = len(refs) - 1 - ranks
    packets, outs, slabs = refs[:kinds], refs[kinds:-1], refs[-1]
    me = me_ref[0]
    rows = packets[0].shape[0]
    group = packets[0].shape[2]
    tiles = group // states
    piece = slabs.shape[2] // 2
    cuts = tiles * LANES // piece
    for n, packet in enumerate(packets):
        turned = [
            packet[:, c].astype(jnp.float32).transpose(1, 0, 2).astype(jnp.bfloat16)
            for c in range(2)
        ]

        def part(c, j):
            return jnp.concatenate([turned[c][t * states + j] for t in range(tiles)], 1)

        pairs = [complex_rows(part(0, j), part(1, j)) for j in range(states)]
        left = jnp.concatenate([p[0] for p in pairs] + [p[1] for p in pairs], 0)
        product = jnp.dot(left, second_ref[...], preferred_element_type=jnp.float32)
        product = product.astype(jnp.bfloat16)
        for c in range(2):
            for j in range(states):
                first = (c * states + j) * rows
                for p in range(cuts):
                    slabs[j * cuts + p, :, c * piece : (c + 1) * piece] = product[
                        first : first + rows, p * piece : (p + 1) * piece
                    ]
        for s, out in enumerate(outs):
            out[n] = slabs[me ^ s]


def right_call(after, me, second, view, chosen, ranks, states, piece, limit):
    rows, _, _, group, _ = view.shape
    width = second.shape[1]
    block = rows // 2
    kinds = len(chosen)
    return pl.pallas_call(
        functools.partial(right_kernel, len(after), ranks, states),
        grid=(rows // block,),
        in_specs=[SMEM, pl.BlockSpec(second.shape, lambda i: (0, 0))]
        + [AFTER] * len(after)
        + [
            pl.BlockSpec((block, 2, None, group, LANES), lambda i, k=k: (i, 0, k, 0, 0))
            for k in chosen
        ],
        out_specs=[pl.BlockSpec((kinds, block, 2 * piece), lambda i: (0, i, 0))] * ranks,
        out_shape=[jax.ShapeDtypeStruct((kinds, rows, 2 * piece), jnp.bfloat16)] * ranks,
        scratch_shapes=[
            pltpu.VMEM((ranks, block, 2 * piece), jnp.bfloat16),
        ],
        compiler_params=params(limit),
        cost_estimate=cost(
            8 * kinds * states * rows * width * width, 8 * kinds * states * rows * width
        ),
        name="right",
    )(me, second, *after, *([view] * kinds))


def left_kernel(after, ranks, me_ref, first_ref, *refs):
    refs = refs[after:]
    ins, outs, lines, slabs = refs[:ranks], refs[ranks:-2], refs[-2], refs[-1]
    me = me_ref[0]
    rows, wide = ins[0].shape
    piece = wide // 2
    whole = ranks * rows
    for s, part in enumerate(ins):
        value = part[...]
        first = pl.multiple_of((me ^ s) * rows, rows)
        lines[pl.ds(first, rows), :] = value
        lines[pl.ds(first + whole, rows), :] = jnp.concatenate(
            [-value[:, piece:], value[:, :piece]], 1
        )
    product = jnp.dot(first_ref[...], lines[...], preferred_element_type=jnp.float32)
    slabs[...] = product.astype(jnp.bfloat16).reshape(ranks, rows, wide)
    for s, out in enumerate(outs):
        out[...] = slabs[me ^ s]


def left_call(after, me, first, slabs):
    ranks = len(slabs)
    kinds, rows, wide = slabs[0].shape
    whole = ranks * rows
    spec = pl.BlockSpec((None, rows, wide), lambda i: (i, 0, 0))
    return pl.pallas_call(
        functools.partial(left_kernel, len(after), ranks),
        grid=(kinds,),
        in_specs=[SMEM, pl.BlockSpec(first.shape, lambda i: (0, 0))]
        + [AFTER] * len(after)
        + [spec] * ranks,
        out_specs=[spec] * ranks,
        out_shape=[jax.ShapeDtypeStruct(slabs[0].shape, jnp.bfloat16)] * ranks,
        scratch_shapes=[
            pltpu.VMEM((2 * whole, wide), jnp.bfloat16),
            pltpu.VMEM((ranks, rows, wide), jnp.bfloat16),
        ],
        compiler_params=params(),
        cost_estimate=cost(
            4 * kinds * whole * whole * wide, 4 * whole * whole + 4 * kinds * whole * wide
        ),
        name="left",
    )(me, first, *after, *slabs)


def phased_product(me, n, second_ref, cosine_ref, sine_ref, ins, order, slabs):
    states, _, width = cosine_ref.shape
    piece = slabs.shape[2] // 2
    cuts = width // piece
    for s, part in zip(order, ins):
        slabs[me ^ s] = part[n]
    pairs = []
    for j in range(states):
        real, imag = (
            jnp.concatenate(
                [slabs[j * cuts + p, :, c * piece : (c + 1) * piece] for p in range(cuts)], 1
            ).astype(jnp.float32)
            for c in range(2)
        )
        cosine, sine = cosine_ref[j], sine_ref[j]
        pairs.append(
            complex_rows(
                (real * cosine + imag * sine).astype(jnp.bfloat16),
                (imag * cosine - real * sine).astype(jnp.bfloat16),
            )
        )
    left = jnp.concatenate([p[0] for p in pairs] + [p[1] for p in pairs], 0)
    product = jnp.dot(left, second_ref[...], preferred_element_type=jnp.float32)
    return product.astype(jnp.bfloat16)


def phase_kernel(after, ranks, me_ref, second_ref, cosine_ref, sine_ref, *refs):
    refs = refs[after:]
    ins, outs, slabs = refs[:ranks], refs[ranks:-1], refs[-1]
    states, rows, _ = cosine_ref.shape
    share = outs[0].shape[1]
    pieces = states // share
    for n in range(len(outs) // pieces):
        product = phased_product(
            me_ref[0], n, second_ref, cosine_ref, sine_ref, ins, range(ranks), slabs
        )
        for c in range(2):
            for j in range(states):
                first = (c * states + j) * rows
                outs[n * pieces + j // share][c, j % share] = product[first : first + rows]


def phase_call(after, me, second, cosine, sine, slabs):
    ranks = len(slabs)
    kinds, rows, wide = slabs[0].shape
    states, _, width = cosine.shape
    block = rows // 2
    share = states // PIECES
    count = kinds * PIECES
    table = pl.BlockSpec((states, block, width), lambda i: (0, i, 0))
    return pl.pallas_call(
        functools.partial(phase_kernel, len(after), ranks),
        grid=(rows // block,),
        in_specs=[SMEM, pl.BlockSpec(second.shape, lambda i: (0, 0)), table, table]
        + [AFTER] * len(after)
        + [pl.BlockSpec((kinds, block, wide), lambda i: (0, i, 0))] * ranks,
        out_specs=[pl.BlockSpec((2, share, block, width), lambda i: (0, 0, i, 0))] * count,
        out_shape=[pltpu.HBM((2, share, rows, width), jnp.bfloat16)] * count,
        scratch_shapes=[pltpu.VMEM((ranks, block, wide), jnp.bfloat16)],
        compiler_params=params(),
        cost_estimate=cost(
            8 * kinds * states * rows * width * width, 8 * kinds * states * rows * width
        ),
        name="phase",
    )(me, second, cosine, sine, *after, *slabs)


def coupled(kinetic, k, up_ref, down_ref, weight_ref, out):
    rows, width = weight_ref.shape
    states = up_ref.shape[1]
    group = out.shape[2]
    for first in range(0, rows, ROWS):
        span = slice(first, first + ROWS)
        weight = weight_ref[span]
        columns = [[None] * group for _ in range(2)]
        for j in range(states):
            up, down = up_ref[k, j], down_ref[k, j]
            here, above, below = (
                [kinetic(n, c, j, span).astype(jnp.float32) for c in range(2)]
                for n in (k, k + 1, k - 1)
            )
            mixed = [up * above[c] + down * below[c] for c in range(2)]
            parts = here[0] + weight * mixed[1], here[1] - weight * mixed[0]
            for c in range(2):
                for t in range(width // LANES):
                    columns[c][t * states + j] = parts[c][:, t * LANES : (t + 1) * LANES]
        for c in range(2):
            out[span, c] = jnp.stack(columns[c], 0).transpose(1, 0, 2).astype(jnp.bfloat16)


def inner_kernel(
    order, me_ref, up_ref, down_ref, second_ref, cosine_ref, sine_ref, weight_ref, *refs
):
    ranks = len(order)
    ins, known, (out, fresh, slabs) = refs[:ranks], refs[ranks:-3], refs[-3:]
    blocks, states = up_ref.shape
    kinds = blocks - 2
    rows, width = weight_ref.shape
    step = pl.program_id(1)

    @pl.when(step == 0)
    def _():
        for n in range(kinds):
            product = phased_product(
                me_ref[0], n, second_ref, cosine_ref, sine_ref, ins, order, slabs
            )
            fresh[n] = product.reshape(2, states, rows, width)

    def kinetic(k, c, j, span):
        if 0 < k < blocks - 1:
            return fresh[k - 1, c, j, span]
        pieces = len(known) // 2
        share = states // pieces
        return known[(k > 0) * pieces + j // share][c, j % share, span]

    for n in range(kinds):

        @pl.when(step == n)
        def _(n=n):
            coupled(kinetic, n + 1, up_ref, down_ref, weight_ref, out)


def inner_call(me, up, down, second, cosine, sine, weight, slabs, known):
    ranks = len(slabs)
    order = tuple(range(ranks))
    kinds, rows, wide = slabs[0].shape
    _, share, _, width = known[0].shape
    blocks, states = up.shape
    group = width // LANES * states
    block = rows // 4
    table = pl.BlockSpec((states, block, width), lambda i, n: (0, i, 0))
    return pl.pallas_call(
        functools.partial(inner_kernel, order),
        grid=(rows // block, kinds),
        in_specs=[SMEM] * 3
        + [pl.BlockSpec(second.shape, lambda i, n: (0, 0)), table, table]
        + [pl.BlockSpec((block, width), lambda i, n: (i, 0))]
        + [pl.BlockSpec((kinds, block, wide), lambda i, n: (0, i, 0))] * ranks
        + [pl.BlockSpec((2, share, block, width), lambda i, n: (0, 0, i, 0))] * len(known),
        out_specs=[
            pl.BlockSpec((block, 2, None, group, LANES), lambda i, n: (i, 0, n + 1, 0, 0)),
            pl.BlockSpec((kinds, 2, states, block, width), lambda i, n: (0, 0, 0, i, 0)),
        ],
        out_shape=[
            jax.ShapeDtypeStruct((rows, 2, blocks, group, LANES), jnp.bfloat16),
            pltpu.HBM((kinds, 2, states, rows, width), jnp.bfloat16),
        ],
        scratch_shapes=[pltpu.VMEM((ranks, block, wide), jnp.bfloat16)],
        compiler_params=params(),
        cost_estimate=cost(
            8 * kinds * states * rows * width * width, 10 * blocks * states * rows * width
        ),
        name="inner",
    )(me, up, down, second, cosine, sine, weight, *in_place([*slabs, *known]))


def edge_kernel(up_ref, down_ref, weight_ref, fresh_ref, *refs):
    known, out = refs[:-2], refs[-1]
    blocks, states = up_ref.shape
    pieces = len(known) // 4
    share = states // pieces
    others = (-1, 0, blocks - 1, blocks)

    def kinetic(k, c, j, span):
        if 0 < k < blocks - 1:
            return fresh_ref[0 if k == 1 else blocks - 3, c, j, span]
        return known[others.index(k) * pieces + j // share][c, j % share, span]

    for n, k in enumerate((0, blocks - 1)):

        @pl.when(pl.program_id(1) == n)
        def _(k=k):
            coupled(kinetic, k, up_ref, down_ref, weight_ref, out)


def edge_call(up, down, weight, fresh, known, inner):
    kinds, _, states, rows, width = fresh.shape
    share = known[0].shape[1]
    _, _, blocks, group, _ = inner.shape
    block = rows // 4
    return pl.pallas_call(
        edge_kernel,
        grid=(rows // block, 2),
        in_specs=[SMEM] * 2
        + [pl.BlockSpec((block, width), lambda i, n: (i, 0))]
        + [pl.BlockSpec((kinds, 2, states, block, width), lambda i, n: (0, 0, 0, i, 0))]
        + [pl.BlockSpec((2, share, block, width), lambda i, n: (0, 0, i, 0))] * len(known)
        + [AFTER],
        out_specs=pl.BlockSpec(
            (block, 2, None, group, LANES), lambda i, n: (i, 0, n * (blocks - 1), 0, 0)
        ),
        out_shape=jax.ShapeDtypeStruct(inner.shape, jnp.bfloat16),
        input_output_aliases={4 + len(known): 0},
        compiler_params=params(),
        cost_estimate=cost(
            20 * 2 * states * rows * width, 10 * blocks * states * rows * width
        ),
        name="edge",
    )(up, down, weight, *in_place([fresh, *known]), inner)


def exchanged(slabs, axis):
    count = lax.axis_size(axis)
    result = [slabs[0]] + [None] * (count - 1)
    for s in reversed(range(1, count)):
        result[s] = lax.ppermute(slabs[s], axis, [(i, i ^ s) for i in range(count)])
    return result


def neighbour(edge, axis, step):
    count = lax.axis_size(axis)
    pairs = [(i, i + step) for i in range(count) if 0 <= i + step < count]
    return lax.ppermute(edge, axis, pairs)


def per_device(packet, first_propagator, second_propagator, potential, coupling, radial_weight):
    rows, _, blocks, states, width = packet.shape
    ranks = lax.axis_size("rad")
    whole = first_propagator.shape[1]
    tiles = width // LANES
    piece = states * width // ranks
    me = lax.axis_index("rad").astype(jnp.int32).reshape(1)
    second = second_propagator.reshape(2 * width, width)
    first = first_propagator.reshape(2 * whole, whole).T
    view = packet.reshape(rows, 2, blocks, states, tiles, LANES).transpose(0, 1, 2, 4, 3, 5)
    view = view.reshape(rows, 2, blocks, tiles * states, LANES)
    edges = sorted({0, blocks - 1})
    chunks = [edges, [k for k in range(blocks) if k not in edges]]

    last = me
    lines = []
    for n, chosen in enumerate(chunks):
        limit = LIMIT if n else WHOLE
        half = right_call([last], me, second, view, chosen, ranks, states, piece, limit)
        last = half[0]
        lines.append(exchanged(half, "rad"))
    angles = potential.transpose(1, 0, 2)
    cosine, sine = jnp.cos(angles), jnp.sin(angles)
    backs = []
    for line in lines:
        moved = left_call([last, cosine], me, first, line)
        last = moved[0]
        backs.append(exchanged(moved, "rad"))

    edge = phase_call([last], me, second, cosine, sine, backs[0])
    low, high = edge[:PIECES], edge[-PIECES:]
    below = [neighbour(x, "hel", 1) for x in high]
    above = [neighbour(x, "hel", -1) for x in low]

    count = coupling.shape[0]
    helicities = jnp.arange(count, dtype=jnp.int32)
    couple_up = jnp.where(helicities[:, None] < count - 1, coupling, 0.0)
    couple_down = jnp.concatenate(
        [jnp.zeros((1, coupling.shape[1]), jnp.float32), coupling[:-1]], axis=0
    )
    start = lax.axis_index("hel") * blocks
    up = lax.dynamic_slice_in_dim(couple_up, start, blocks, 0)
    down = lax.dynamic_slice_in_dim(couple_down, start, blocks, 0)
    inner, fresh = inner_call(
        me, up, down, second, cosine, sine, radial_weight, backs[1], [*low, *high]
    )
    known = [*below, *low, *high, *above]
    out = edge_call(up, down, radial_weight, fresh, known, inner)
    out = out.reshape(rows, 2, blocks, tiles, states, LANES).transpose(0, 1, 2, 4, 3, 5)
    return out.reshape(rows, 2, blocks, states, width)


def solution(mesh):
    return jax.shard_map(
        per_device,
        mesh=mesh,
        in_specs=(
            P("rad", None, "hel", None, None),
            P(),
            P(),
            P("rad", None, None),
            P(),
            P("rad", None),
        ),
        out_specs=P("rad", None, "hel", None, None),
        check_vma=False,
    )
```

```python
import functools

import jax
import jax.numpy as jnp
from jax import lax
from jax.experimental import pallas as pl
from jax.experimental.pallas import tpu as pltpu
from jax.sharding import PartitionSpec as P

LANES = 128
ROWS = 16
PIECES = 4
LIMIT = 18 * 1024 * 1024
WHOLE = 3 * LIMIT
SMEM = pl.BlockSpec(memory_space=pltpu.SMEM)
AFTER = pl.BlockSpec(memory_space=pl.ANY)


def params(limit=LIMIT):
    return pltpu.CompilerParams(vmem_limit_bytes=limit)


def in_place(arrays):
    return [pltpu.with_memory_space_constraint(x, pltpu.HBM) for x in arrays]


def cost(flops, moved):
    return pl.CostEstimate(flops=flops, bytes_accessed=moved, transcendentals=0)


def complex_rows(real, imag):
    return jnp.concatenate([real, -imag], 1), jnp.concatenate([imag, real], 1)


def right_kernel(after, ranks, states, me_ref, second_ref, *refs):
    refs = refs[after:]
    kinds = len(refs) - 1 - ranks
    packets, outs, slabs = refs[:kinds], refs[kinds:-1], refs[-1]
    me = me_ref[0]
    rows = packets[0].shape[0]
    group = packets[0].shape[2]
    tiles = group // states
    piece = slabs.shape[2] // 2
    cuts = tiles * LANES // piece
    for n, packet in enumerate(packets):
        turned = [
            packet[:, c].astype(jnp.float32).transpose(1, 0, 2).astype(jnp.bfloat16)
            for c in range(2)
        ]

        def part(c, j):
            return jnp.concatenate([turned[c][t * states + j] for t in range(tiles)], 1)

        pairs = [complex_rows(part(0, j), part(1, j)) for j in range(states)]
        left = jnp.concatenate([p[0] for p in pairs] + [p[1] for p in pairs], 0)
        product = jnp.dot(left, second_ref[...], preferred_element_type=jnp.float32)
        product = product.astype(jnp.bfloat16)
        for c in range(2):
            for j in range(states):
                first = (c * states + j) * rows
                for p in range(cuts):
                    slabs[j * cuts + p, :, c * piece : (c + 1) * piece] = product[
                        first : first + rows, p * piece : (p + 1) * piece
                    ]
        for s, out in enumerate(outs):
            out[n] = slabs[me ^ s]


def right_call(after, me, second, view, chosen, ranks, states, piece, limit):
    rows, _, _, group, _ = view.shape
    width = second.shape[1]
    block = rows
    kinds = len(chosen)
    return pl.pallas_call(
        functools.partial(right_kernel, len(after), ranks, states),
        grid=(rows // block,),
        in_specs=[SMEM, pl.BlockSpec(second.shape, lambda i: (0, 0))]
        + [AFTER] * len(after)
        + [
            pl.BlockSpec((block, 2, None, group, LANES), lambda i, k=k: (i, 0, k, 0, 0))
            for k in chosen
        ],
        out_specs=[pl.BlockSpec((kinds, block, 2 * piece), lambda i: (0, i, 0))] * ranks,
        out_shape=[jax.ShapeDtypeStruct((kinds, rows, 2 * piece), jnp.bfloat16)] * ranks,
        scratch_shapes=[
            pltpu.VMEM((ranks, block, 2 * piece), jnp.bfloat16),
        ],
        compiler_params=params(limit),
        cost_estimate=cost(
            8 * kinds * states * rows * width * width, 8 * kinds * states * rows * width
        ),
        name="right",
    )(me, second, *after, *([view] * kinds))


def left_kernel(after, ranks, me_ref, first_ref, *refs):
    refs = refs[after:]
    ins, outs, lines, slabs = refs[:ranks], refs[ranks:-2], refs[-2], refs[-1]
    me = me_ref[0]
    rows, wide = ins[0].shape
    piece = wide // 2
    whole = ranks * rows
    for s, part in enumerate(ins):
        value = part[...]
        first = pl.multiple_of((me ^ s) * rows, rows)
        lines[pl.ds(first, rows), :] = value
        lines[pl.ds(first + whole, rows), :] = jnp.concatenate(
            [-value[:, piece:], value[:, :piece]], 1
        )
    product = jnp.dot(first_ref[...], lines[...], preferred_element_type=jnp.float32)
    slabs[...] = product.astype(jnp.bfloat16).reshape(ranks, rows, wide)
    for s, out in enumerate(outs):
        out[...] = slabs[me ^ s]


def left_call(after, me, first, slabs):
    ranks = len(slabs)
    kinds, rows, wide = slabs[0].shape
    whole = ranks * rows
    spec = pl.BlockSpec((None, rows, wide), lambda i: (i, 0, 0))
    return pl.pallas_call(
        functools.partial(left_kernel, len(after), ranks),
        grid=(kinds,),
        in_specs=[SMEM, pl.BlockSpec(first.shape, lambda i: (0, 0))]
        + [AFTER] * len(after)
        + [spec] * ranks,
        out_specs=[spec] * ranks,
        out_shape=[jax.ShapeDtypeStruct(slabs[0].shape, jnp.bfloat16)] * ranks,
        scratch_shapes=[
            pltpu.VMEM((2 * whole, wide), jnp.bfloat16),
            pltpu.VMEM((ranks, rows, wide), jnp.bfloat16),
        ],
        compiler_params=params(),
        cost_estimate=cost(
            4 * kinds * whole * whole * wide, 4 * whole * whole + 4 * kinds * whole * wide
        ),
        name="left",
    )(me, first, *after, *slabs)


def phased_product(me, n, second_ref, cosine_ref, sine_ref, ins, order, slabs):
    states, _, width = cosine_ref.shape
    piece = slabs.shape[2] // 2
    cuts = width // piece
    for s, part in zip(order, ins):
        slabs[me ^ s] = part[n]
    pairs = []
    for j in range(states):
        real, imag = (
            jnp.concatenate(
                [slabs[j * cuts + p, :, c * piece : (c + 1) * piece] for p in range(cuts)], 1
            ).astype(jnp.float32)
            for c in range(2)
        )
        cosine, sine = cosine_ref[j], sine_ref[j]
        pairs.append(
            complex_rows(
                (real * cosine + imag * sine).astype(jnp.bfloat16),
                (imag * cosine - real * sine).astype(jnp.bfloat16),
            )
        )
    left = jnp.concatenate([p[0] for p in pairs] + [p[1] for p in pairs], 0)
    product = jnp.dot(left, second_ref[...], preferred_element_type=jnp.float32)
    return product.astype(jnp.bfloat16)


def phase_kernel(after, ranks, me_ref, second_ref, cosine_ref, sine_ref, *refs):
    refs = refs[after:]
    ins, outs, whole, slabs = refs[:ranks], refs[ranks:-2], refs[-2], refs[-1]
    states, rows, width = cosine_ref.shape
    share = outs[0].shape[1]
    pieces = states // share
    for n in range(len(outs) // pieces):
        product = phased_product(
            me_ref[0], n, second_ref, cosine_ref, sine_ref, ins, range(ranks), slabs
        )
        for c in range(2):
            for j in range(states):
                first = (c * states + j) * rows
                outs[n * pieces + j // share][c, j % share] = product[first : first + rows]
        whole[n] = product.reshape(2, states, rows, width)


def phase_call(after, me, second, cosine, sine, slabs):
    ranks = len(slabs)
    kinds, rows, wide = slabs[0].shape
    states, _, width = cosine.shape
    block = rows // 2
    share = states // PIECES
    count = kinds * PIECES
    table = pl.BlockSpec((states, block, width), lambda i: (0, i, 0))
    return pl.pallas_call(
        functools.partial(phase_kernel, len(after), ranks),
        grid=(rows // block,),
        in_specs=[SMEM, pl.BlockSpec(second.shape, lambda i: (0, 0)), table, table]
        + [AFTER] * len(after)
        + [pl.BlockSpec((kinds, block, wide), lambda i: (0, i, 0))] * ranks,
        out_specs=[pl.BlockSpec((2, share, block, width), lambda i: (0, 0, i, 0))] * count
        + [pl.BlockSpec((kinds, 2, states, block, width), lambda i: (0, 0, 0, i, 0))],
        out_shape=[pltpu.HBM((2, share, rows, width), jnp.bfloat16)] * count
        + [pltpu.HBM((kinds, 2, states, rows, width), jnp.bfloat16)],
        scratch_shapes=[pltpu.VMEM((ranks, block, wide), jnp.bfloat16)],
        compiler_params=params(),
        cost_estimate=cost(
            8 * kinds * states * rows * width * width, 8 * kinds * states * rows * width
        ),
        name="phase",
    )(me, second, cosine, sine, *after, *slabs)


def mix_kernel(
    chosen, order, me_ref, up_ref, down_ref, second_ref, cosine_ref, sine_ref, weight_ref, *refs
):
    ranks = len(order)
    ins, edges, halo, (out, slabs, fresh) = (
        refs[:ranks],
        refs[ranks],
        refs[ranks + 1 : -3],
        refs[-3:],
    )
    blocks, states = up_ref.shape
    rows, width = weight_ref.shape
    share = halo[0].shape[1]
    pieces = states // share
    group = out.shape[3]
    others = [k for k in range(blocks) if k not in chosen]
    for n in range(len(chosen)):
        product = phased_product(
            me_ref[0], n, second_ref, cosine_ref, sine_ref, ins, order, slabs
        )
        fresh[n] = product.reshape(2, states, rows, width)

    def kinetic(k, c, j, span):
        if k in chosen:
            value = fresh[chosen.index(k), c, j, span]
        elif k in others:
            value = edges[others.index(k), c, j, span]
        else:
            value = halo[(k > 0) * pieces + j // share][c, j % share, span]
        return value.astype(jnp.float32)

    for first in range(0, rows, ROWS):
        span = slice(first, first + ROWS)
        weight = weight_ref[span]
        for k in range(blocks):
            columns = [[None] * group for _ in range(2)]
            for j in range(states):
                up, down = up_ref[k, j], down_ref[k, j]
                mixed = [
                    up * kinetic(k + 1, c, j, span) + down * kinetic(k - 1, c, j, span)
                    for c in range(2)
                ]
                parts = (
                    kinetic(k, 0, j, span) + weight * mixed[1],
                    kinetic(k, 1, j, span) - weight * mixed[0],
                )
                for c in range(2):
                    for t in range(width // LANES):
                        columns[c][t * states + j] = parts[c][:, t * LANES : (t + 1) * LANES]
            for c in range(2):
                out[span, c, k] = jnp.stack(columns[c], 0).transpose(1, 0, 2).astype(jnp.bfloat16)


def mix_call(me, up, down, second, cosine, sine, weight, chosen, slabs, edges, halo):
    ranks = len(slabs)
    order = tuple(range(ranks))
    kinds, rows, wide = slabs[0].shape
    _, share, _, width = halo[0].shape
    blocks, states = up.shape
    group = width // LANES * states
    block = rows // 2
    table = pl.BlockSpec((states, block, width), lambda i: (0, i, 0))
    return pl.pallas_call(
        functools.partial(mix_kernel, tuple(chosen), order),
        grid=(rows // block,),
        in_specs=[SMEM] * 3
        + [pl.BlockSpec(second.shape, lambda i: (0, 0)), table, table]
        + [pl.BlockSpec((block, width), lambda i: (i, 0))]
        + [pl.BlockSpec((kinds, block, wide), lambda i: (0, i, 0))] * ranks
        + [pl.BlockSpec((*edges.shape[:3], block, width), lambda i: (0, 0, 0, i, 0))]
        + [pl.BlockSpec((2, share, block, width), lambda i: (0, 0, i, 0))] * len(halo),
        out_specs=pl.BlockSpec((block, 2, blocks, group, LANES), lambda i: (i, 0, 0, 0, 0)),
        out_shape=jax.ShapeDtypeStruct((rows, 2, blocks, group, LANES), jnp.bfloat16),
        scratch_shapes=[
            pltpu.VMEM((ranks, block, wide), jnp.bfloat16),
            pltpu.VMEM((kinds, 2, states, block, width), jnp.bfloat16),
        ],
        compiler_params=params(LIMIT + LIMIT // 2),
        cost_estimate=cost(
            8 * kinds * states * rows * width * width, 10 * blocks * states * rows * width
        ),
        name="mix",
    )(me, up, down, second, cosine, sine, weight, *in_place([slabs[s] for s in order] + [edges, *halo]))


def exchanged(slabs, axis):
    count = lax.axis_size(axis)
    result = [slabs[0]] + [None] * (count - 1)
    for s in reversed(range(1, count)):
        result[s] = lax.ppermute(slabs[s], axis, [(i, i ^ s) for i in range(count)])
    return result


def neighbour(edge, axis, step):
    count = lax.axis_size(axis)
    pairs = [(i, i + step) for i in range(count) if 0 <= i + step < count]
    return lax.ppermute(edge, axis, pairs)


def per_device(packet, first_propagator, second_propagator, potential, coupling, radial_weight):
    rows, _, blocks, states, width = packet.shape
    ranks = lax.axis_size("rad")
    whole = first_propagator.shape[1]
    tiles = width // LANES
    piece = states * width // ranks
    me = lax.axis_index("rad").astype(jnp.int32).reshape(1)
    second = second_propagator.reshape(2 * width, width)
    first = first_propagator.reshape(2 * whole, whole).T
    view = packet.reshape(rows, 2, blocks, states, tiles, LANES).transpose(0, 1, 2, 4, 3, 5)
    view = view.reshape(rows, 2, blocks, tiles * states, LANES)
    edges = sorted({0, blocks - 1})
    chunks = [edges, [k for k in range(blocks) if k not in edges]]

    last = me
    lines = []
    for n, chosen in enumerate(chunks):
        limit = LIMIT if n else WHOLE
        half = right_call([last], me, second, view, chosen, ranks, states, piece, limit)
        last = half[0]
        lines.append(exchanged(half, "rad"))
    backs = []
    for line in lines:
        moved = left_call([last], me, first, line)
        last = moved[0]
        backs.append(exchanged(moved, "rad"))

    angles = potential.transpose(1, 0, 2)
    cosine, sine = jnp.cos(angles), jnp.sin(angles)
    edge = phase_call([last], me, second, cosine, sine, backs[0])
    low, high, edges_here = edge[:PIECES], edge[-PIECES - 1 : -1], edge[-1]
    below = [neighbour(x, "hel", 1) for x in high]
    above = [neighbour(x, "hel", -1) for x in low]

    count = coupling.shape[0]
    helicities = jnp.arange(count, dtype=jnp.int32)
    couple_up = jnp.where(helicities[:, None] < count - 1, coupling, 0.0)
    couple_down = jnp.concatenate(
        [jnp.zeros((1, coupling.shape[1]), jnp.float32), coupling[:-1]], axis=0
    )
    start = lax.axis_index("hel") * blocks
    up = lax.dynamic_slice_in_dim(couple_up, start, blocks, 0)
    down = lax.dynamic_slice_in_dim(couple_down, start, blocks, 0)
    halo = [*below, *above]
    out = mix_call(
        me, up, down, second, cosine, sine, radial_weight, chunks[1], backs[1], edges_here, halo
    )
    out = out.reshape(rows, 2, blocks, tiles, states, LANES).transpose(0, 1, 2, 4, 3, 5)
    return out.reshape(rows, 2, blocks, states, width)


def solution(mesh):
    return jax.shard_map(
        per_device,
        mesh=mesh,
        in_specs=(
            P("rad", None, "hel", None, None),
            P(),
            P(),
            P("rad", None, None),
            P(),
            P("rad", None),
        ),
        out_specs=P("rad", None, "hel", None, None),
        check_vma=False,
    )
```

```python
import functools

import jax
import jax.numpy as jnp
from jax import lax
from jax.experimental import pallas as pl
from jax.experimental.pallas import tpu as pltpu
from jax.sharding import PartitionSpec as P

LANES = 128
ROWS = 16
PIECES = 4
LIMIT = 18 * 1024 * 1024
WHOLE = 3 * LIMIT
SMEM = pl.BlockSpec(memory_space=pltpu.SMEM)
AFTER = pl.BlockSpec(memory_space=pl.ANY)


def params(limit=LIMIT):
    return pltpu.CompilerParams(vmem_limit_bytes=limit)


def in_place(arrays):
    return [pltpu.with_memory_space_constraint(x, pltpu.HBM) for x in arrays]


def cost(flops, moved):
    return pl.CostEstimate(flops=flops, bytes_accessed=moved, transcendentals=0)


def complex_rows(real, imag):
    return jnp.concatenate([real, -imag], 1), jnp.concatenate([imag, real], 1)


def right_kernel(after, chosen, states, me_ref, second_ref, *refs):
    refs = refs[after:]
    packet, outs, slabs = refs[0], refs[1:-1], refs[-1]
    me = me_ref[0]
    rows, _, _, group, _ = packet.shape
    tiles = group // states
    piece = slabs.shape[2] // 2
    cuts = tiles * LANES // piece
    for n, k in enumerate(chosen):
        turned = [
            packet[:, c, k].astype(jnp.float32).transpose(1, 0, 2).astype(jnp.bfloat16)
            for c in range(2)
        ]

        def part(c, j):
            return jnp.concatenate([turned[c][t * states + j] for t in range(tiles)], 1)

        pairs = [complex_rows(part(0, j), part(1, j)) for j in range(states)]
        left = jnp.concatenate([p[0] for p in pairs] + [p[1] for p in pairs], 0)
        product = jnp.dot(left, second_ref[...], preferred_element_type=jnp.float32)
        product = product.astype(jnp.bfloat16)
        for c in range(2):
            for j in range(states):
                first = (c * states + j) * rows
                for p in range(cuts):
                    slabs[j * cuts + p, :, c * piece : (c + 1) * piece] = product[
                        first : first + rows, p * piece : (p + 1) * piece
                    ]
        for s, out in enumerate(outs):
            out[n] = slabs[me ^ s]


def right_call(after, me, second, view, chosen, ranks, states, piece, limit):
    rows, _, blocks, group, _ = view.shape
    width = second.shape[1]
    block = rows // 2
    kinds = len(chosen)
    return pl.pallas_call(
        functools.partial(right_kernel, len(after), tuple(chosen), states),
        grid=(rows // block,),
        in_specs=[SMEM, pl.BlockSpec(second.shape, lambda i: (0, 0))]
        + [AFTER] * len(after)
        + [pl.BlockSpec((block, 2, blocks, group, LANES), lambda i: (i, 0, 0, 0, 0))],
        out_specs=[pl.BlockSpec((kinds, block, 2 * piece), lambda i: (0, i, 0))] * ranks,
        out_shape=[jax.ShapeDtypeStruct((kinds, rows, 2 * piece), jnp.bfloat16)] * ranks,
        scratch_shapes=[
            pltpu.VMEM((ranks, block, 2 * piece), jnp.bfloat16),
        ],
        compiler_params=params(limit),
        cost_estimate=cost(
            8 * kinds * states * rows * width * width, 8 * kinds * states * rows * width
        ),
        name="right",
    )(me, second, *after, view)


def left_kernel(after, ranks, me_ref, first_ref, *refs):
    refs = refs[after:]
    ins, outs, lines, slabs = refs[:ranks], refs[ranks:-2], refs[-2], refs[-1]
    me = me_ref[0]
    rows, wide = ins[0].shape
    piece = wide // 2
    whole = ranks * rows
    for s, part in enumerate(ins):
        value = part[...]
        first = pl.multiple_of((me ^ s) * rows, rows)
        lines[pl.ds(first, rows), :] = value
        lines[pl.ds(first + whole, rows), :] = jnp.concatenate(
            [-value[:, piece:], value[:, :piece]], 1
        )
    product = jnp.dot(first_ref[...], lines[...], preferred_element_type=jnp.float32)
    slabs[...] = product.astype(jnp.bfloat16).reshape(ranks, rows, wide)
    for s, out in enumerate(outs):
        out[...] = slabs[me ^ s]


def left_call(after, me, first, slabs):
    ranks = len(slabs)
    kinds, rows, wide = slabs[0].shape
    whole = ranks * rows
    spec = pl.BlockSpec((None, rows, wide), lambda i: (i, 0, 0))
    return pl.pallas_call(
        functools.partial(left_kernel, len(after), ranks),
        grid=(kinds,),
        in_specs=[SMEM, pl.BlockSpec(first.shape, lambda i: (0, 0))]
        + [AFTER] * len(after)
        + [spec] * ranks,
        out_specs=[spec] * ranks,
        out_shape=[jax.ShapeDtypeStruct(slabs[0].shape, jnp.bfloat16)] * ranks,
        scratch_shapes=[
            pltpu.VMEM((2 * whole, wide), jnp.bfloat16),
            pltpu.VMEM((ranks, rows, wide), jnp.bfloat16),
        ],
        compiler_params=params(),
        cost_estimate=cost(
            4 * kinds * whole * whole * wide, 4 * whole * whole + 4 * kinds * whole * wide
        ),
        name="left",
    )(me, first, *after, *slabs)


def phased_product(me, n, second_ref, cosine_ref, sine_ref, ins, order, slabs):
    states, _, width = cosine_ref.shape
    piece = slabs.shape[2] // 2
    cuts = width // piece
    for s, part in zip(order, ins):
        slabs[me ^ s] = part[n]
    pairs = []
    for j in range(states):
        real, imag = (
            jnp.concatenate(
                [slabs[j * cuts + p, :, c * piece : (c + 1) * piece] for p in range(cuts)], 1
            ).astype(jnp.float32)
            for c in range(2)
        )
        cosine, sine = cosine_ref[j], sine_ref[j]
        pairs.append(
            complex_rows(
                (real * cosine + imag * sine).astype(jnp.bfloat16),
                (imag * cosine - real * sine).astype(jnp.bfloat16),
            )
        )
    left = jnp.concatenate([p[0] for p in pairs] + [p[1] for p in pairs], 0)
    product = jnp.dot(left, second_ref[...], preferred_element_type=jnp.float32)
    return product.astype(jnp.bfloat16)


def phase_kernel(after, ranks, me_ref, second_ref, cosine_ref, sine_ref, *refs):
    refs = refs[after:]
    ins, outs, whole, slabs = refs[:ranks], refs[ranks:-2], refs[-2], refs[-1]
    states, rows, width = cosine_ref.shape
    share = outs[0].shape[1]
    pieces = states // share
    for n in range(whole.shape[0]):
        product = phased_product(
            me_ref[0], n, second_ref, cosine_ref, sine_ref, ins, range(ranks), slabs
        )
        whole[n] = product.reshape(2, states, rows, width)
    for n, out in enumerate(outs):
        end = me_ref[1] if n < pieces else 1 - me_ref[1]
        first = n % pieces * share
        out[...] = whole[end, :, first : first + share]


def phase_call(after, me, second, cosine, sine, slabs):
    ranks = len(slabs)
    kinds, rows, wide = slabs[0].shape
    states, _, width = cosine.shape
    block = rows // 2
    share = states // PIECES
    count = kinds * PIECES
    table = pl.BlockSpec((states, block, width), lambda i: (0, i, 0))
    return pl.pallas_call(
        functools.partial(phase_kernel, len(after), ranks),
        grid=(rows // block,),
        in_specs=[SMEM, pl.BlockSpec(second.shape, lambda i: (0, 0)), table, table]
        + [AFTER] * len(after)
        + [pl.BlockSpec((kinds, block, wide), lambda i: (0, i, 0))] * ranks,
        out_specs=[pl.BlockSpec((2, share, block, width), lambda i: (0, 0, i, 0))] * count
        + [pl.BlockSpec((kinds, 2, states, block, width), lambda i: (0, 0, 0, i, 0))],
        out_shape=[pltpu.HBM((2, share, rows, width), jnp.bfloat16)] * count
        + [pltpu.HBM((kinds, 2, states, rows, width), jnp.bfloat16)],
        scratch_shapes=[pltpu.VMEM((ranks, block, wide), jnp.bfloat16)],
        compiler_params=params(),
        cost_estimate=cost(
            8 * kinds * states * rows * width * width, 8 * kinds * states * rows * width
        ),
        name="phase",
    )(me, second, cosine, sine, *after, *slabs)


def mix_kernel(
    chosen, order, me_ref, up_ref, down_ref, second_ref, cosine_ref, sine_ref, weight_ref, *refs
):
    ranks = len(order)
    ins, edges, pairs, (out, slabs, fresh, halo) = (
        refs[:ranks],
        refs[ranks],
        refs[ranks + 1 : -4],
        refs[-4:],
    )
    blocks, states = up_ref.shape
    rows, width = weight_ref.shape
    share = pairs[0].shape[1]
    pieces = states // share
    group = out.shape[3]
    for n, part in enumerate(pairs):
        end = me_ref[1] if n < pieces else 1 - me_ref[1]
        first = n % pieces * share
        halo[end, :, first : first + share] = part[...]
    others = [k for k in range(blocks) if k not in chosen]
    for n in range(len(chosen)):
        product = phased_product(
            me_ref[0], n, second_ref, cosine_ref, sine_ref, ins, order, slabs
        )
        fresh[n] = product.reshape(2, states, rows, width)

    def kinetic(k, c, j, span):
        if k in chosen:
            value = fresh[chosen.index(k), c, j, span]
        elif k in others:
            value = edges[others.index(k), c, j, span]
        else:
            value = halo[int(k > 0), c, j, span]
        return value.astype(jnp.float32)

    for first in range(0, rows, ROWS):
        span = slice(first, first + ROWS)
        weight = weight_ref[span]
        for k in range(blocks):
            columns = [[None] * group for _ in range(2)]
            for j in range(states):
                up, down = up_ref[k, j], down_ref[k, j]
                mixed = [
                    up * kinetic(k + 1, c, j, span) + down * kinetic(k - 1, c, j, span)
                    for c in range(2)
                ]
                parts = (
                    kinetic(k, 0, j, span) + weight * mixed[1],
                    kinetic(k, 1, j, span) - weight * mixed[0],
                )
                for c in range(2):
                    for t in range(width // LANES):
                        columns[c][t * states + j] = parts[c][:, t * LANES : (t + 1) * LANES]
            for c in range(2):
                out[span, c, k] = jnp.stack(columns[c], 0).transpose(1, 0, 2).astype(jnp.bfloat16)


def mix_call(me, up, down, second, cosine, sine, weight, chosen, slabs, edges, halo):
    ranks = len(slabs)
    order = tuple(range(ranks))
    kinds, rows, wide = slabs[0].shape
    _, share, _, width = halo[0].shape
    blocks, states = up.shape
    group = width // LANES * states
    block = rows // 2
    table = pl.BlockSpec((states, block, width), lambda i: (0, i, 0))
    return pl.pallas_call(
        functools.partial(mix_kernel, tuple(chosen), order),
        grid=(rows // block,),
        in_specs=[SMEM] * 3
        + [pl.BlockSpec(second.shape, lambda i: (0, 0)), table, table]
        + [pl.BlockSpec((block, width), lambda i: (i, 0))]
        + [pl.BlockSpec((kinds, block, wide), lambda i: (0, i, 0))] * ranks
        + [pl.BlockSpec((*edges.shape[:3], block, width), lambda i: (0, 0, 0, i, 0))]
        + [pl.BlockSpec((2, share, block, width), lambda i: (0, 0, i, 0))] * len(halo),
        out_specs=pl.BlockSpec((block, 2, blocks, group, LANES), lambda i: (i, 0, 0, 0, 0)),
        out_shape=jax.ShapeDtypeStruct((rows, 2, blocks, group, LANES), jnp.bfloat16),
        scratch_shapes=[
            pltpu.VMEM((ranks, block, wide), jnp.bfloat16),
            pltpu.VMEM((kinds, 2, states, block, width), jnp.bfloat16),
            pltpu.VMEM((2, 2, states, block, width), jnp.bfloat16),
        ],
        compiler_params=params(LIMIT + LIMIT // 2),
        cost_estimate=cost(
            8 * kinds * states * rows * width * width, 10 * blocks * states * rows * width
        ),
        name="mix",
    )(me, up, down, second, cosine, sine, weight, *in_place([slabs[s] for s in order] + [edges, *halo]))


def exchanged(slabs, axis):
    count = lax.axis_size(axis)
    result = [slabs[0]] + [None] * (count - 1)
    for s in reversed(range(1, count)):
        result[s] = lax.ppermute(slabs[s], axis, [(i, i ^ s) for i in range(count)])
    return result


def paired(edge, axis, first):
    count = lax.axis_size(axis)
    pairs = [(i, i + 1) for i in range(first, count - 1, 2)]
    return lax.ppermute(edge, axis, pairs + [(j, i) for i, j in pairs])


def per_device(packet, first_propagator, second_propagator, potential, coupling, radial_weight):
    rows, _, blocks, states, width = packet.shape
    ranks = lax.axis_size("rad")
    whole = first_propagator.shape[1]
    tiles = width // LANES
    piece = states * width // ranks
    me = lax.axis_index("rad").astype(jnp.int32).reshape(1)
    place = jnp.stack([lax.axis_index("rad"), lax.axis_index("hel") % 2]).astype(jnp.int32)
    second = second_propagator.reshape(2 * width, width)
    first = first_propagator.reshape(2 * whole, whole).T
    view = packet.reshape(rows, 2, blocks, states, tiles, LANES).transpose(0, 1, 2, 4, 3, 5)
    view = view.reshape(rows, 2, blocks, tiles * states, LANES)
    edges = sorted({0, blocks - 1})
    chunks = [edges, [k for k in range(blocks) if k not in edges]]

    last = me
    lines = []
    for n, chosen in enumerate(chunks):
        limit = LIMIT if n else WHOLE
        half = right_call([last], me, second, view, chosen, ranks, states, piece, limit)
        last = half[0]
        lines.append(exchanged(half, "rad"))
    backs = []
    for line in lines:
        moved = left_call([last], me, first, line)
        last = moved[0]
        backs.append(exchanged(moved, "rad"))

    angles = potential.transpose(1, 0, 2)
    cosine, sine = jnp.cos(angles), jnp.sin(angles)
    edge = phase_call([last], place, second, cosine, sine, backs[0])
    halo = [paired(x, "hel", 1) for x in edge[:PIECES]]
    halo += [paired(x, "hel", 0) for x in edge[PIECES:-1]]

    count = coupling.shape[0]
    helicities = jnp.arange(count, dtype=jnp.int32)
    couple_up = jnp.where(helicities[:, None] < count - 1, coupling, 0.0)
    couple_down = jnp.concatenate(
        [jnp.zeros((1, coupling.shape[1]), jnp.float32), coupling[:-1]], axis=0
    )
    start = lax.axis_index("hel") * blocks
    up = lax.dynamic_slice_in_dim(couple_up, start, blocks, 0)
    down = lax.dynamic_slice_in_dim(couple_down, start, blocks, 0)
    out = mix_call(
        place, up, down, second, cosine, sine, radial_weight, chunks[1], backs[1], edge[-1], halo
    )
    out = out.reshape(rows, 2, blocks, tiles, states, LANES).transpose(0, 1, 2, 4, 3, 5)
    return out.reshape(rows, 2, blocks, states, width)


def solution(mesh):
    return jax.shard_map(
        per_device,
        mesh=mesh,
        in_specs=(
            P("rad", None, "hel", None, None),
            P(),
            P(),
            P("rad", None, None),
            P(),
            P("rad", None),
        ),
        out_specs=P("rad", None, "hel", None, None),
        check_vma=False,
    )
```

```python
import functools

import jax
import jax.numpy as jnp
from jax import lax
from jax.experimental import pallas as pl
from jax.experimental.pallas import tpu as pltpu
from jax.sharding import PartitionSpec as P

LANES = 128
ROWS = 16
PIECES = 4
LIMIT = 18 * 1024 * 1024
WHOLE = 3 * LIMIT
SMEM = pl.BlockSpec(memory_space=pltpu.SMEM)
AFTER = pl.BlockSpec(memory_space=pl.ANY)


def params(limit=LIMIT):
    return pltpu.CompilerParams(vmem_limit_bytes=limit)


def in_place(arrays):
    return [pltpu.with_memory_space_constraint(x, pltpu.HBM) for x in arrays]


def cost(flops, moved):
    return pl.CostEstimate(flops=flops, bytes_accessed=moved, transcendentals=0)


def complex_rows(real, imag):
    return jnp.concatenate([real, -imag], 1), jnp.concatenate([imag, real], 1)


def right_kernel(after, ranks, states, me_ref, second_ref, *refs):
    refs = refs[after:]
    kinds = len(refs) - 1 - ranks
    packets, outs, slabs = refs[:kinds], refs[kinds:-1], refs[-1]
    me = me_ref[0]
    rows = packets[0].shape[0]
    group = packets[0].shape[2]
    tiles = group // states
    piece = slabs.shape[2] // 2
    cuts = tiles * LANES // piece
    for n, packet in enumerate(packets):
        turned = [
            packet[:, c].astype(jnp.float32).transpose(1, 0, 2).astype(jnp.bfloat16)
            for c in range(2)
        ]

        def part(c, j):
            return jnp.concatenate([turned[c][t * states + j] for t in range(tiles)], 1)

        pairs = [complex_rows(part(0, j), part(1, j)) for j in range(states)]
        left = jnp.concatenate([p[0] for p in pairs] + [p[1] for p in pairs], 0)
        product = jnp.dot(left, second_ref[...], preferred_element_type=jnp.float32)
        product = product.astype(jnp.bfloat16)
        for c in range(2):
            for j in range(states):
                first = (c * states + j) * rows
                for p in range(cuts):
                    slabs[j * cuts + p, :, c * piece : (c + 1) * piece] = product[
                        first : first + rows, p * piece : (p + 1) * piece
                    ]
        for s, out in enumerate(outs):
            out[n] = slabs[me ^ s]


def right_call(after, me, second, view, chosen, ranks, states, piece, limit):
    rows, _, _, group, _ = view.shape
    width = second.shape[1]
    block = rows // 2
    kinds = len(chosen)
    return pl.pallas_call(
        functools.partial(right_kernel, len(after), ranks, states),
        grid=(rows // block,),
        in_specs=[SMEM, pl.BlockSpec(second.shape, lambda i: (0, 0))]
        + [AFTER] * len(after)
        + [
            pl.BlockSpec((block, 2, None, group, LANES), lambda i, k=k: (i, 0, k, 0, 0))
            for k in chosen
        ],
        out_specs=[pl.BlockSpec((kinds, block, 2 * piece), lambda i: (0, i, 0))] * ranks,
        out_shape=[jax.ShapeDtypeStruct((kinds, rows, 2 * piece), jnp.bfloat16)] * ranks,
        scratch_shapes=[
            pltpu.VMEM((ranks, block, 2 * piece), jnp.bfloat16),
        ],
        compiler_params=params(limit),
        cost_estimate=cost(
            8 * kinds * states * rows * width * width, 8 * kinds * states * rows * width
        ),
        name="right",
    )(me, second, *after, *([view] * kinds))


def left_kernel(after, order, me_ref, first_ref, *refs):
    refs = refs[after:]
    ranks = len(order)
    ins, outs, lines, slabs = refs[:ranks], refs[ranks:-2], refs[-2], refs[-1]
    me = me_ref[0]
    rows, wide = ins[0].shape
    piece = wide // 2
    whole = ranks * rows
    for s, part in zip(order, ins):
        value = part[...]
        first = pl.multiple_of((me ^ s) * rows, rows)
        lines[pl.ds(first, rows), :] = value
        lines[pl.ds(first + whole, rows), :] = jnp.concatenate(
            [-value[:, piece:], value[:, :piece]], 1
        )
    product = jnp.dot(first_ref[...], lines[...], preferred_element_type=jnp.float32)
    slabs[...] = product.astype(jnp.bfloat16).reshape(ranks, rows, wide)
    for s, out in enumerate(outs):
        out[...] = slabs[me ^ s]


def left_call(after, me, first, slabs, order):
    ranks = len(slabs)
    kinds, rows, wide = slabs[0].shape
    whole = ranks * rows
    spec = pl.BlockSpec((None, rows, wide), lambda i: (i, 0, 0))
    return pl.pallas_call(
        functools.partial(left_kernel, len(after), order),
        grid=(kinds,),
        in_specs=[SMEM, pl.BlockSpec(first.shape, lambda i: (0, 0))]
        + [AFTER] * len(after)
        + [spec] * ranks,
        out_specs=[spec] * ranks,
        out_shape=[jax.ShapeDtypeStruct(slabs[0].shape, jnp.bfloat16)] * ranks,
        scratch_shapes=[
            pltpu.VMEM((2 * whole, wide), jnp.bfloat16),
            pltpu.VMEM((ranks, rows, wide), jnp.bfloat16),
        ],
        compiler_params=params(),
        cost_estimate=cost(
            4 * kinds * whole * whole * wide, 4 * whole * whole + 4 * kinds * whole * wide
        ),
        name="left",
    )(me, first, *after, *[slabs[s] for s in order])


def phased_product(me, n, second_ref, cosine_ref, sine_ref, ins, order, slabs):
    states, _, width = cosine_ref.shape
    piece = slabs.shape[2] // 2
    cuts = width // piece
    for s, part in zip(order, ins):
        slabs[me ^ s] = part[n]
    pairs = []
    for j in range(states):
        real, imag = (
            jnp.concatenate(
                [slabs[j * cuts + p, :, c * piece : (c + 1) * piece] for p in range(cuts)], 1
            ).astype(jnp.float32)
            for c in range(2)
        )
        cosine, sine = cosine_ref[j], sine_ref[j]
        pairs.append(
            complex_rows(
                (real * cosine + imag * sine).astype(jnp.bfloat16),
                (imag * cosine - real * sine).astype(jnp.bfloat16),
            )
        )
    left = jnp.concatenate([p[0] for p in pairs] + [p[1] for p in pairs], 0)
    product = jnp.dot(left, second_ref[...], preferred_element_type=jnp.float32)
    return product.astype(jnp.bfloat16)


def phase_kernel(after, ranks, me_ref, second_ref, cosine_ref, sine_ref, *refs):
    refs = refs[after:]
    ins, outs, whole, slabs = refs[:ranks], refs[ranks:-2], refs[-2], refs[-1]
    states, rows, width = cosine_ref.shape
    share = outs[0].shape[1]
    pieces = states // share
    for n in range(whole.shape[0]):
        product = phased_product(
            me_ref[0], n, second_ref, cosine_ref, sine_ref, ins, range(ranks), slabs
        )
        whole[n] = product.reshape(2, states, rows, width)
    for n, out in enumerate(outs):
        end = me_ref[1] if n < pieces else 1 - me_ref[1]
        first = n % pieces * share
        out[...] = whole[end, :, first : first + share]


def phase_call(after, me, second, cosine, sine, slabs):
    ranks = len(slabs)
    kinds, rows, wide = slabs[0].shape
    states, _, width = cosine.shape
    block = rows // 2
    share = states // PIECES
    count = kinds * PIECES
    table = pl.BlockSpec((states, block, width), lambda i: (0, i, 0))
    return pl.pallas_call(
        functools.partial(phase_kernel, len(after), ranks),
        grid=(rows // block,),
        in_specs=[SMEM, pl.BlockSpec(second.shape, lambda i: (0, 0)), table, table]
        + [AFTER] * len(after)
        + [pl.BlockSpec((kinds, block, wide), lambda i: (0, i, 0))] * ranks,
        out_specs=[pl.BlockSpec((2, share, block, width), lambda i: (0, 0, i, 0))] * count
        + [pl.BlockSpec((kinds, 2, states, block, width), lambda i: (0, 0, 0, i, 0))],
        out_shape=[pltpu.HBM((2, share, rows, width), jnp.bfloat16)] * count
        + [pltpu.HBM((kinds, 2, states, rows, width), jnp.bfloat16)],
        scratch_shapes=[pltpu.VMEM((ranks, block, wide), jnp.bfloat16)],
        compiler_params=params(),
        cost_estimate=cost(
            8 * kinds * states * rows * width * width, 8 * kinds * states * rows * width
        ),
        name="phase",
    )(me, second, cosine, sine, *after, *slabs)


def mix_kernel(
    chosen, order, me_ref, up_ref, down_ref, second_ref, cosine_ref, sine_ref, weight_ref, *refs
):
    ranks = len(order)
    ins, edges, pairs, (out, slabs, fresh, halo) = (
        refs[:ranks],
        refs[ranks],
        refs[ranks + 1 : -4],
        refs[-4:],
    )
    blocks, states = up_ref.shape
    rows, width = weight_ref.shape
    share = pairs[0].shape[1]
    pieces = states // share
    group = out.shape[3]
    for n, part in enumerate(pairs):
        end = me_ref[1] if n < pieces else 1 - me_ref[1]
        first = n % pieces * share
        halo[end, :, first : first + share] = part[...]
    others = [k for k in range(blocks) if k not in chosen]
    for n in range(len(chosen)):
        product = phased_product(
            me_ref[0], n, second_ref, cosine_ref, sine_ref, ins, order, slabs
        )
        fresh[n] = product.reshape(2, states, rows, width)

    def kinetic(k, c, j, span):
        if k in chosen:
            value = fresh[chosen.index(k), c, j, span]
        elif k in others:
            value = edges[others.index(k), c, j, span]
        else:
            value = halo[int(k > 0), c, j, span]
        return value.astype(jnp.float32)

    for first in range(0, rows, ROWS):
        span = slice(first, first + ROWS)
        weight = weight_ref[span]
        for k in range(blocks):
            columns = [[None] * group for _ in range(2)]
            for j in range(states):
                up, down = up_ref[k, j], down_ref[k, j]
                mixed = [
                    up * kinetic(k + 1, c, j, span) + down * kinetic(k - 1, c, j, span)
                    for c in range(2)
                ]
                parts = (
                    kinetic(k, 0, j, span) + weight * mixed[1],
                    kinetic(k, 1, j, span) - weight * mixed[0],
                )
                for c in range(2):
                    for t in range(width // LANES):
                        columns[c][t * states + j] = parts[c][:, t * LANES : (t + 1) * LANES]
            for c in range(2):
                out[span, c, k] = jnp.stack(columns[c], 0).transpose(1, 0, 2).astype(jnp.bfloat16)


def mix_call(me, up, down, second, cosine, sine, weight, chosen, slabs, edges, halo):
    ranks = len(slabs)
    order = tuple(range(ranks))
    kinds, rows, wide = slabs[0].shape
    _, share, _, width = halo[0].shape
    blocks, states = up.shape
    group = width // LANES * states
    block = rows // 2
    table = pl.BlockSpec((states, block, width), lambda i: (0, i, 0))
    return pl.pallas_call(
        functools.partial(mix_kernel, tuple(chosen), order),
        grid=(rows // block,),
        in_specs=[SMEM] * 3
        + [pl.BlockSpec(second.shape, lambda i: (0, 0)), table, table]
        + [pl.BlockSpec((block, width), lambda i: (i, 0))]
        + [pl.BlockSpec((kinds, block, wide), lambda i: (0, i, 0))] * ranks
        + [pl.BlockSpec((*edges.shape[:3], block, width), lambda i: (0, 0, 0, i, 0))]
        + [pl.BlockSpec((2, share, block, width), lambda i: (0, 0, i, 0))] * len(halo),
        out_specs=pl.BlockSpec((block, 2, blocks, group, LANES), lambda i: (i, 0, 0, 0, 0)),
        out_shape=jax.ShapeDtypeStruct((rows, 2, blocks, group, LANES), jnp.bfloat16),
        scratch_shapes=[
            pltpu.VMEM((ranks, block, wide), jnp.bfloat16),
            pltpu.VMEM((kinds, 2, states, block, width), jnp.bfloat16),
            pltpu.VMEM((2, 2, states, block, width), jnp.bfloat16),
        ],
        compiler_params=params(LIMIT + LIMIT // 2),
        cost_estimate=cost(
            8 * kinds * states * rows * width * width, 10 * blocks * states * rows * width
        ),
        name="mix",
    )(me, up, down, second, cosine, sine, weight, *in_place([slabs[s] for s in order] + [edges, *halo]))


def exchanged(slabs, axis):
    count = lax.axis_size(axis)
    result = [slabs[0]] + [None] * (count - 1)
    for s in reversed(range(1, count)):
        result[s] = lax.ppermute(slabs[s], axis, [(i, i ^ s) for i in range(count)])
    return result


def paired(edge, axis, first):
    count = lax.axis_size(axis)
    pairs = [(i, i + 1) for i in range(first, count - 1, 2)]
    return lax.ppermute(edge, axis, pairs + [(j, i) for i, j in pairs])


def per_device(packet, first_propagator, second_propagator, potential, coupling, radial_weight):
    rows, _, blocks, states, width = packet.shape
    ranks = lax.axis_size("rad")
    whole = first_propagator.shape[1]
    tiles = width // LANES
    piece = states * width // ranks
    me = lax.axis_index("rad").astype(jnp.int32).reshape(1)
    place = jnp.stack([lax.axis_index("rad"), lax.axis_index("hel") % 2]).astype(jnp.int32)
    second = second_propagator.reshape(2 * width, width)
    first = first_propagator.reshape(2 * whole, whole).T
    view = packet.reshape(rows, 2, blocks, states, tiles, LANES).transpose(0, 1, 2, 4, 3, 5)
    view = view.reshape(rows, 2, blocks, tiles * states, LANES)
    edges = sorted({0, blocks - 1})
    chunks = [edges, [k for k in range(blocks) if k not in edges]]

    last = me
    lines = []
    for n, chosen in enumerate(chunks):
        limit = LIMIT if n else WHOLE
        half = right_call([last], me, second, view, chosen, ranks, states, piece, limit)
        last = half[0]
        lines.append(exchanged(half, "rad"))
    backs = []
    far_first = (0, *range(ranks // 2, ranks), *range(1, ranks // 2))
    orders = (far_first, tuple(range(ranks)))
    for line, order in zip(lines, orders):
        moved = left_call([last], me, first, line, order)
        last = moved[0]
        backs.append(exchanged(moved, "rad"))

    angles = potential.transpose(1, 0, 2)
    cosine, sine = jnp.cos(angles), jnp.sin(angles)
    edge = phase_call([last], place, second, cosine, sine, backs[0])
    halo = [paired(x, "hel", 1) for x in edge[:PIECES]]
    halo += [paired(x, "hel", 0) for x in edge[PIECES:-1]]

    count = coupling.shape[0]
    helicities = jnp.arange(count, dtype=jnp.int32)
    couple_up = jnp.where(helicities[:, None] < count - 1, coupling, 0.0)
    couple_down = jnp.concatenate(
        [jnp.zeros((1, coupling.shape[1]), jnp.float32), coupling[:-1]], axis=0
    )
    start = lax.axis_index("hel") * blocks
    up = lax.dynamic_slice_in_dim(couple_up, start, blocks, 0)
    down = lax.dynamic_slice_in_dim(couple_down, start, blocks, 0)
    out = mix_call(
        place, up, down, second, cosine, sine, radial_weight, chunks[1], backs[1], edge[-1], halo
    )
    out = out.reshape(rows, 2, blocks, tiles, states, LANES).transpose(0, 1, 2, 4, 3, 5)
    return out.reshape(rows, 2, blocks, states, width)


def solution(mesh):
    return jax.shard_map(
        per_device,
        mesh=mesh,
        in_specs=(
            P("rad", None, "hel", None, None),
            P(),
            P(),
            P("rad", None, None),
            P(),
            P("rad", None),
        ),
        out_specs=P("rad", None, "hel", None, None),
        check_vma=False,
    )
```

```python
import functools

import jax
import jax.numpy as jnp
from jax import lax
from jax.experimental import pallas as pl
from jax.experimental.pallas import tpu as pltpu
from jax.sharding import PartitionSpec as P

LANES = 128
ROWS = 16
PIECES = 4
LIMIT = 18 * 1024 * 1024
WHOLE = 3 * LIMIT
SMEM = pl.BlockSpec(memory_space=pltpu.SMEM)
AFTER = pl.BlockSpec(memory_space=pl.ANY)


def params(limit=LIMIT):
    return pltpu.CompilerParams(vmem_limit_bytes=limit)


def in_place(arrays):
    return [pltpu.with_memory_space_constraint(x, pltpu.HBM) for x in arrays]


def cost(flops, moved):
    return pl.CostEstimate(flops=flops, bytes_accessed=moved, transcendentals=0)


def complex_rows(real, imag):
    return jnp.concatenate([real, -imag], 1), jnp.concatenate([imag, real], 1)


def right_kernel(after, ranks, states, me_ref, second_ref, *refs):
    refs = refs[after:]
    kinds = len(refs) - 1 - ranks
    packets, outs, slabs = refs[:kinds], refs[kinds:-1], refs[-1]
    me = me_ref[0]
    rows = packets[0].shape[0]
    group = packets[0].shape[2]
    tiles = group // states
    piece = slabs.shape[2] // 2
    cuts = tiles * LANES // piece
    for n, packet in enumerate(packets):
        turned = [
            packet[:, c].astype(jnp.float32).transpose(1, 0, 2).astype(jnp.bfloat16)
            for c in range(2)
        ]

        def part(c, j):
            return jnp.concatenate([turned[c][t * states + j] for t in range(tiles)], 1)

        pairs = [complex_rows(part(0, j), part(1, j)) for j in range(states)]
        left = jnp.concatenate([p[0] for p in pairs] + [p[1] for p in pairs], 0)
        product = jnp.dot(left, second_ref[...], preferred_element_type=jnp.float32)
        product = product.astype(jnp.bfloat16)
        for c in range(2):
            for j in range(states):
                first = (c * states + j) * rows
                for p in range(cuts):
                    slabs[j * cuts + p, :, c * piece : (c + 1) * piece] = product[
                        first : first + rows, p * piece : (p + 1) * piece
                    ]
        for s, out in enumerate(outs):
            out[n] = slabs[me ^ s]


def right_call(after, me, second, view, chosen, ranks, states, piece, limit):
    rows, _, _, group, _ = view.shape
    width = second.shape[1]
    block = rows // 2
    kinds = len(chosen)
    return pl.pallas_call(
        functools.partial(right_kernel, len(after), ranks, states),
        grid=(rows // block,),
        in_specs=[SMEM, pl.BlockSpec(second.shape, lambda i: (0, 0))]
        + [AFTER] * len(after)
        + [
            pl.BlockSpec((block, 2, None, group, LANES), lambda i, k=k: (i, 0, k, 0, 0))
            for k in chosen
        ],
        out_specs=[pl.BlockSpec((kinds, block, 2 * piece), lambda i: (0, i, 0))] * ranks,
        out_shape=[jax.ShapeDtypeStruct((kinds, rows, 2 * piece), jnp.bfloat16)] * ranks,
        scratch_shapes=[
            pltpu.VMEM((ranks, block, 2 * piece), jnp.bfloat16),
        ],
        compiler_params=params(limit),
        cost_estimate=cost(
            8 * kinds * states * rows * width * width, 8 * kinds * states * rows * width
        ),
        name="right",
    )(me, second, *after, *([view] * kinds))


def left_kernel(after, order, me_ref, first_ref, *refs):
    refs = refs[after:]
    ranks = len(order)
    ins, outs, lines, slabs = refs[:ranks], refs[ranks:-2], refs[-2], refs[-1]
    me = me_ref[0]
    rows, wide = ins[0].shape
    piece = wide // 2
    whole = ranks * rows
    for s, part in zip(order, ins):
        value = part[...]
        first = pl.multiple_of((me ^ s) * rows, rows)
        lines[pl.ds(first, rows), :] = value
        lines[pl.ds(first + whole, rows), :] = jnp.concatenate(
            [-value[:, piece:], value[:, :piece]], 1
        )
    product = jnp.dot(first_ref[...], lines[...], preferred_element_type=jnp.float32)
    slabs[...] = product.astype(jnp.bfloat16).reshape(ranks, rows, wide)
    for s, out in enumerate(outs):
        out[...] = slabs[me ^ s]


def left_call(after, me, first, slabs, order):
    ranks = len(slabs)
    kinds, rows, wide = slabs[0].shape
    whole = ranks * rows
    spec = pl.BlockSpec((None, rows, wide), lambda i: (i, 0, 0))
    return pl.pallas_call(
        functools.partial(left_kernel, len(after), order),
        grid=(kinds,),
        in_specs=[SMEM, pl.BlockSpec(first.shape, lambda i: (0, 0))]
        + [AFTER] * len(after)
        + [spec] * ranks,
        out_specs=[spec] * ranks,
        out_shape=[jax.ShapeDtypeStruct(slabs[0].shape, jnp.bfloat16)] * ranks,
        scratch_shapes=[
            pltpu.VMEM((2 * whole, wide), jnp.bfloat16),
            pltpu.VMEM((ranks, rows, wide), jnp.bfloat16),
        ],
        compiler_params=params(),
        cost_estimate=cost(
            4 * kinds * whole * whole * wide, 4 * whole * whole + 4 * kinds * whole * wide
        ),
        name="left",
    )(me, first, *after, *[slabs[s] for s in order])


def phased_product(me, n, second_ref, cosine_ref, sine_ref, ins, order, slabs):
    states, _, width = cosine_ref.shape
    piece = slabs.shape[2] // 2
    cuts = width // piece
    for s, part in zip(order, ins):
        slabs[me ^ s] = part[n]
    pairs = []
    for j in range(states):
        real, imag = (
            jnp.concatenate(
                [slabs[j * cuts + p, :, c * piece : (c + 1) * piece] for p in range(cuts)], 1
            ).astype(jnp.float32)
            for c in range(2)
        )
        cosine, sine = cosine_ref[j], sine_ref[j]
        pairs.append(
            complex_rows(
                (real * cosine + imag * sine).astype(jnp.bfloat16),
                (imag * cosine - real * sine).astype(jnp.bfloat16),
            )
        )
    left = jnp.concatenate([p[0] for p in pairs] + [p[1] for p in pairs], 0)
    product = jnp.dot(left, second_ref[...], preferred_element_type=jnp.float32)
    return product.astype(jnp.bfloat16)


def phase_kernel(after, ranks, me_ref, second_ref, cosine_ref, sine_ref, *refs):
    refs = refs[after:]
    ins, outs, whole, slabs = refs[:ranks], refs[ranks:-2], refs[-2], refs[-1]
    states, rows, width = cosine_ref.shape
    share = outs[0].shape[1]
    pieces = states // share
    for n in range(whole.shape[0]):
        product = phased_product(
            me_ref[0], n, second_ref, cosine_ref, sine_ref, ins, range(ranks), slabs
        )
        whole[n] = product.reshape(2, states, rows, width)
    for n, out in enumerate(outs):
        end = me_ref[1] if n < pieces else 1 - me_ref[1]
        first = n % pieces * share
        out[...] = whole[end, :, first : first + share]


def phase_call(after, me, second, cosine, sine, slabs):
    ranks = len(slabs)
    kinds, rows, wide = slabs[0].shape
    states, _, width = cosine.shape
    block = rows // 2
    share = states // PIECES
    count = kinds * PIECES
    table = pl.BlockSpec((states, block, width), lambda i: (0, i, 0))
    return pl.pallas_call(
        functools.partial(phase_kernel, len(after), ranks),
        grid=(rows // block,),
        in_specs=[SMEM, pl.BlockSpec(second.shape, lambda i: (0, 0)), table, table]
        + [AFTER] * len(after)
        + [pl.BlockSpec((kinds, block, wide), lambda i: (0, i, 0))] * ranks,
        out_specs=[pl.BlockSpec((2, share, block, width), lambda i: (0, 0, i, 0))] * count
        + [pl.BlockSpec((kinds, 2, states, block, width), lambda i: (0, 0, 0, i, 0))],
        out_shape=[pltpu.HBM((2, share, rows, width), jnp.bfloat16)] * count
        + [pltpu.HBM((kinds, 2, states, rows, width), jnp.bfloat16)],
        scratch_shapes=[pltpu.VMEM((ranks, block, wide), jnp.bfloat16)],
        compiler_params=params(),
        cost_estimate=cost(
            8 * kinds * states * rows * width * width, 8 * kinds * states * rows * width
        ),
        name="phase",
    )(me, second, cosine, sine, *after, *slabs)


def mix_kernel(
    chosen, order, me_ref, up_ref, down_ref, second_ref, cosine_ref, sine_ref, weight_ref, *refs
):
    ranks = len(order)
    ins, edges, pairs, (out, slabs, fresh, halo) = (
        refs[:ranks],
        refs[ranks],
        refs[ranks + 1 : -4],
        refs[-4:],
    )
    blocks, states = up_ref.shape
    rows, width = weight_ref.shape
    share = pairs[0].shape[1]
    pieces = states // share
    group = out.shape[3]
    for n, part in enumerate(pairs):
        end = me_ref[1] if n < pieces else 1 - me_ref[1]
        first = n % pieces * share
        halo[end, :, first : first + share] = part[...]
    others = [k for k in range(blocks) if k not in chosen]
    for n in range(len(chosen)):
        product = phased_product(
            me_ref[0], n, second_ref, cosine_ref, sine_ref, ins, order, slabs
        )
        fresh[n] = product.reshape(2, states, rows, width)

    def kinetic(k, c, j, span):
        if k in chosen:
            value = fresh[chosen.index(k), c, j, span]
        elif k in others:
            value = edges[others.index(k), c, j, span]
        else:
            value = halo[int(k > 0), c, j, span]
        return value.astype(jnp.float32)

    for first in range(0, rows, ROWS):
        span = slice(first, first + ROWS)
        weight = weight_ref[span]
        for k in range(blocks):
            columns = [[None] * group for _ in range(2)]
            for j in range(states):
                up, down = up_ref[k, j], down_ref[k, j]
                mixed = [
                    up * kinetic(k + 1, c, j, span) + down * kinetic(k - 1, c, j, span)
                    for c in range(2)
                ]
                parts = (
                    kinetic(k, 0, j, span) + weight * mixed[1],
                    kinetic(k, 1, j, span) - weight * mixed[0],
                )
                for c in range(2):
                    for t in range(width // LANES):
                        columns[c][t * states + j] = parts[c][:, t * LANES : (t + 1) * LANES]
            for c in range(2):
                out[span, c, k] = jnp.stack(columns[c], 0).transpose(1, 0, 2).astype(jnp.bfloat16)


def mix_call(me, up, down, second, cosine, sine, weight, chosen, slabs, edges, halo):
    ranks = len(slabs)
    order = tuple(range(ranks))
    kinds, rows, wide = slabs[0].shape
    _, share, _, width = halo[0].shape
    blocks, states = up.shape
    group = width // LANES * states
    block = rows // 4
    table = pl.BlockSpec((states, block, width), lambda i: (0, i, 0))
    return pl.pallas_call(
        functools.partial(mix_kernel, tuple(chosen), order),
        grid=(rows // block,),
        in_specs=[SMEM] * 3
        + [pl.BlockSpec(second.shape, lambda i: (0, 0)), table, table]
        + [pl.BlockSpec((block, width), lambda i: (i, 0))]
        + [pl.BlockSpec((kinds, block, wide), lambda i: (0, i, 0))] * ranks
        + [pl.BlockSpec((*edges.shape[:3], block, width), lambda i: (0, 0, 0, i, 0))]
        + [pl.BlockSpec((2, share, block, width), lambda i: (0, 0, i, 0))] * len(halo),
        out_specs=pl.BlockSpec((block, 2, blocks, group, LANES), lambda i: (i, 0, 0, 0, 0)),
        out_shape=jax.ShapeDtypeStruct((rows, 2, blocks, group, LANES), jnp.bfloat16),
        scratch_shapes=[
            pltpu.VMEM((ranks, block, wide), jnp.bfloat16),
            pltpu.VMEM((kinds, 2, states, block, width), jnp.bfloat16),
            pltpu.VMEM((2, 2, states, block, width), jnp.bfloat16),
        ],
        compiler_params=params(LIMIT + LIMIT // 2),
        cost_estimate=cost(
            8 * kinds * states * rows * width * width, 10 * blocks * states * rows * width
        ),
        name="mix",
    )(me, up, down, second, cosine, sine, weight, *in_place([slabs[s] for s in order] + [edges, *halo]))


def exchanged(slabs, axis):
    count = lax.axis_size(axis)
    result = [slabs[0]] + [None] * (count - 1)
    for s in reversed(range(1, count)):
        result[s] = lax.ppermute(slabs[s], axis, [(i, i ^ s) for i in range(count)])
    return result


def paired(edge, axis, first):
    count = lax.axis_size(axis)
    pairs = [(i, i + 1) for i in range(first, count - 1, 2)]
    return lax.ppermute(edge, axis, pairs + [(j, i) for i, j in pairs])


def per_device(packet, first_propagator, second_propagator, potential, coupling, radial_weight):
    rows, _, blocks, states, width = packet.shape
    ranks = lax.axis_size("rad")
    whole = first_propagator.shape[1]
    tiles = width // LANES
    piece = states * width // ranks
    me = lax.axis_index("rad").astype(jnp.int32).reshape(1)
    place = jnp.stack([lax.axis_index("rad"), lax.axis_index("hel") % 2]).astype(jnp.int32)
    second = second_propagator.reshape(2 * width, width)
    first = first_propagator.reshape(2 * whole, whole).T
    view = packet.reshape(rows, 2, blocks, states, tiles, LANES).transpose(0, 1, 2, 4, 3, 5)
    view = view.reshape(rows, 2, blocks, tiles * states, LANES)
    edges = sorted({0, blocks - 1})
    chunks = [edges, [k for k in range(blocks) if k not in edges]]

    last = me
    lines = []
    for n, chosen in enumerate(chunks):
        limit = LIMIT if n else WHOLE
        half = right_call([last], me, second, view, chosen, ranks, states, piece, limit)
        last = half[0]
        lines.append(exchanged(half, "rad"))
    backs = []
    for line in lines:
        moved = left_call([last], me, first, line, tuple(range(ranks)))
        last = moved[0]
        backs.append(exchanged(moved, "rad"))

    angles = potential.transpose(1, 0, 2)
    cosine, sine = jnp.cos(angles), jnp.sin(angles)
    edge = phase_call([last], place, second, cosine, sine, backs[0])
    halo = [paired(x, "hel", 1) for x in edge[:PIECES]]
    halo += [paired(x, "hel", 0) for x in edge[PIECES:-1]]

    count = coupling.shape[0]
    helicities = jnp.arange(count, dtype=jnp.int32)
    couple_up = jnp.where(helicities[:, None] < count - 1, coupling, 0.0)
    couple_down = jnp.concatenate(
        [jnp.zeros((1, coupling.shape[1]), jnp.float32), coupling[:-1]], axis=0
    )
    start = lax.axis_index("hel") * blocks
    up = lax.dynamic_slice_in_dim(couple_up, start, blocks, 0)
    down = lax.dynamic_slice_in_dim(couple_down, start, blocks, 0)
    out = mix_call(
        place, up, down, second, cosine, sine, radial_weight, chunks[1], backs[1], edge[-1], halo
    )
    out = out.reshape(rows, 2, blocks, tiles, states, LANES).transpose(0, 1, 2, 4, 3, 5)
    return out.reshape(rows, 2, blocks, states, width)


def solution(mesh):
    return jax.shard_map(
        per_device,
        mesh=mesh,
        in_specs=(
            P("rad", None, "hel", None, None),
            P(),
            P(),
            P("rad", None, None),
            P(),
            P("rad", None),
        ),
        out_specs=P("rad", None, "hel", None, None),
        check_vma=False,
    )
```

```python
import functools

import jax
import jax.numpy as jnp
from jax import lax
from jax.experimental import pallas as pl
from jax.experimental.pallas import tpu as pltpu
from jax.sharding import PartitionSpec as P

LANES = 128
ROWS = 16
PIECES = 4
LIMIT = 18 * 1024 * 1024
WHOLE = 3 * LIMIT
SMEM = pl.BlockSpec(memory_space=pltpu.SMEM)
AFTER = pl.BlockSpec(memory_space=pl.ANY)


def params(limit=LIMIT):
    return pltpu.CompilerParams(vmem_limit_bytes=limit)


def in_place(arrays):
    return [pltpu.with_memory_space_constraint(x, pltpu.HBM) for x in arrays]


def cost(flops, moved):
    return pl.CostEstimate(flops=flops, bytes_accessed=moved, transcendentals=0)


def complex_rows(real, imag):
    return jnp.concatenate([real, -imag], 1), jnp.concatenate([imag, real], 1)


def right_kernel(after, ranks, states, me_ref, second_ref, *refs):
    refs = refs[after:]
    kinds = len(refs) - 1 - ranks
    packets, outs, slabs = refs[:kinds], refs[kinds:-1], refs[-1]
    me = me_ref[0]
    rows = packets[0].shape[0]
    group = packets[0].shape[2]
    tiles = group // states
    piece = slabs.shape[2] // 2
    cuts = tiles * LANES // piece
    for n, packet in enumerate(packets):
        turned = [
            packet[:, c].astype(jnp.float32).transpose(1, 0, 2).astype(jnp.bfloat16)
            for c in range(2)
        ]

        def part(c, j):
            return jnp.concatenate([turned[c][t * states + j] for t in range(tiles)], 1)

        pairs = [complex_rows(part(0, j), part(1, j)) for j in range(states)]
        left = jnp.concatenate([p[0] for p in pairs] + [p[1] for p in pairs], 0)
        product = jnp.dot(left, second_ref[...], preferred_element_type=jnp.float32)
        product = product.astype(jnp.bfloat16)
        for c in range(2):
            for j in range(states):
                first = (c * states + j) * rows
                for p in range(cuts):
                    slabs[j * cuts + p, :, c * piece : (c + 1) * piece] = product[
                        first : first + rows, p * piece : (p + 1) * piece
                    ]
        for s, out in enumerate(outs):
            out[n] = slabs[me ^ s]


def right_call(after, me, second, view, chosen, ranks, states, piece, limit):
    rows, _, _, group, _ = view.shape
    width = second.shape[1]
    block = rows // 4
    kinds = len(chosen)
    return pl.pallas_call(
        functools.partial(right_kernel, len(after), ranks, states),
        grid=(rows // block,),
        in_specs=[SMEM, pl.BlockSpec(second.shape, lambda i: (0, 0))]
        + [AFTER] * len(after)
        + [
            pl.BlockSpec((block, 2, None, group, LANES), lambda i, k=k: (i, 0, k, 0, 0))
            for k in chosen
        ],
        out_specs=[pl.BlockSpec((kinds, block, 2 * piece), lambda i: (0, i, 0))] * ranks,
        out_shape=[jax.ShapeDtypeStruct((kinds, rows, 2 * piece), jnp.bfloat16)] * ranks,
        scratch_shapes=[
            pltpu.VMEM((ranks, block, 2 * piece), jnp.bfloat16),
        ],
        compiler_params=params(limit),
        cost_estimate=cost(
            8 * kinds * states * rows * width * width, 8 * kinds * states * rows * width
        ),
        name="right",
    )(me, second, *after, *([view] * kinds))


def left_kernel(after, order, me_ref, first_ref, *refs):
    refs = refs[after:]
    ranks = len(order)
    ins, outs, lines, slabs = refs[:ranks], refs[ranks:-2], refs[-2], refs[-1]
    me = me_ref[0]
    rows, wide = ins[0].shape
    piece = wide // 2
    whole = ranks * rows
    for s, part in zip(order, ins):
        value = part[...]
        first = pl.multiple_of((me ^ s) * rows, rows)
        lines[pl.ds(first, rows), :] = value
        lines[pl.ds(first + whole, rows), :] = jnp.concatenate(
            [-value[:, piece:], value[:, :piece]], 1
        )
    product = jnp.dot(first_ref[...], lines[...], preferred_element_type=jnp.float32)
    slabs[...] = product.astype(jnp.bfloat16).reshape(ranks, rows, wide)
    for s, out in enumerate(outs):
        out[...] = slabs[me ^ s]


def left_call(after, me, first, slabs, order):
    ranks = len(slabs)
    kinds, rows, wide = slabs[0].shape
    whole = ranks * rows
    spec = pl.BlockSpec((None, rows, wide), lambda i: (i, 0, 0))
    return pl.pallas_call(
        functools.partial(left_kernel, len(after), order),
        grid=(kinds,),
        in_specs=[SMEM, pl.BlockSpec(first.shape, lambda i: (0, 0))]
        + [AFTER] * len(after)
        + [spec] * ranks,
        out_specs=[spec] * ranks,
        out_shape=[jax.ShapeDtypeStruct(slabs[0].shape, jnp.bfloat16)] * ranks,
        scratch_shapes=[
            pltpu.VMEM((2 * whole, wide), jnp.bfloat16),
            pltpu.VMEM((ranks, rows, wide), jnp.bfloat16),
        ],
        compiler_params=params(),
        cost_estimate=cost(
            4 * kinds * whole * whole * wide, 4 * whole * whole + 4 * kinds * whole * wide
        ),
        name="left",
    )(me, first, *after, *[slabs[s] for s in order])


def phased_product(me, n, second_ref, cosine_ref, sine_ref, ins, order, slabs):
    states, _, width = cosine_ref.shape
    piece = slabs.shape[2] // 2
    cuts = width // piece
    for s, part in zip(order, ins):
        slabs[me ^ s] = part[n]
    pairs = []
    for j in range(states):
        real, imag = (
            jnp.concatenate(
                [slabs[j * cuts + p, :, c * piece : (c + 1) * piece] for p in range(cuts)], 1
            ).astype(jnp.float32)
            for c in range(2)
        )
        cosine, sine = cosine_ref[j], sine_ref[j]
        pairs.append(
            complex_rows(
                (real * cosine + imag * sine).astype(jnp.bfloat16),
                (imag * cosine - real * sine).astype(jnp.bfloat16),
            )
        )
    left = jnp.concatenate([p[0] for p in pairs] + [p[1] for p in pairs], 0)
    product = jnp.dot(left, second_ref[...], preferred_element_type=jnp.float32)
    return product.astype(jnp.bfloat16)


def phase_kernel(after, ranks, me_ref, second_ref, cosine_ref, sine_ref, *refs):
    refs = refs[after:]
    ins, outs, whole, slabs = refs[:ranks], refs[ranks:-2], refs[-2], refs[-1]
    states, rows, width = cosine_ref.shape
    share = outs[0].shape[1]
    pieces = states // share
    for n in range(whole.shape[0]):
        product = phased_product(
            me_ref[0], n, second_ref, cosine_ref, sine_ref, ins, range(ranks), slabs
        )
        whole[n] = product.reshape(2, states, rows, width)
    for n, out in enumerate(outs):
        end = me_ref[1] if n < pieces else 1 - me_ref[1]
        first = n % pieces * share
        out[...] = whole[end, :, first : first + share]


def phase_call(after, me, second, cosine, sine, slabs):
    ranks = len(slabs)
    kinds, rows, wide = slabs[0].shape
    states, _, width = cosine.shape
    block = rows // 2
    share = states // PIECES
    count = kinds * PIECES
    table = pl.BlockSpec((states, block, width), lambda i: (0, i, 0))
    return pl.pallas_call(
        functools.partial(phase_kernel, len(after), ranks),
        grid=(rows // block,),
        in_specs=[SMEM, pl.BlockSpec(second.shape, lambda i: (0, 0)), table, table]
        + [AFTER] * len(after)
        + [pl.BlockSpec((kinds, block, wide), lambda i: (0, i, 0))] * ranks,
        out_specs=[pl.BlockSpec((2, share, block, width), lambda i: (0, 0, i, 0))] * count
        + [pl.BlockSpec((kinds, 2, states, block, width), lambda i: (0, 0, 0, i, 0))],
        out_shape=[pltpu.HBM((2, share, rows, width), jnp.bfloat16)] * count
        + [pltpu.HBM((kinds, 2, states, rows, width), jnp.bfloat16)],
        scratch_shapes=[pltpu.VMEM((ranks, block, wide), jnp.bfloat16)],
        compiler_params=params(),
        cost_estimate=cost(
            8 * kinds * states * rows * width * width, 8 * kinds * states * rows * width
        ),
        name="phase",
    )(me, second, cosine, sine, *after, *slabs)


def mix_kernel(
    chosen, order, me_ref, up_ref, down_ref, second_ref, cosine_ref, sine_ref, weight_ref, *refs
):
    ranks = len(order)
    ins, edges, pairs, (out, slabs, fresh, halo) = (
        refs[:ranks],
        refs[ranks],
        refs[ranks + 1 : -4],
        refs[-4:],
    )
    blocks, states = up_ref.shape
    rows, width = weight_ref.shape
    share = pairs[0].shape[1]
    pieces = states // share
    group = out.shape[3]
    for n, part in enumerate(pairs):
        end = me_ref[1] if n < pieces else 1 - me_ref[1]
        first = n % pieces * share
        halo[end, :, first : first + share] = part[...]
    others = [k for k in range(blocks) if k not in chosen]
    for n in range(len(chosen)):
        product = phased_product(
            me_ref[0], n, second_ref, cosine_ref, sine_ref, ins, order, slabs
        )
        fresh[n] = product.reshape(2, states, rows, width)

    def kinetic(k, c, j, span):
        if k in chosen:
            value = fresh[chosen.index(k), c, j, span]
        elif k in others:
            value = edges[others.index(k), c, j, span]
        else:
            value = halo[int(k > 0), c, j, span]
        return value.astype(jnp.float32)

    for first in range(0, rows, ROWS):
        span = slice(first, first + ROWS)
        weight = weight_ref[span]
        for k in range(blocks):
            columns = [[None] * group for _ in range(2)]
            for j in range(states):
                up, down = up_ref[k, j], down_ref[k, j]
                mixed = [
                    up * kinetic(k + 1, c, j, span) + down * kinetic(k - 1, c, j, span)
                    for c in range(2)
                ]
                parts = (
                    kinetic(k, 0, j, span) + weight * mixed[1],
                    kinetic(k, 1, j, span) - weight * mixed[0],
                )
                for c in range(2):
                    for t in range(width // LANES):
                        columns[c][t * states + j] = parts[c][:, t * LANES : (t + 1) * LANES]
            for c in range(2):
                out[span, c, k] = jnp.stack(columns[c], 0).transpose(1, 0, 2).astype(jnp.bfloat16)


def mix_call(me, up, down, second, cosine, sine, weight, chosen, slabs, edges, halo):
    ranks = len(slabs)
    order = tuple(range(ranks))
    kinds, rows, wide = slabs[0].shape
    _, share, _, width = halo[0].shape
    blocks, states = up.shape
    group = width // LANES * states
    block = rows // 4
    table = pl.BlockSpec((states, block, width), lambda i: (0, i, 0))
    return pl.pallas_call(
        functools.partial(mix_kernel, tuple(chosen), order),
        grid=(rows // block,),
        in_specs=[SMEM] * 3
        + [pl.BlockSpec(second.shape, lambda i: (0, 0)), table, table]
        + [pl.BlockSpec((block, width), lambda i: (i, 0))]
        + [pl.BlockSpec((kinds, block, wide), lambda i: (0, i, 0))] * ranks
        + [pl.BlockSpec((*edges.shape[:3], block, width), lambda i: (0, 0, 0, i, 0))]
        + [pl.BlockSpec((2, share, block, width), lambda i: (0, 0, i, 0))] * len(halo),
        out_specs=pl.BlockSpec((block, 2, blocks, group, LANES), lambda i: (i, 0, 0, 0, 0)),
        out_shape=jax.ShapeDtypeStruct((rows, 2, blocks, group, LANES), jnp.bfloat16),
        scratch_shapes=[
            pltpu.VMEM((ranks, block, wide), jnp.bfloat16),
            pltpu.VMEM((kinds, 2, states, block, width), jnp.bfloat16),
            pltpu.VMEM((2, 2, states, block, width), jnp.bfloat16),
        ],
        compiler_params=params(LIMIT + LIMIT // 2),
        cost_estimate=cost(
            8 * kinds * states * rows * width * width, 10 * blocks * states * rows * width
        ),
        name="mix",
    )(me, up, down, second, cosine, sine, weight, *in_place([slabs[s] for s in order] + [edges, *halo]))


def exchanged(slabs, axis):
    count = lax.axis_size(axis)
    result = [slabs[0]] + [None] * (count - 1)
    for s in reversed(range(1, count)):
        result[s] = lax.ppermute(slabs[s], axis, [(i, i ^ s) for i in range(count)])
    return result


def paired(edge, axis, first):
    count = lax.axis_size(axis)
    pairs = [(i, i + 1) for i in range(first, count - 1, 2)]
    return lax.ppermute(edge, axis, pairs + [(j, i) for i, j in pairs])


def per_device(packet, first_propagator, second_propagator, potential, coupling, radial_weight):
    rows, _, blocks, states, width = packet.shape
    ranks = lax.axis_size("rad")
    whole = first_propagator.shape[1]
    tiles = width // LANES
    piece = states * width // ranks
    me = lax.axis_index("rad").astype(jnp.int32).reshape(1)
    place = jnp.stack([lax.axis_index("rad"), lax.axis_index("hel") % 2]).astype(jnp.int32)
    second = second_propagator.reshape(2 * width, width)
    first = first_propagator.reshape(2 * whole, whole).T
    view = packet.reshape(rows, 2, blocks, states, tiles, LANES).transpose(0, 1, 2, 4, 3, 5)
    view = view.reshape(rows, 2, blocks, tiles * states, LANES)
    edges = sorted({0, blocks - 1})
    chunks = [edges, [k for k in range(blocks) if k not in edges]]

    last = me
    lines = []
    for n, chosen in enumerate(chunks):
        limit = LIMIT if n else WHOLE
        half = right_call([last], me, second, view, chosen, ranks, states, piece, limit)
        last = half[0]
        lines.append(exchanged(half, "rad"))
    backs = []
    for line in lines:
        moved = left_call([last], me, first, line, tuple(range(ranks)))
        last = moved[0]
        backs.append(exchanged(moved, "rad"))

    angles = potential.transpose(1, 0, 2)
    cosine, sine = jnp.cos(angles), jnp.sin(angles)
    edge = phase_call([last], place, second, cosine, sine, backs[0])
    halo = [paired(x, "hel", 1) for x in edge[:PIECES]]
    halo += [paired(x, "hel", 0) for x in edge[PIECES:-1]]

    count = coupling.shape[0]
    helicities = jnp.arange(count, dtype=jnp.int32)
    couple_up = jnp.where(helicities[:, None] < count - 1, coupling, 0.0)
    couple_down = jnp.concatenate(
        [jnp.zeros((1, coupling.shape[1]), jnp.float32), coupling[:-1]], axis=0
    )
    start = lax.axis_index("hel") * blocks
    up = lax.dynamic_slice_in_dim(couple_up, start, blocks, 0)
    down = lax.dynamic_slice_in_dim(couple_down, start, blocks, 0)
    out = mix_call(
        place, up, down, second, cosine, sine, radial_weight, chunks[1], backs[1], edge[-1], halo
    )
    out = out.reshape(rows, 2, blocks, tiles, states, LANES).transpose(0, 1, 2, 4, 3, 5)
    return out.reshape(rows, 2, blocks, states, width)


def solution(mesh):
    return jax.shard_map(
        per_device,
        mesh=mesh,
        in_specs=(
            P("rad", None, "hel", None, None),
            P(),
            P(),
            P("rad", None, None),
            P(),
            P("rad", None),
        ),
        out_specs=P("rad", None, "hel", None, None),
        check_vma=False,
    )
```
